512 devices in a mesh: seq: 64 (over z, x), grp: 8 (over y, core).
Axes of the slice: x: 4, y: 4, z: 16, core: 2. Of those that a mesh axis runs over, the one named last changes fastest.
Arguments:
- queries: bfloat16 [8192, 5120], P('seq', 'grp'), may hold values from -52 to 52
- keys_in: bfloat16 [8192, 5120], P('seq', 'grp'), may hold values from -5 to 5
- values: bfloat16 [8192, 5120], P('seq', 'grp'), may hold values from -6 to 6
- cluster_ids: int32 [8192, 1], P('seq'), may hold values from 0 to 255, as said below
- out_weight: bfloat16 [5120, 5120], P('seq', 'grp'), may hold values from -0.078125 to 0.078125
Outputs:
- mixed: bfloat16 [8192, 5120], P('seq', 'grp')
The draws below stay inside these ranges and needn't reach their ends.
Inputs may be any that keep to these rules, and one draw needn't show every extreme that they name: `cluster_ids`: among the 128 tokens of one index of seq, no cluster is named more than 2 times, and some cluster is named exactly 2 times.
All inputs are finite; a program needn't handle non-finite values.
Results may differ from the reference program's by a relative error of at most 0.014.
Values may be sent and summed in bfloat16 or wider, within the bound.
No kernel may reach another device: no remote copies, remote signals or barrier semaphores. Data moves between devices by JAX's collectives and lax.ppermute only.
A program may use at most 64 MiB of HBM per device.

```python
import jax
import jax.numpy as jnp
from jax import lax

HEADS = 40
HEAD = 128
D = 5120
CLUSTERS = 256
TOK_SEQ = 128
SLOT_CAP = 2
TOKENS = 8192
N_SEQ = 64


def draw_keys_in(key, part):
    key = jax.random.fold_in(key, 1)
    noise = jnp.clip(jax.random.normal(key, (TOKENS, HEADS * HEAD), jnp.float32), -4.0, 4.0)
    return noise.astype(jnp.bfloat16)


def draw_queries(key, part):
    key = jax.random.fold_in(key, 2)
    base = jnp.clip(jax.random.normal(key, (TOKENS, HEADS * HEAD), jnp.float32), -4.0, 4.0)
    return base.astype(jnp.bfloat16)


def draw_cluster_ids(key, part):
    key = jax.random.fold_in(key, 7)
    blocks = TOKENS // TOK_SEQ
    slot_total = CLUSTERS * SLOT_CAP
    owner_slots = CLUSTERS // blocks * SLOT_CAP
    slot_index = jnp.arange(slot_total, dtype=jnp.int32)
    owner_of = slot_index // owner_slots
    owner_bias = jax.random.randint(jax.random.fold_in(key, 1), (blocks,), 0, slot_total)

    def one_block(index):
        block_key = jax.random.fold_in(key, index + 100)
        priority = jax.random.permutation(jax.random.fold_in(block_key, 1), slot_total).astype(jnp.int32)
        chosen = jax.random.randint(jax.random.fold_in(block_key, 2), (), 0, blocks)
        score = jnp.where(owner_of == chosen, -1, priority + owner_bias[owner_of])
        picked = jnp.argsort(score, stable=True)[:TOK_SEQ].astype(jnp.int32)
        clusters = picked // SLOT_CAP
        shuffle = jax.random.permutation(jax.random.fold_in(block_key, 3), TOK_SEQ)
        return clusters[shuffle]
    result = jax.vmap(one_block)(jnp.arange(blocks, dtype=jnp.int32))
    return result.reshape(TOKENS, 1).astype(jnp.int32)


def levels(rng, dims, split, low, top_value):
    loudness, own = 1.0, jax.random.fold_in(rng, 6)
    for dim, parts in split:
        heights = jnp.exp(jax.random.uniform(jax.random.fold_in(own, dim), (parts,), jnp.float32, low / len(split), top_value / len(split)))
        loudness = loudness * jnp.repeat(heights, dims[dim] // parts).reshape([-1 if axis == dim else 1 for axis in range(len(dims))])
    return loudness


def gaussian(key, extent, deviation, most, shards=(), kind=jnp.bfloat16):
    entries = deviation * jax.random.normal(key, extent, jnp.float32)
    if shards:
        entries = entries * levels(key, extent, shards, -0.22, 0.18)
    return jnp.clip(entries, -most, most).astype(kind)


def setup_inputs(seed: int = 0) -> dict:
    arg_keys = jax.random.split(jax.random.key(seed), 6)
    queries = draw_queries(jax.random.fold_in(arg_keys[5], 71), 0)
    keys_in = draw_keys_in(jax.random.fold_in(arg_keys[5], 71), 0)
    values = gaussian(arg_keys[2], (TOKENS, D), 1.0, 6.0, ((0, 64), (1, 8)))
    cluster_ids = draw_cluster_ids(jax.random.fold_in(arg_keys[5], 71), 0)
    out_weight = gaussian(arg_keys[4], (D, D), D ** -0.5, 0.078125, ((0, 64), (1, 8)))
    return dict(queries=queries, keys_in=keys_in, values=values, cluster_ids=cluster_ids, out_weight=out_weight)


def reference(queries, keys_in, values, cluster_ids, out_weight):
    cluster_of = cluster_ids[:, 0]
    total = cluster_of.shape[0]
    cap_all = N_SEQ * SLOT_CAP
    counts = jnp.sum((cluster_of[:, None] == jnp.arange(CLUSTERS, dtype=jnp.int32)[None, :]).astype(jnp.int32), axis=0)
    order = jnp.argsort(cluster_of, stable=True).astype(jnp.int32)
    starts = (jnp.cumsum(counts) - counts).astype(jnp.int32)
    order_pad = jnp.concatenate([order, jnp.zeros((cap_all,), jnp.int32)])
    scale = HEAD ** -0.5

    def one_cluster(cluster):
        members = lax.dynamic_slice_in_dim(order_pad, starts[cluster].astype(jnp.int32), cap_all)
        live = jnp.arange(cap_all, dtype=jnp.int32) < counts[cluster]
        where_at = jnp.where(live, members, -1)
        query_part = queries[members].astype(jnp.float32).reshape(cap_all, HEADS, HEAD)
        key_part = keys_in[members].astype(jnp.float32).reshape(cap_all, HEADS, HEAD)
        value_part = values[members].astype(jnp.float32).reshape(cap_all, HEADS, HEAD)
        scores = jnp.einsum("qhd,shd->hqs", query_part, key_part) * scale
        allowed = (where_at[None, :] >= 0) & (where_at[None, :] <= where_at[:, None])
        scores = jnp.where(allowed[None], scores, jnp.float32(-1e30))
        peak = jnp.max(scores, axis=-1, keepdims=True)
        expo = jnp.exp(scores - peak)
        totals = jnp.sum(expo, axis=-1, keepdims=True)
        weights = (expo / totals).astype(jnp.bfloat16)
        output = jnp.einsum("hqs,shd->qhd", weights.astype(jnp.float32), value_part)
        output = output.astype(jnp.bfloat16).reshape(cap_all, HEADS * HEAD)
        target = jnp.where(live, members, total)
        return output, target

    outputs, targets = lax.map(one_cluster, jnp.arange(CLUSTERS, dtype=jnp.int32))
    attended = jnp.zeros((total, HEADS * HEAD), jnp.bfloat16)
    attended = attended.at[targets.reshape(-1)].set(outputs.reshape(-1, HEADS * HEAD), mode="drop")
    return jnp.dot(attended, out_weight, preferred_element_type=jnp.float32).astype(jnp.bfloat16)
```

```python
import functools

import jax
import jax.numpy as jnp
from jax import lax
from jax.experimental import pallas as pl
from jax.experimental.pallas import tpu as pltpu
from jax.sharding import Mesh
from jax.sharding import PartitionSpec as P

HEAD = 128
HEADS_HERE = 5
TOK = 128
Z, X, Y, C = 16, 4, 4, 2
PARTS = 3
STARTS = (0, 44, 88)
LENGTHS = (44, 44, 40)
SLOT = 48
ID_ROW = 46
POSITIONS = 8192
NEVER = 1e9
BLOCKED = -1e30
F32 = jnp.float32
BF16 = jnp.bfloat16
VMEM_LIMIT = 56 * 1024 * 1024


def vmem_call(body, out_shape, *operands):
    space = pl.BlockSpec(memory_space=pltpu.VMEM)
    many = isinstance(out_shape, (list, tuple))
    return pl.pallas_call(
        body,
        out_shape=out_shape,
        in_specs=[space] * len(operands),
        out_specs=[space] * len(out_shape) if many else space,
        compiler_params=pltpu.CompilerParams(vmem_limit_bytes=VMEM_LIMIT),
    )(*operands)


def scatter_heads(q_ref, k_ref, v_ref, ids_ref, out_ref):
    ids = ids_ref[...].astype(F32)
    lane = lax.broadcasted_iota(jnp.int32, (SLOT, HEAD), 1)
    row = lax.broadcasted_iota(jnp.int32, (SLOT, HEAD), 0)
    id_rows = []
    for start, length in zip(STARTS, LENGTHS):
        moved = ids if start == 0 else pltpu.roll(ids, TOK - start, 1)
        id_rows.append(jnp.where(lane < length, jnp.broadcast_to(moved, (SLOT, HEAD)), -1.0))
    every = jnp.broadcast_to(ids, (SLOT, HEAD))
    for h in range(HEADS_HERE):
        for part, source in enumerate((q_ref, k_ref, v_ref)):
            block = source[:, h * HEAD : (h + 1) * HEAD].astype(F32)
            block = jnp.concatenate([block, jnp.zeros((16, HEAD), F32)], axis=0)
            for r, (start, length) in enumerate(zip(STARTS, LENGTHS)):
                piece = jnp.where(row < length, block[start : start + SLOT], 0.0)
                if part == 0:
                    piece = jnp.where(row == ID_ROW, id_rows[r], piece)
                    piece = jnp.where(row == ID_ROW + 1, every, piece)
                out_ref[PARTS * h + r, part * SLOT : (part + 1) * SLOT, :] = piece.astype(BF16)
    out_ref[PARTS * HEADS_HERE] = jnp.zeros((3 * SLOT, HEAD), BF16)


def attend(q_ref, kv0_ref, kv1_ref, kv2_ref, qcode_ref, kcode_ref, out_ref):
    rows = Z * SLOT
    keys = [ref[:, :SLOT, :].reshape(rows, HEAD) for ref in (kv0_ref, kv1_ref, kv2_ref)]
    vals = [ref[:, SLOT:, :].reshape(rows, HEAD) for ref in (kv0_ref, kv1_ref, kv2_ref)]
    codes = qcode_ref[...].T
    lane = lax.broadcasted_iota(jnp.int32, (SLOT, HEAD), 1)
    stats = [jnp.zeros((SLOT, HEAD), F32) for _ in range(X)]
    group = 4
    for g in range(Z // group):
        count = -(-(g + 1) * group * SLOT // HEAD) * HEAD
        for x in range(X):
            code = jnp.concatenate(
                [codes[:SLOT, x * Z + z : x * Z + z + 1] for z in range(g * group, (g + 1) * group)], axis=0
            )
            base = jnp.floor(code * (1.0 / POSITIONS)) * POSITIONS
            query = q_ref[x, g * group * SLOT : (g + 1) * group * SLOT, :]
            scores = []
            for j in range(PARTS):
                score = lax.dot_general(
                    query, keys[j][:count], (((1,), (1,)), ((), ())), preferred_element_type=F32
                ) * HEAD ** (-0.5)
                key_code = kcode_ref[j : j + 1, :count]
                allowed = (key_code <= code) & (key_code >= base)
                scores.append(jnp.where(allowed, score, BLOCKED))
            peak = functools.reduce(jnp.maximum, [jnp.max(s, axis=1, keepdims=True) for s in scores])
            total = jnp.zeros_like(peak)
            output = jnp.zeros((group * SLOT, HEAD), F32)
            for j in range(PARTS):
                expo = jnp.exp(scores[j] - peak)
                total = total + jnp.sum(expo, axis=1, keepdims=True)
                output = output + jnp.dot(
                    expo.astype(BF16), vals[j][:count], preferred_element_type=F32
                )
            out_ref[x, g * group * SLOT : (g + 1) * group * SLOT, :] = (output / total).astype(BF16)
            logsum = peak + jnp.log(total)
            high = logsum.astype(BF16).astype(F32)
            rest = logsum - high
            middle = rest.astype(BF16).astype(F32)
            low = rest - middle
            for n in range(group):
                for part, column in enumerate((high, middle, low)):
                    stats[x] = jnp.where(
                        lane == part * Z + g * group + n, column[n * SLOT : (n + 1) * SLOT], stats[x]
                    )
    for x in range(X):
        out_ref[x, rows:, :] = stats[x].astype(BF16)


def join(part_ref, out_ref):
    rows = Z * SLOT
    sums = []
    for x in range(X):
        stat = part_ref[x, rows:, :].astype(F32)
        sums.append(stat + pltpu.roll(stat, HEAD - Z, 1) + pltpu.roll(stat, HEAD - 2 * Z, 1))
    peak = functools.reduce(jnp.maximum, sums)
    weights = [jnp.exp(s - peak) for s in sums]
    total = functools.reduce(jnp.add, weights)
    weights = [w / total for w in weights]
    for z in range(Z):
        joined = functools.reduce(
            jnp.add,
            [
                weights[x][:, z : z + 1] * part_ref[x, z * SLOT : (z + 1) * SLOT, :].astype(F32)
                for x in range(X)
            ],
        )
        out_ref[z] = joined.astype(BF16)


def assemble(part_ref, out_ref):
    width = HEADS_HERE * HEAD
    heads = []
    for h in range(HEADS_HERE):
        pieces = [
            part_ref[PARTS * h + r].astype(F32)[:length] for r, length in enumerate(LENGTHS)
        ]
        heads.append(jnp.concatenate(pieces, axis=0))
    whole = jnp.concatenate(heads, axis=1)
    chunk = width // (2 * X)
    for x in range(X):
        halves = [whole[:, a * width // 2 + x * chunk : a * width // 2 + (x + 1) * chunk] for a in range(2)]
        out_ref[x] = jnp.concatenate(halves, axis=1).astype(BF16)


def project(mine_ref, other_ref, weight_ref, core_ref, out_ref):
    depth = mine_ref.shape[2]
    core = core_ref[0]
    tokens = mine_ref.shape[1]
    for x in range(X):
        rows = slice(x * tokens // X, (x + 1) * tokens // X)
        total = jnp.zeros((tokens // X, weight_ref.shape[1]), F32)
        for y in range(Y):
            for source, which in ((mine_ref, core), (other_ref, 1 - core)):
                first = pl.multiple_of((C * y + which) * depth, 32)
                total = total + jnp.dot(
                    source[y, rows, :], weight_ref[pl.ds(first, depth), :], preferred_element_type=F32
                )
        out_ref[x] = total.astype(BF16)


def local(queries, keys_in, values, cluster_ids, out_weight):
    plane, side, core = lax.axis_index("z"), lax.axis_index("x"), lax.axis_index("c")
    third = lax.rem(plane, PARTS)
    weight = lax.all_gather(out_weight, "z", axis=0, tiled=True)

    send = vmem_call(
        scatter_heads,
        jax.ShapeDtypeStruct((Z, 3 * SLOT, HEAD), BF16),
        queries,
        keys_in,
        values,
        cluster_ids.reshape(1, TOK),
    )
    here = lax.all_to_all(send, "z", 0, 0, tiled=True)
    kv = here[:, SLOT:, :]
    turns = [
        [(PARTS * h + r, PARTS * h + (r + k) % PARTS) for h in range(HEADS_HERE) for r in range(PARTS)]
        for k in (1, 2)
    ]
    kv_others = [lax.ppermute(kv, "z", turn) for turn in turns]
    query = lax.all_gather(here[:, :SLOT, :].reshape(Z * SLOT, HEAD), "x", axis=0)

    lane = jnp.arange(HEAD, dtype=jnp.int32)
    home = (X * jnp.arange(Z, dtype=jnp.int32) + side) * TOK
    key_code = here[:, ID_ROW + 1, :].astype(F32) * POSITIONS + (home[:, None] + lane[None, :]).astype(F32)
    key_code = jnp.stack(
        [
            jnp.pad(
                key_code[:, start : start + length], ((0, 0), (0, SLOT - length)), constant_values=NEVER
            ).reshape(Z * SLOT)
            for start, length in zip(STARTS, LENGTHS)
        ]
    )
    order = [third, lax.rem(third + 2, PARTS), lax.rem(third + 1, PARTS)]
    key_code = jnp.concatenate(
        [lax.dynamic_slice_in_dim(key_code, turn, 1, axis=0) for turn in order], axis=0
    )
    first = jnp.where(third == 0, STARTS[0], jnp.where(third == 1, STARTS[1], STARTS[2]))
    all_home = (
        X * jnp.arange(Z, dtype=jnp.int32)[None, :] + jnp.arange(X, dtype=jnp.int32)[:, None]
    ) * TOK + first
    query_code = query.reshape(X, Z, SLOT, HEAD)[:, :, ID_ROW, :].astype(F32) * POSITIONS + (
        all_home[:, :, None] + lane[None, None, :]
    ).astype(F32)
    query_code = jnp.pad(query_code.reshape(X * Z, HEAD), ((0, HEAD - X * Z), (0, 0)))

    part = vmem_call(
        attend,
        jax.ShapeDtypeStruct((X, (Z + 1) * SLOT, HEAD), BF16),
        query,
        kv,
        kv_others[0],
        kv_others[1],
        query_code,
        key_code,
    )
    part = lax.all_to_all(part, "x", 0, 0, tiled=True)
    joined = vmem_call(join, jax.ShapeDtypeStruct((Z, SLOT, HEAD), BF16), part)
    joined = lax.all_to_all(joined, "z", 0, 0, tiled=True)
    depth = HEADS_HERE * HEAD // X
    rows = vmem_call(assemble, jax.ShapeDtypeStruct((X, TOK, depth), BF16), joined)
    rows = lax.all_to_all(rows, "x", 0, 0, tiled=True).reshape(X * TOK, depth)
    rows = lax.all_gather(rows, "y", axis=0)
    others = lax.ppermute(rows, "c", [(0, 1), (1, 0)])
    partial = pl.pallas_call(
        project,
        out_shape=jax.ShapeDtypeStruct((X, TOK, out_weight.shape[1]), BF16),
        in_specs=[pl.BlockSpec(memory_space=pltpu.VMEM)] * 3 + [pl.BlockSpec(memory_space=pltpu.SMEM)],
        out_specs=pl.BlockSpec(memory_space=pltpu.VMEM),
        compiler_params=pltpu.CompilerParams(vmem_limit_bytes=VMEM_LIMIT),
    )(rows, others, weight, core.reshape(1))
    partial = lax.all_to_all(partial, "x", 0, 0, tiled=True)
    return jnp.sum(partial.astype(F32), axis=0).astype(BF16)


def solution(mesh):
    fine = Mesh(mesh.devices.reshape(Z, X, Y, C), ("z", "x", "y", "c"))
    both = P(("z", "x"), ("y", "c"))
    return jax.shard_map(
        local,
        mesh=fine,
        in_specs=(both, both, both, P(("z", "x"), None), both),
        out_specs=both,
        check_vma=False,
    )
```

```python
import functools

import jax
import jax.numpy as jnp
from jax import lax
from jax.experimental import pallas as pl
from jax.experimental.pallas import tpu as pltpu
from jax.sharding import Mesh
from jax.sharding import PartitionSpec as P

HEAD = 128
HEADS_HERE = 5
TOK = 128
Z, X, Y, C = 16, 4, 4, 2
PARTS = 3
STARTS = (0, 44, 88)
LENGTHS = (44, 44, 40)
SLOT = 48
ID_ROW = 46
POSITIONS = 8192
NEVER = 1e9
BLOCKED = -1e30
F32 = jnp.float32
BF16 = jnp.bfloat16
LOG2E = 1.4426950408889634
SHARE = 32
GRANULE = 16


def vmem_call(body, mebibytes, shape, *operands, scalars=None):
    specs = [pl.BlockSpec(memory_space=pltpu.VMEM)] * len(operands)
    if scalars is not None:
        specs = [pl.BlockSpec(memory_space=pltpu.SMEM)] + specs
        operands = (scalars,) + operands
    return pl.pallas_call(
        body,
        out_shape=jax.ShapeDtypeStruct(shape, BF16),
        in_specs=specs,
        out_specs=pl.BlockSpec(memory_space=pltpu.VMEM),
        compiler_params=pltpu.CompilerParams(vmem_limit_bytes=mebibytes * 1024 * 1024),
    )(*operands)


def scatter_heads(q_ref, k_ref, v_ref, ids_ref, out_ref):
    ids = ids_ref[...].astype(F32)
    lane = lax.broadcasted_iota(jnp.int32, (SLOT, HEAD), 1)
    row = lax.broadcasted_iota(jnp.int32, (SLOT, HEAD), 0)
    id_rows = []
    for start, length in zip(STARTS, LENGTHS):
        moved = ids if start == 0 else pltpu.roll(ids, TOK - start, 1)
        id_rows.append(jnp.where(lane < length, jnp.broadcast_to(moved, (SLOT, HEAD)), -1.0))
    every = jnp.broadcast_to(ids, (SLOT, HEAD))
    source = lax.broadcasted_iota(jnp.int32, (HEAD, HEAD), 0)
    to = lax.broadcasted_iota(jnp.int32, (HEAD, HEAD), 1)
    origin = (to % SHARE) // GRANULE * (X * GRANULE) + to // SHARE * GRANULE + to % GRANULE
    turn = jnp.where(source == origin, 1.0, 0.0).astype(BF16)
    for h in range(HEADS_HERE):
        for part, ref in enumerate((q_ref, k_ref, v_ref)):
            block = ref[:, h * HEAD : (h + 1) * HEAD]
            if part == 2:
                block = jnp.dot(block, turn, preferred_element_type=F32)
            block = jnp.concatenate([block.astype(F32), jnp.zeros((16, HEAD), F32)], axis=0)
            for r, (start, length) in enumerate(zip(STARTS, LENGTHS)):
                piece = jnp.where(row < length, block[start : start + SLOT], 0.0)
                if part == 0:
                    piece = jnp.where(row == ID_ROW, id_rows[r], piece)
                    piece = jnp.where(row == ID_ROW + 1, every, piece)
                out_ref[PARTS * h + r, part * SLOT : (part + 1) * SLOT, :] = piece.astype(BF16)
    out_ref[PARTS * HEADS_HERE] = jnp.zeros((3 * SLOT, HEAD), BF16)


def attend(third_ref, q_ref, kv0_ref, kv1_ref, kv2_ref, kcode_ref, out_ref):
    rows = Z * SLOT
    third = third_ref[0]
    order = [third, lax.rem(third + 2, PARTS), lax.rem(third + 1, PARTS)]
    key_codes = [kcode_ref[pl.ds(j, 1), :] for j in order]
    keys = [ref[:, :SLOT, :].reshape(rows, HEAD) for ref in (kv0_ref, kv1_ref, kv2_ref)]
    ones = jnp.ones((rows, HEAD), BF16)
    vals = [
        jnp.concatenate([ref[:, SLOT:, :].reshape(rows, HEAD), ones], axis=1)
        for ref in (kv0_ref, kv1_ref, kv2_ref)
    ]
    tile = 16
    at = ID_ROW % tile
    ids = jnp.concatenate(
        [
            q_ref[x, z * SLOT + ID_ROW - at : z * SLOT + ID_ROW - at + tile, :].astype(F32)[at : at + 1]
            for x in range(X)
            for z in range(Z)
        ],
        axis=0,
    )
    which = lax.broadcasted_iota(jnp.int32, (X * Z, HEAD), 0)
    home = (X * (which % Z) + which // Z) * TOK + third * STARTS[1]
    first = ids * POSITIONS
    last = first + (home + lax.broadcasted_iota(jnp.int32, (X * Z, HEAD), 1)).astype(F32)
    codes = jnp.concatenate([first, last], axis=0).T
    lane = lax.broadcasted_iota(jnp.int32, (SLOT, HEAD), 1)
    stats = [jnp.zeros((SLOT, HEAD), F32) for _ in range(X)]
    group = 4
    for g in range(Z // group):
        count = -(-(g + 1) * group * SLOT // HEAD) * HEAD
        zs = range(g * group, (g + 1) * group)
        for x in range(X):
            low_code = jnp.concatenate([codes[:SLOT, x * Z + z : x * Z + z + 1] for z in zs], axis=0)
            high_code = jnp.concatenate(
                [codes[:SLOT, (X + x) * Z + z : (X + x) * Z + z + 1] for z in zs], axis=0
            )
            query = q_ref[x, g * group * SLOT : (g + 1) * group * SLOT, :]
            scores = []
            for j in range(PARTS):
                score = lax.dot_general(
                    query, keys[j][:count], (((1,), (1,)), ((), ())), preferred_element_type=F32
                ) * (HEAD ** (-0.5) * LOG2E)
                key_code = key_codes[j][:, :count]
                allowed = (key_code <= high_code) & (key_code >= low_code)
                scores.append(jnp.where(allowed, score, BLOCKED))
            peak = functools.reduce(jnp.maximum, [jnp.max(s, axis=1, keepdims=True) for s in scores])
            output = jnp.zeros((group * SLOT, 2 * HEAD), F32)
            for j in range(PARTS):
                expo = jnp.exp2(scores[j] - peak)
                output = output + jnp.dot(
                    expo.astype(BF16), vals[j][:count], preferred_element_type=F32
                )
            out_ref[x, g * group * SLOT : (g + 1) * group * SLOT, :] = (
                output[:, :HEAD] / output[:, HEAD:]
            ).astype(BF16)
            logsum = peak + jnp.log2(output[:, HEAD : HEAD + 1])
            high = logsum.astype(BF16).astype(F32)
            rest = logsum - high
            middle = rest.astype(BF16).astype(F32)
            low = rest - middle
            for n in range(group):
                for part, column in enumerate((high, middle, low)):
                    stats[x] = jnp.where(
                        lane == part * Z + g * group + n, column[n * SLOT : (n + 1) * SLOT], stats[x]
                    )
    for x in range(X):
        out_ref[x, rows:, :] = stats[x].astype(BF16)


def join(part_ref, out_ref):
    rows = Z * SLOT
    sums = []
    for x in range(X):
        stat = part_ref[x, rows:, :].astype(F32)
        sums.append(stat + pltpu.roll(stat, HEAD - Z, 1) + pltpu.roll(stat, HEAD - 2 * Z, 1))
    peak = functools.reduce(jnp.maximum, sums)
    weights = [jnp.exp2(s - peak) for s in sums]
    total = functools.reduce(jnp.add, weights)
    weights = [w / total for w in weights]
    share = lax.broadcasted_iota(jnp.int32, (16, HEAD), 1) // SHARE
    for z in range(Z):
        joined = functools.reduce(
            jnp.add,
            [
                weights[x][:, z : z + 1] * part_ref[x, z * SLOT : (z + 1) * SLOT, :].astype(F32)
                for x in range(X)
            ],
        )
        for x in range(X):
            slot = jnp.zeros((16, HEAD), F32)
            for n in range(SLOT // 16):
                piece = joined[16 * n : 16 * (n + 1)]
                if n != x:
                    piece = pltpu.roll(piece, (SHARE * (n - x)) % HEAD, 1)
                slot = jnp.where(share == n, piece, slot)
            out_ref[X * z + x] = slot.astype(BF16)


def assemble(part_ref, out_ref):
    share = lax.broadcasted_iota(jnp.int32, (16, HEAD), 1) // SHARE
    pieces = SLOT // 16
    for x in range(X):
        for r in range(PARTS):
            came = [part_ref[(PARTS * h + r) * X + x] for h in range(HEADS_HERE)]
            wide = [c.astype(F32) for c in came[:4]]
            for n in range(pieces):
                block = jnp.zeros((16, HEAD), F32)
                for h in range(4):
                    piece = wide[h] if h == n else pltpu.roll(wide[h], (SHARE * (h - n)) % HEAD, 1)
                    block = jnp.where(share == h, piece, block)
                first = ((x * PARTS + r) * pieces + n) * 16
                for y in range(Y):
                    out_ref[y, first : first + 16, :] = block.astype(BF16)
            first = X * PARTS * SLOT + (x * PARTS + r) * 16
            for y in range(Y):
                out_ref[y, first : first + 16, :] = came[4]


def project(core_ref, mine_ref, other_ref, weight_ref, out_ref):
    core = core_ref[0]
    depth = HEADS_HERE * SHARE
    pieces = SLOT // 16
    share = lax.broadcasted_iota(jnp.int32, (16, HEAD), 1) // SHARE
    weights = []
    for y in range(Y):
        for which in (core, 1 - core):
            first = pl.multiple_of((C * y + which) * depth, SHARE)
            fifth = weight_ref[pl.ds(first + HEAD, SHARE), :]
            weights += [weight_ref[pl.ds(first, HEAD), :]] + [fifth] * (HEAD // SHARE)
    weights = jnp.concatenate(weights, axis=0)
    for x in range(X):
        span = PARTS * SLOT
        inputs = []
        for y in range(Y):
            for ref in (mine_ref, other_ref):
                inputs.append(ref[y, x * span : (x + 1) * span, :])
                blocks = []
                for r in range(PARTS):
                    first = X * span + (x * PARTS + r) * 16
                    block = ref[y, first : first + 16, :].astype(F32)
                    blocks += [jnp.where(share == n, block, 0.0) for n in range(pieces)]
                inputs.append(jnp.concatenate(blocks, axis=0).astype(BF16))
        total = jnp.dot(jnp.concatenate(inputs, axis=1), weights, preferred_element_type=F32)
        total = [total[r * SLOT : r * SLOT + length] for r, length in enumerate(LENGTHS)]
        out_ref[x] = jnp.concatenate(total, axis=0).astype(BF16)


def share_rows(out_weight, side):
    width = out_weight.shape[1]
    own = out_weight.reshape(X + 1, GRANULE, width)
    ring = jnp.concatenate([own[:X], own[:X]], axis=0)
    came = lax.all_to_all(lax.dynamic_slice_in_dim(ring, X - side, X, axis=0), "x", 0, 0, tiled=True)
    place = jnp.arange(X + 1, dtype=jnp.int32)[:, None, None]
    earlier = jnp.concatenate([came, came[X - 1 :]], axis=0)
    later = jnp.concatenate([came[:1], came], axis=0)
    rows = jnp.where(place <= side, earlier, jnp.where(place == side + 1, own[X:], later))
    return rows.reshape((X + 1) * GRANULE, width)


def local(queries, keys_in, values, cluster_ids, out_weight):
    plane, side, core = lax.axis_index("z"), lax.axis_index("x"), lax.axis_index("c")
    third = lax.rem(plane, PARTS)
    width = out_weight.shape[1]

    send = vmem_call(
        scatter_heads,
        8,
        (Z, 3 * SLOT, HEAD),
        queries,
        keys_in,
        values,
        cluster_ids.reshape(1, TOK),
    )
    here = lax.all_to_all(send, "z", 0, 0, tiled=True)
    rows = share_rows(out_weight, side)
    here, rows = lax.optimization_barrier((here, rows))
    weight = lax.all_gather(rows, "z", axis=0, tiled=True)
    kv = here[:, SLOT:, :]
    turns = [
        [(PARTS * h + r, PARTS * h + (r + k) % PARTS) for h in range(HEADS_HERE) for r in range(PARTS)]
        for k in (1, 2)
    ]
    kv_others = [lax.ppermute(kv, "z", turn) for turn in turns]
    query = here[:, :SLOT, :].reshape(1, Z * SLOT, HEAD)
    query = lax.all_to_all(jnp.broadcast_to(query, (X, Z * SLOT, HEAD)), "x", 0, 0, tiled=True)

    home = (X * jnp.arange(Z, dtype=jnp.int32) + side) * TOK
    key_code = here[:, ID_ROW + 1, :].astype(F32) * POSITIONS + (
        home[:, None] + jnp.arange(HEAD, dtype=jnp.int32)[None, :]
    ).astype(F32)
    key_code = jnp.stack(
        [
            jnp.pad(
                key_code[:, start : start + length], ((0, 0), (0, SLOT - length)), constant_values=NEVER
            ).reshape(Z * SLOT)
            for start, length in zip(STARTS, LENGTHS)
        ]
    )
    part = vmem_call(
        attend,
        32,
        (X, (Z + 1) * SLOT, HEAD),
        query,
        kv,
        kv_others[0],
        kv_others[1],
        key_code,
        scalars=third.reshape(1),
    )
    part = lax.all_to_all(part, "x", 0, 0, tiled=True)
    joined = vmem_call(join, 8, (Z * X, 16, HEAD), part)
    joined = lax.all_to_all(joined, ("z", "x"), 0, 0, tiled=True)
    packed = vmem_call(assemble, 8, (Y, X * PARTS * (SLOT + 16), HEAD), joined)
    packed = lax.all_to_all(packed, "y", 0, 0, tiled=True)
    others = lax.ppermute(packed, "c", [(0, 1), (1, 0)])
    partial = vmem_call(
        project, 24, (X, TOK, width), packed, others, weight, scalars=core.reshape(1)
    )
    partial = lax.all_to_all(partial, "x", 0, 0, tiled=True)
    return jnp.sum(partial.astype(F32), axis=0).astype(BF16)


def solution(mesh):
    fine = Mesh(mesh.devices.reshape(Z, X, Y, C), ("z", "x", "y", "c"))
    both = P(("z", "x"), ("y", "c"))
    return jax.shard_map(
        local,
        mesh=fine,
        in_specs=(both, both, both, P(("z", "x"), None), both),
        out_specs=both,
        check_vma=False,
    )
```

```python
import functools

import jax
import jax.numpy as jnp
from jax import lax
from jax.experimental import pallas as pl
from jax.experimental.pallas import tpu as pltpu
from jax.sharding import Mesh
from jax.sharding import PartitionSpec as P

HEAD = 128
HEADS_HERE = 5
TOK = 128
Z, X, Y, C = 16, 4, 4, 2
PARTS = 3
STARTS = (0, 44, 88)
LENGTHS = (44, 44, 40)
SLOT = 48
ID_ROW = 46
POSITIONS = 8192
NEVER = 1e9
BLOCKED = -1e30
F32 = jnp.float32
BF16 = jnp.bfloat16
LOG2E = 1.4426950408889634
SHARE = 32
GRANULE = 16


def vmem_call(body, mebibytes, shapes, *operands, scalars=None):
    specs = [pl.BlockSpec(memory_space=pltpu.VMEM)] * len(operands)
    if scalars is not None:
        specs = [pl.BlockSpec(memory_space=pltpu.SMEM)] + specs
        operands = (scalars,) + operands
    return pl.pallas_call(
        body,
        out_shape=[jax.ShapeDtypeStruct(shape, BF16) for shape in shapes],
        in_specs=specs,
        out_specs=[pl.BlockSpec(memory_space=pltpu.VMEM)] * len(shapes),
        compiler_params=pltpu.CompilerParams(vmem_limit_bytes=mebibytes * 1024 * 1024),
    )(*operands)


def scatter_heads(q_ref, k_ref, v_ref, ids_ref, out_ref):
    ids = ids_ref[...].astype(F32)
    lane = lax.broadcasted_iota(jnp.int32, (SLOT, HEAD), 1)
    row = lax.broadcasted_iota(jnp.int32, (SLOT, HEAD), 0)
    id_rows = []
    for start, length in zip(STARTS, LENGTHS):
        moved = ids if start == 0 else pltpu.roll(ids, TOK - start, 1)
        id_rows.append(jnp.where(lane < length, jnp.broadcast_to(moved, (SLOT, HEAD)), -1.0))
    every = jnp.broadcast_to(ids, (SLOT, HEAD))
    source = lax.broadcasted_iota(jnp.int32, (HEAD, HEAD), 0)
    to = lax.broadcasted_iota(jnp.int32, (HEAD, HEAD), 1)
    origin = (to % SHARE) // GRANULE * (X * GRANULE) + to // SHARE * GRANULE + to % GRANULE
    turn = jnp.where(source == origin, 1.0, 0.0).astype(BF16)
    for h in range(HEADS_HERE):
        for part, ref in enumerate((q_ref, k_ref, v_ref)):
            block = ref[:, h * HEAD : (h + 1) * HEAD]
            if part == 2:
                block = jnp.dot(block, turn, preferred_element_type=F32)
            block = jnp.concatenate([block.astype(F32), jnp.zeros((16, HEAD), F32)], axis=0)
            for r, (start, length) in enumerate(zip(STARTS, LENGTHS)):
                piece = jnp.where(row < length, block[start : start + SLOT], 0.0)
                if part == 0:
                    piece = jnp.where(row == ID_ROW, id_rows[r], piece)
                elif part == 1:
                    piece = jnp.where(row == ID_ROW, every, piece)
                out_ref[PARTS * h + r, part * SLOT : (part + 1) * SLOT, :] = piece.astype(BF16)
    out_ref[PARTS * HEADS_HERE] = jnp.zeros((3 * SLOT, HEAD), BF16)


def attend(third_ref, q_ref, kv0_ref, kv1_ref, kv2_ref, kcode_ref, out_ref):
    rows = Z * SLOT
    third = third_ref[0]
    order = [third, lax.rem(third + 2, PARTS), lax.rem(third + 1, PARTS)]
    key_codes = [kcode_ref[pl.ds(j, 1), :] for j in order]
    keys = [ref[:, :SLOT, :].reshape(rows, HEAD) for ref in (kv0_ref, kv1_ref, kv2_ref)]
    ones = jnp.ones((rows, HEAD), BF16)
    vals = [
        jnp.concatenate([ref[:, SLOT:, :].reshape(rows, HEAD), ones], axis=1)
        for ref in (kv0_ref, kv1_ref, kv2_ref)
    ]
    tile = 16
    at = ID_ROW % tile
    ids = jnp.concatenate(
        [
            q_ref[x, z * SLOT + ID_ROW - at : z * SLOT + ID_ROW - at + tile, :].astype(F32)[at : at + 1]
            for x in range(X)
            for z in range(Z)
        ],
        axis=0,
    )
    which = lax.broadcasted_iota(jnp.int32, (X * Z, HEAD), 0)
    home = (X * (which % Z) + which // Z) * TOK + third * STARTS[1]
    first = ids * POSITIONS
    last = first + (home + lax.broadcasted_iota(jnp.int32, (X * Z, HEAD), 1)).astype(F32)
    codes = jnp.concatenate([first, last], axis=0).T
    lane = lax.broadcasted_iota(jnp.int32, (SLOT, HEAD), 1)
    stats = [jnp.zeros((SLOT, HEAD), F32) for _ in range(2)]
    group = 4
    share = lax.broadcasted_iota(jnp.int32, (group * SLOT, HEAD), 1) // SHARE
    for g in range(Z // group):
        count = -(-(g + 1) * group * SLOT // HEAD) * HEAD
        zs = range(g * group, (g + 1) * group)
        slots = [jnp.zeros((group * SLOT, HEAD), F32) for _ in range(X)]
        for x in range(X):
            low_code = jnp.concatenate([codes[:SLOT, x * Z + z : x * Z + z + 1] for z in zs], axis=0)
            high_code = jnp.concatenate(
                [codes[:SLOT, (X + x) * Z + z : (X + x) * Z + z + 1] for z in zs], axis=0
            )
            query = q_ref[x, g * group * SLOT : (g + 1) * group * SLOT, :]
            scores = []
            for j in range(PARTS):
                score = lax.dot_general(
                    query, keys[j][:count], (((1,), (1,)), ((), ())), preferred_element_type=F32
                ) * (HEAD ** (-0.5) * LOG2E)
                key_code = key_codes[j][:, :count]
                allowed = (key_code <= high_code) & (key_code >= low_code)
                scores.append(jnp.where(allowed, score, BLOCKED))
            peak = functools.reduce(jnp.maximum, [jnp.max(s, axis=1, keepdims=True) for s in scores])
            output = jnp.zeros((group * SLOT, 2 * HEAD), F32)
            for j in range(PARTS):
                expo = jnp.exp2(scores[j] - peak)
                output = output + jnp.dot(
                    expo.astype(BF16), vals[j][:count], preferred_element_type=F32
                )
            normal = output[:, :HEAD] / output[:, HEAD:]
            for to in range(X):
                piece = normal if to == x else pltpu.roll(normal, (SHARE * (x - to)) % HEAD, 1)
                slots[to] = jnp.where(share == x, piece, slots[to])
            logsum = peak + jnp.log2(output[:, HEAD : HEAD + 1])
            high = logsum.astype(BF16).astype(F32)
            rest = logsum - high
            middle = rest.astype(BF16).astype(F32)
            low = rest - middle
            for n in range(group):
                for part, column in enumerate((high, middle, low)):
                    at = part * X * Z + x * Z + g * group + n
                    stats[at // HEAD] = jnp.where(
                        lane == at % HEAD, column[n * SLOT : (n + 1) * SLOT], stats[at // HEAD]
                    )
        for x in range(X):
            out_ref[x, g * group * SLOT : (g + 1) * group * SLOT, :] = slots[x].astype(BF16)
    for x in range(X):
        out_ref[x, rows : rows + SLOT, :] = stats[0].astype(BF16)
        out_ref[x, rows + SLOT :, :] = stats[1].astype(BF16)


def join(part_ref, out_ref):
    rows = Z * SLOT
    sums = []
    for x in range(X):
        stat = part_ref[x, rows : rows + SLOT, :].astype(F32)
        rest = part_ref[x, rows + SLOT :, :].astype(F32)
        sums.append(stat + pltpu.roll(stat, HEAD // 2, 1) + rest)
    peak = functools.reduce(jnp.maximum, sums)
    weights = [jnp.exp2(s - peak) for s in sums]
    total = functools.reduce(jnp.add, weights)
    weights = [w / total for w in weights]
    share = lax.broadcasted_iota(jnp.int32, (SLOT, HEAD), 1) // SHARE
    for z in range(Z):
        joined = functools.reduce(
            jnp.add,
            [
                jnp.take_along_axis(weights[x], share * Z + z, axis=1)
                * part_ref[x, z * SLOT : (z + 1) * SLOT, :].astype(F32)
                for x in range(X)
            ],
        )
        out_ref[z] = joined.astype(BF16)


def assemble(part_ref, out_ref):
    share = lax.broadcasted_iota(jnp.int32, (SLOT, HEAD), 1) // SHARE
    for r in range(PARTS):
        came = [part_ref[PARTS * h + r] for h in range(HEADS_HERE)]
        wide = [c.astype(F32) for c in came[:4]]
        for x in range(X):
            block = jnp.zeros((SLOT, HEAD), F32)
            for h in range(4):
                piece = wide[h] if h == x else pltpu.roll(wide[h], (SHARE * (h - x)) % HEAD, 1)
                block = jnp.where(share == h, piece, block)
            first = (x * PARTS + r) * SLOT
            for y in range(Y):
                out_ref[y, first : first + SLOT, :] = block.astype(BF16)
        first = (X * PARTS + r) * SLOT
        for y in range(Y):
            out_ref[y, first : first + SLOT, :] = came[4]


def project(core_ref, mine_ref, other_ref, weight_ref, out_ref):
    core = core_ref[0]
    depth = HEADS_HERE * SHARE
    span = PARTS * SLOT
    share = lax.broadcasted_iota(jnp.int32, (span, HEAD), 1) // SHARE
    weights = []
    for y in range(Y):
        for which in (core, 1 - core):
            first = pl.multiple_of((C * y + which) * depth, SHARE)
            fifth = weight_ref[pl.ds(first + HEAD, SHARE), :]
            weights += [weight_ref[pl.ds(first, HEAD), :]] + [fifth] * (HEAD // SHARE)
    weights = jnp.concatenate(weights, axis=0)
    for x in range(X):
        inputs = []
        for y in range(Y):
            for ref in (mine_ref, other_ref):
                inputs.append(ref[y, x * span : (x + 1) * span, :])
                fifth = ref[y, X * span :, :].astype(F32)
                inputs.append(jnp.where(share == x, fifth, 0.0).astype(BF16))
        total = jnp.dot(jnp.concatenate(inputs, axis=1), weights, preferred_element_type=F32)
        total = [total[r * SLOT : r * SLOT + length] for r, length in enumerate(LENGTHS)]
        out_ref[x] = jnp.concatenate(total, axis=0).astype(BF16)


def share_rows(out_weight, side):
    width = out_weight.shape[1]
    own = out_weight.reshape(X + 1, GRANULE, width)
    ring = jnp.concatenate([own[:X], own[:X]], axis=0)
    came = lax.all_to_all(lax.dynamic_slice_in_dim(ring, X - side, X, axis=0), "x", 0, 0, tiled=True)
    place = jnp.arange(X + 1, dtype=jnp.int32)[:, None, None]
    earlier = jnp.concatenate([came, came[X - 1 :]], axis=0)
    later = jnp.concatenate([came[:1], came], axis=0)
    rows = jnp.where(place <= side, earlier, jnp.where(place == side + 1, own[X:], later))
    return rows.reshape((X + 1) * GRANULE, width)


def local(queries, keys_in, values, cluster_ids, out_weight):
    plane, side, core = lax.axis_index("z"), lax.axis_index("x"), lax.axis_index("c")
    third = lax.rem(plane, PARTS)
    width = out_weight.shape[1]

    (send,) = vmem_call(
        scatter_heads,
        56,
        [(Z, 3 * SLOT, HEAD)],
        queries,
        keys_in,
        values,
        cluster_ids.reshape(1, TOK),
    )
    weight = lax.all_gather(share_rows(out_weight, side), "z", axis=0, tiled=True)
    here = lax.all_to_all(send, "z", 0, 0, tiled=True)
    kv = here[:, SLOT:, :]
    turns = [
        [(PARTS * h + r, PARTS * h + (r + k) % PARTS) for h in range(HEADS_HERE) for r in range(PARTS)]
        for k in (1, 2)
    ]
    kv_others = [lax.ppermute(kv, "z", turn) for turn in turns]
    query = jnp.broadcast_to(here[:, :SLOT, :].reshape(1, Z * SLOT, HEAD), (X, Z * SLOT, HEAD))
    query = lax.all_to_all(query, "x", 0, 0, tiled=True)

    home = (X * jnp.arange(Z, dtype=jnp.int32) + side) * TOK
    key_code = kv[:, ID_ROW, :].astype(F32) * POSITIONS + (
        home[:, None] + jnp.arange(HEAD, dtype=jnp.int32)[None, :]
    ).astype(F32)
    key_code = jnp.stack(
        [
            jnp.pad(
                key_code[:, start : start + length], ((0, 0), (0, SLOT - length)), constant_values=NEVER
            ).reshape(Z * SLOT)
            for start, length in zip(STARTS, LENGTHS)
        ]
    )
    (part,) = vmem_call(
        attend,
        32,
        [(X, (Z + 2) * SLOT, HEAD)],
        query,
        kv,
        kv_others[0],
        kv_others[1],
        key_code,
        scalars=third.reshape(1),
    )
    part = lax.all_to_all(part, "x", 0, 0, tiled=True)
    (joined,) = vmem_call(join, 8, [(Z, SLOT, HEAD)], part)
    joined = lax.all_to_all(joined, "z", 0, 0, tiled=True)
    (packed,) = vmem_call(assemble, 8, [(Y, (X + 1) * PARTS * SLOT, HEAD)], joined)
    packed = lax.all_to_all(packed, "y", 0, 0, tiled=True)
    others = lax.ppermute(packed, "c", [(0, 1), (1, 0)])
    (partial,) = vmem_call(
        project, 24, [(X, TOK, width)], packed, others, weight, scalars=core.reshape(1)
    )
    partial = lax.all_to_all(partial, "x", 0, 0, tiled=True)
    return jnp.sum(partial.astype(F32), axis=0).astype(BF16)


def solution(mesh):
    fine = Mesh(mesh.devices.reshape(Z, X, Y, C), ("z", "x", "y", "c"))
    both = P(("z", "x"), ("y", "c"))
    return jax.shard_map(
        local,
        mesh=fine,
        in_specs=(both, both, both, P(("z", "x"), None), both),
        out_specs=both,
        check_vma=False,
    )
```

```python
import functools

import jax
import jax.numpy as jnp
from jax import lax
from jax.experimental import pallas as pl
from jax.experimental.pallas import tpu as pltpu
from jax.sharding import Mesh
from jax.sharding import PartitionSpec as P

HEAD = 128
HEADS_HERE = 5
TOK = 128
Z, X, Y, C = 16, 4, 4, 2
PARTS = 3
STARTS = (0, 44, 88)
LENGTHS = (44, 44, 40)
SLOT = 48
ID_ROW = 46
POSITIONS = 8192
NEVER = 1e9
BLOCKED = -1e30
F32 = jnp.float32
BF16 = jnp.bfloat16
LOG2E = 1.4426950408889634
SHARE = 32
GRANULE = 16


def vmem_call(body, mebibytes, shapes, *operands, scalars=None):
    specs = [pl.BlockSpec(memory_space=pltpu.VMEM)] * len(operands)
    if scalars is not None:
        specs = [pl.BlockSpec(memory_space=pltpu.SMEM)] + specs
        operands = (scalars,) + operands
    return pl.pallas_call(
        body,
        out_shape=[jax.ShapeDtypeStruct(shape, BF16) for shape in shapes],
        in_specs=specs,
        out_specs=[pl.BlockSpec(memory_space=pltpu.VMEM)] * len(shapes),
        compiler_params=pltpu.CompilerParams(vmem_limit_bytes=mebibytes * 1024 * 1024),
    )(*operands)


def scatter_heads(q_ref, k_ref, v_ref, ids_ref, weight_ref, out_ref, granules_ref):
    for n in range(X + 1):
        granules_ref[n] = weight_ref[n * GRANULE : (n + 1) * GRANULE, :]
    ids = ids_ref[...].astype(F32)
    lane = lax.broadcasted_iota(jnp.int32, (SLOT, HEAD), 1)
    row = lax.broadcasted_iota(jnp.int32, (SLOT, HEAD), 0)
    id_rows = []
    for start, length in zip(STARTS, LENGTHS):
        moved = ids if start == 0 else pltpu.roll(ids, TOK - start, 1)
        id_rows.append(jnp.where(lane < length, jnp.broadcast_to(moved, (SLOT, HEAD)), -1.0))
    every = jnp.broadcast_to(ids, (SLOT, HEAD))
    source = lax.broadcasted_iota(jnp.int32, (HEAD, HEAD), 0)
    to = lax.broadcasted_iota(jnp.int32, (HEAD, HEAD), 1)
    origin = (to % SHARE) // GRANULE * (X * GRANULE) + to // SHARE * GRANULE + to % GRANULE
    turn = jnp.where(source == origin, 1.0, 0.0).astype(BF16)
    for h in range(HEADS_HERE):
        for part, ref in enumerate((q_ref, k_ref, v_ref)):
            block = ref[:, h * HEAD : (h + 1) * HEAD]
            if part == 2:
                block = jnp.dot(block, turn, preferred_element_type=F32)
            block = jnp.concatenate([block.astype(F32), jnp.zeros((16, HEAD), F32)], axis=0)
            for r, (start, length) in enumerate(zip(STARTS, LENGTHS)):
                piece = jnp.where(row < length, block[start : start + SLOT], 0.0)
                if part == 0:
                    piece = jnp.where(row == ID_ROW, id_rows[r], piece)
                elif part == 1:
                    piece = jnp.where(row == ID_ROW, every, piece)
                out_ref[PARTS * h + r, part * SLOT : (part + 1) * SLOT, :] = piece.astype(BF16)
    out_ref[PARTS * HEADS_HERE] = jnp.zeros((3 * SLOT, HEAD), BF16)


def attend(third_ref, q_ref, kv0_ref, kv1_ref, kv2_ref, kcode_ref, out_ref):
    rows = Z * SLOT
    third = third_ref[0]
    order = [third, lax.rem(third + 2, PARTS), lax.rem(third + 1, PARTS)]
    key_codes = [kcode_ref[pl.ds(j, 1), :] for j in order]
    keys = [ref[:, :SLOT, :].reshape(rows, HEAD) for ref in (kv0_ref, kv1_ref, kv2_ref)]
    ones = jnp.ones((rows, HEAD), BF16)
    vals = [
        jnp.concatenate([ref[:, SLOT:, :].reshape(rows, HEAD), ones], axis=1)
        for ref in (kv0_ref, kv1_ref, kv2_ref)
    ]
    tile = 16
    at = ID_ROW % tile
    ids = jnp.concatenate(
        [
            q_ref[x, z * SLOT + ID_ROW - at : z * SLOT + ID_ROW - at + tile, :].astype(F32)[at : at + 1]
            for x in range(X)
            for z in range(Z)
        ],
        axis=0,
    )
    which = lax.broadcasted_iota(jnp.int32, (X * Z, HEAD), 0)
    home = (X * (which % Z) + which // Z) * TOK + third * STARTS[1]
    first = ids * POSITIONS
    last = first + (home + lax.broadcasted_iota(jnp.int32, (X * Z, HEAD), 1)).astype(F32)
    codes = jnp.concatenate([first, last], axis=0).T
    lane = lax.broadcasted_iota(jnp.int32, (SLOT, HEAD), 1)
    stats = [jnp.zeros((SLOT, HEAD), F32) for _ in range(2)]
    group = 4
    share = lax.broadcasted_iota(jnp.int32, (group * SLOT, HEAD), 1) // SHARE
    for g in range(Z // group):
        count = -(-(g + 1) * group * SLOT // HEAD) * HEAD
        zs = range(g * group, (g + 1) * group)
        slots = [jnp.zeros((group * SLOT, HEAD), F32) for _ in range(X)]
        for x in range(X):
            low_code = jnp.concatenate([codes[:SLOT, x * Z + z : x * Z + z + 1] for z in zs], axis=0)
            high_code = jnp.concatenate(
                [codes[:SLOT, (X + x) * Z + z : (X + x) * Z + z + 1] for z in zs], axis=0
            )
            query = q_ref[x, g * group * SLOT : (g + 1) * group * SLOT, :]
            scores = []
            for j in range(PARTS):
                score = lax.dot_general(
                    query, keys[j][:count], (((1,), (1,)), ((), ())), preferred_element_type=F32
                ) * (HEAD ** (-0.5) * LOG2E)
                key_code = key_codes[j][:, :count]
                allowed = (key_code <= high_code) & (key_code >= low_code)
                scores.append(jnp.where(allowed, score, BLOCKED))
            peak = functools.reduce(jnp.maximum, [jnp.max(s, axis=1, keepdims=True) for s in scores])
            output = jnp.zeros((group * SLOT, 2 * HEAD), F32)
            for j in range(PARTS):
                expo = jnp.exp2(scores[j] - peak)
                output = output + jnp.dot(
                    expo.astype(BF16), vals[j][:count], preferred_element_type=F32
                )
            normal = output[:, :HEAD] / output[:, HEAD:]
            for to in range(X):
                piece = normal if to == x else pltpu.roll(normal, (SHARE * (x - to)) % HEAD, 1)
                slots[to] = jnp.where(share == x, piece, slots[to])
            logsum = peak + jnp.log2(output[:, HEAD : HEAD + 1])
            high = logsum.astype(BF16).astype(F32)
            rest = logsum - high
            middle = rest.astype(BF16).astype(F32)
            low = rest - middle
            for n in range(group):
                for part, column in enumerate((high, middle, low)):
                    at = part * X * Z + x * Z + g * group + n
                    stats[at // HEAD] = jnp.where(
                        lane == at % HEAD, column[n * SLOT : (n + 1) * SLOT], stats[at // HEAD]
                    )
        for x in range(X):
            out_ref[x, g * group * SLOT : (g + 1) * group * SLOT, :] = slots[x].astype(BF16)
    for x in range(X):
        out_ref[x, rows : rows + SLOT, :] = stats[0].astype(BF16)
        out_ref[x, rows + SLOT :, :] = stats[1].astype(BF16)


def join(part_ref, out_ref):
    rows = Z * SLOT
    sums = []
    for x in range(X):
        stat = part_ref[x, rows : rows + SLOT, :].astype(F32)
        rest = part_ref[x, rows + SLOT :, :].astype(F32)
        sums.append(stat + pltpu.roll(stat, HEAD // 2, 1) + rest)
    peak = functools.reduce(jnp.maximum, sums)
    weights = [jnp.exp2(s - peak) for s in sums]
    total = functools.reduce(jnp.add, weights)
    weights = [w / total for w in weights]
    share = lax.broadcasted_iota(jnp.int32, (SLOT, HEAD), 1) // SHARE
    for z in range(Z):
        joined = functools.reduce(
            jnp.add,
            [
                jnp.take_along_axis(weights[x], share * Z + z, axis=1)
                * part_ref[x, z * SLOT : (z + 1) * SLOT, :].astype(F32)
                for x in range(X)
            ],
        )
        out_ref[z] = joined.astype(BF16)


def assemble(part_ref, out_ref):
    share = lax.broadcasted_iota(jnp.int32, (SLOT, HEAD), 1) // SHARE
    for r in range(PARTS):
        came = [part_ref[PARTS * h + r] for h in range(HEADS_HERE)]
        wide = [c.astype(F32) for c in came[:4]]
        for x in range(X):
            block = jnp.zeros((SLOT, HEAD), F32)
            for h in range(4):
                piece = wide[h] if h == x else pltpu.roll(wide[h], (SHARE * (h - x)) % HEAD, 1)
                block = jnp.where(share == h, piece, block)
            first = (x * PARTS + r) * SLOT
            for y in range(Y):
                out_ref[y, first : first + SLOT, :] = block.astype(BF16)
        first = (X * PARTS + r) * SLOT
        for y in range(Y):
            out_ref[y, first : first + SLOT, :] = came[4]


def project(place_ref, mine_ref, other_ref, weight_ref, out_ref):
    core, side = place_ref[0], place_ref[1]
    places = [lax.rem(side + (X + 1) - m, X + 1) * GRANULE for m in range(X + 1)]
    plane_rows = (X + 1) * GRANULE
    pieces = SHARE // GRANULE
    span = PARTS * SLOT
    share = lax.broadcasted_iota(jnp.int32, (span, HEAD), 1) // SHARE
    weights = []
    for y in range(Y):
        for which in (core, 1 - core):
            rows = []
            for n in range(HEADS_HERE * pieces):
                first = (C * y + which) * pieces * plane_rows + n // (X + 1) * plane_rows + places[n % (X + 1)]
                rows.append(weight_ref[pl.ds(pl.multiple_of(first, GRANULE), GRANULE), :])
            weights += rows[: 4 * pieces] + rows[4 * pieces :] * (HEAD // SHARE)
    weights = jnp.concatenate(weights, axis=0)
    for x in range(X):
        inputs = []
        for y in range(Y):
            for ref in (mine_ref, other_ref):
                inputs.append(ref[y, x * span : (x + 1) * span, :])
                fifth = ref[y, X * span :, :].astype(F32)
                inputs.append(jnp.where(share == x, fifth, 0.0).astype(BF16))
        total = jnp.dot(jnp.concatenate(inputs, axis=1), weights, preferred_element_type=F32)
        total = [total[r * SLOT : r * SLOT + length] for r, length in enumerate(LENGTHS)]
        out_ref[x] = jnp.concatenate(total, axis=0).astype(BF16)


def share_rows(granules):
    came = [granules[0]]
    for n in range(1, X):
        came.append(lax.ppermute(granules[n], "x", [(x, (x + n) % X) for x in range(X)]))
    return jnp.concatenate(came + [granules[X]], axis=0)


def local(queries, keys_in, values, cluster_ids, out_weight):
    plane, side, core = lax.axis_index("z"), lax.axis_index("x"), lax.axis_index("c")
    third = lax.rem(plane, PARTS)
    width = out_weight.shape[1]

    send, granules = vmem_call(
        scatter_heads,
        56,
        [(Z, 3 * SLOT, HEAD), (X + 1, GRANULE, width)],
        queries,
        keys_in,
        values,
        cluster_ids.reshape(1, TOK),
        out_weight,
    )
    here = lax.all_to_all(send, "z", 0, 0, tiled=True)
    weight = lax.all_gather(share_rows(granules), "z", axis=0, tiled=True)
    kv = here[:, SLOT:, :]
    turns = [
        [(PARTS * h + r, PARTS * h + (r + k) % PARTS) for h in range(HEADS_HERE) for r in range(PARTS)]
        for k in (1, 2)
    ]
    kv_others = [lax.ppermute(kv, "z", turn) for turn in turns]
    query = jnp.broadcast_to(here[:, :SLOT, :].reshape(1, Z * SLOT, HEAD), (X, Z * SLOT, HEAD))
    query = lax.all_to_all(query, "x", 0, 0, tiled=True)

    home = (X * jnp.arange(Z, dtype=jnp.int32) + side) * TOK
    key_code = kv[:, ID_ROW, :].astype(F32) * POSITIONS + (
        home[:, None] + jnp.arange(HEAD, dtype=jnp.int32)[None, :]
    ).astype(F32)
    key_code = jnp.stack(
        [
            jnp.pad(
                key_code[:, start : start + length], ((0, 0), (0, SLOT - length)), constant_values=NEVER
            ).reshape(Z * SLOT)
            for start, length in zip(STARTS, LENGTHS)
        ]
    )
    (part,) = vmem_call(
        attend,
        32,
        [(X, (Z + 2) * SLOT, HEAD)],
        query,
        kv,
        kv_others[0],
        kv_others[1],
        key_code,
        scalars=third.reshape(1),
    )
    part = lax.all_to_all(part, "x", 0, 0, tiled=True)
    (joined,) = vmem_call(join, 8, [(Z, SLOT, HEAD)], part)
    joined = lax.all_to_all(joined, "z", 0, 0, tiled=True)
    (packed,) = vmem_call(assemble, 8, [(Y, (X + 1) * PARTS * SLOT, HEAD)], joined)
    packed = lax.all_to_all(packed, "y", 0, 0, tiled=True)
    others = lax.ppermute(packed, "c", [(0, 1), (1, 0)])
    (partial,) = vmem_call(
        project, 24, [(X, TOK, width)], packed, others, weight, scalars=jnp.stack([core, side])
    )
    partial = lax.all_to_all(partial, "x", 0, 0, tiled=True)
    return jnp.sum(partial.astype(F32), axis=0).astype(BF16)


def solution(mesh):
    fine = Mesh(mesh.devices.reshape(Z, X, Y, C), ("z", "x", "y", "c"))
    both = P(("z", "x"), ("y", "c"))
    return jax.shard_map(
        local,
        mesh=fine,
        in_specs=(both, both, both, P(("z", "x"), None), both),
        out_specs=both,
        check_vma=False,
    )
```

```python
import functools

import jax
import jax.numpy as jnp
from jax import lax
from jax.experimental import pallas as pl
from jax.experimental.pallas import tpu as pltpu
from jax.sharding import Mesh
from jax.sharding import PartitionSpec as P

HEAD = 128
HEADS_HERE = 5
TOK = 128
Z, X, Y, C = 16, 4, 4, 2
PARTS = 3
STARTS = (0, 44, 88)
LENGTHS = (44, 44, 40)
SLOT = 48
ID_ROW = 46
POSITIONS = 8192
NEVER = 1e9
BLOCKED = -1e30
F32 = jnp.float32
BF16 = jnp.bfloat16
LOG2E = 1.4426950408889634
SHARE = 32
GRANULE = 16


def vmem_call(body, mebibytes, shapes, *operands, scalars=None, scratch=()):
    specs = [pl.BlockSpec(memory_space=pltpu.VMEM)] * len(operands)
    if scalars is not None:
        specs = [pl.BlockSpec(memory_space=pltpu.SMEM)] + specs
        operands = (scalars,) + operands
    return pl.pallas_call(
        body,
        out_shape=[jax.ShapeDtypeStruct(shape, BF16) for shape in shapes],
        in_specs=specs,
        out_specs=[pl.BlockSpec(memory_space=pltpu.VMEM)] * len(shapes),
        scratch_shapes=[pltpu.VMEM(shape, BF16) for shape in scratch],
        compiler_params=pltpu.CompilerParams(vmem_limit_bytes=mebibytes * 1024 * 1024),
    )(*operands)


def scatter_heads(q_ref, k_ref, v_ref, ids_ref, weight_ref, out_ref, granules_ref):
    for n in range(X + 1):
        granules_ref[n] = weight_ref[n * GRANULE : (n + 1) * GRANULE, :]
    ids = ids_ref[...].astype(F32)
    lane = lax.broadcasted_iota(jnp.int32, (SLOT, HEAD), 1)
    row = lax.broadcasted_iota(jnp.int32, (SLOT, HEAD), 0)
    id_rows = []
    for start, length in zip(STARTS, LENGTHS):
        moved = ids if start == 0 else pltpu.roll(ids, TOK - start, 1)
        id_rows.append(jnp.where(lane < length, jnp.broadcast_to(moved, (SLOT, HEAD)), -1.0))
    every = jnp.broadcast_to(ids, (SLOT, HEAD))
    source = lax.broadcasted_iota(jnp.int32, (HEAD, HEAD), 0)
    to = lax.broadcasted_iota(jnp.int32, (HEAD, HEAD), 1)
    origin = (to % SHARE) // GRANULE * (X * GRANULE) + to // SHARE * GRANULE + to % GRANULE
    turn = jnp.where(source == origin, 1.0, 0.0).astype(BF16)
    for h in range(HEADS_HERE):
        for part, ref in enumerate((q_ref, k_ref, v_ref)):
            block = ref[:, h * HEAD : (h + 1) * HEAD]
            if part == 2:
                block = jnp.dot(block, turn, preferred_element_type=F32)
            block = jnp.concatenate([block.astype(F32), jnp.zeros((16, HEAD), F32)], axis=0)
            for r, (start, length) in enumerate(zip(STARTS, LENGTHS)):
                piece = jnp.where(row < length, block[start : start + SLOT], 0.0)
                if part == 0:
                    piece = jnp.where(row == ID_ROW, id_rows[r], piece)
                elif part == 1:
                    piece = jnp.where(row == ID_ROW, every, piece)
                out_ref[PARTS * h + r, part * SLOT : (part + 1) * SLOT, :] = piece.astype(BF16)
    out_ref[PARTS * HEADS_HERE] = jnp.zeros((3 * SLOT, HEAD), BF16)


def attend(third_ref, q_ref, kv0_ref, kv1_ref, kv2_ref, kcode_ref, out_ref):
    rows = Z * SLOT
    third = third_ref[0]
    order = [third, lax.rem(third + 2, PARTS), lax.rem(third + 1, PARTS)]
    key_codes = [kcode_ref[pl.ds(j, 1), :] for j in order]
    keys = [ref[:, :SLOT, :].reshape(rows, HEAD) for ref in (kv0_ref, kv1_ref, kv2_ref)]
    ones = jnp.ones((rows, HEAD), BF16)
    vals = [
        jnp.concatenate([ref[:, SLOT:, :].reshape(rows, HEAD), ones], axis=1)
        for ref in (kv0_ref, kv1_ref, kv2_ref)
    ]
    tile = 16
    at = ID_ROW % tile
    ids = jnp.concatenate(
        [
            q_ref[x, z * SLOT + ID_ROW - at : z * SLOT + ID_ROW - at + tile, :].astype(F32)[at : at + 1]
            for x in range(X)
            for z in range(Z)
        ],
        axis=0,
    )
    which = lax.broadcasted_iota(jnp.int32, (X * Z, HEAD), 0)
    home = (X * (which % Z) + which // Z) * TOK + third * STARTS[1]
    first = ids * POSITIONS
    last = first + (home + lax.broadcasted_iota(jnp.int32, (X * Z, HEAD), 1)).astype(F32)
    codes = jnp.concatenate([first, last], axis=0).T
    lane = lax.broadcasted_iota(jnp.int32, (SLOT, HEAD), 1)
    stats = [jnp.zeros((SLOT, HEAD), F32) for _ in range(2)]
    group = 4
    share = lax.broadcasted_iota(jnp.int32, (group * SLOT, HEAD), 1) // SHARE
    for g in range(Z // group):
        count = -(-(g + 1) * group * SLOT // HEAD) * HEAD
        zs = range(g * group, (g + 1) * group)
        slots = [jnp.zeros((group * SLOT, HEAD), F32) for _ in range(X)]
        for x in range(X):
            low_code = jnp.concatenate([codes[:SLOT, x * Z + z : x * Z + z + 1] for z in zs], axis=0)
            high_code = jnp.concatenate(
                [codes[:SLOT, (X + x) * Z + z : (X + x) * Z + z + 1] for z in zs], axis=0
            )
            query = q_ref[x, g * group * SLOT : (g + 1) * group * SLOT, :]
            scores = []
            for j in range(PARTS):
                score = lax.dot_general(
                    query, keys[j][:count], (((1,), (1,)), ((), ())), preferred_element_type=F32
                ) * (HEAD ** (-0.5) * LOG2E)
                key_code = key_codes[j][:, :count]
                allowed = (key_code <= high_code) & (key_code >= low_code)
                scores.append(jnp.where(allowed, score, BLOCKED))
            peak = functools.reduce(jnp.maximum, [jnp.max(s, axis=1, keepdims=True) for s in scores])
            output = jnp.zeros((group * SLOT, 2 * HEAD), F32)
            for j in range(PARTS):
                expo = jnp.exp2(scores[j] - peak)
                output = output + jnp.dot(
                    expo.astype(BF16), vals[j][:count], preferred_element_type=F32
                )
            normal = output[:, :HEAD] / output[:, HEAD:]
            for to in range(X):
                piece = normal if to == x else pltpu.roll(normal, (SHARE * (x - to)) % HEAD, 1)
                slots[to] = jnp.where(share == x, piece, slots[to])
            logsum = peak + jnp.log2(output[:, HEAD : HEAD + 1])
            high = logsum.astype(BF16).astype(F32)
            rest = logsum - high
            middle = rest.astype(BF16).astype(F32)
            low = rest - middle
            for n in range(group):
                for part, column in enumerate((high, middle, low)):
                    at = part * X * Z + x * Z + g * group + n
                    stats[at // HEAD] = jnp.where(
                        lane == at % HEAD, column[n * SLOT : (n + 1) * SLOT], stats[at // HEAD]
                    )
        for x in range(X):
            out_ref[x, g * group * SLOT : (g + 1) * group * SLOT, :] = slots[x].astype(BF16)
    for x in range(X):
        out_ref[x, rows : rows + SLOT, :] = stats[0].astype(BF16)
        out_ref[x, rows + SLOT :, :] = stats[1].astype(BF16)


def join(part_ref, out_ref):
    rows = Z * SLOT
    sums = []
    for x in range(X):
        stat = part_ref[x, rows : rows + SLOT, :].astype(F32)
        rest = part_ref[x, rows + SLOT :, :].astype(F32)
        sums.append(stat + pltpu.roll(stat, HEAD // 2, 1) + rest)
    peak = functools.reduce(jnp.maximum, sums)
    weights = [jnp.exp2(s - peak) for s in sums]
    total = functools.reduce(jnp.add, weights)
    weights = [w / total for w in weights]
    share = lax.broadcasted_iota(jnp.int32, (SLOT, HEAD), 1) // SHARE
    for z in range(Z):
        joined = functools.reduce(
            jnp.add,
            [
                jnp.take_along_axis(weights[x], share * Z + z, axis=1)
                * part_ref[x, z * SLOT : (z + 1) * SLOT, :].astype(F32)
                for x in range(X)
            ],
        )
        out_ref[z] = joined.astype(BF16)


def assemble(part_ref, out_ref):
    share = lax.broadcasted_iota(jnp.int32, (SLOT, HEAD), 1) // SHARE
    for r in range(PARTS):
        came = [part_ref[PARTS * h + r] for h in range(HEADS_HERE)]
        wide = [c.astype(F32) for c in came[:4]]
        for x in range(X):
            block = jnp.zeros((SLOT, HEAD), F32)
            for h in range(4):
                piece = wide[h] if h == x else pltpu.roll(wide[h], (SHARE * (h - x)) % HEAD, 1)
                block = jnp.where(share == h, piece, block)
            first = (x * PARTS + r) * SLOT
            for y in range(Y):
                out_ref[y, first : first + SLOT, :] = block.astype(BF16)
        first = (X * PARTS + r) * SLOT
        for y in range(Y):
            out_ref[y, first : first + SLOT, :] = came[4]


def project(place_ref, mine_ref, other_ref, *refs):
    parts, out_ref, weight_ref = refs[:Z], refs[Z], refs[Z + 1]
    core, side, plane = place_ref[0], place_ref[1], place_ref[2]
    for n, part in enumerate(parts):
        turn = Z - n if n <= Z // 2 else n - Z // 2
        first = pl.multiple_of(lax.rem(plane + turn, Z) * part.shape[0], GRANULE)
        weight_ref[pl.ds(first, part.shape[0]), :] = part[...]
    places = [lax.rem(side + (X + 1) - m, X + 1) * GRANULE for m in range(X + 1)]
    plane_rows = (X + 1) * GRANULE
    pieces = SHARE // GRANULE
    span = PARTS * SLOT
    share = lax.broadcasted_iota(jnp.int32, (span, HEAD), 1) // SHARE
    weights = []
    for y in range(Y):
        for which in (core, 1 - core):
            rows = []
            for n in range(HEADS_HERE * pieces):
                first = (C * y + which) * pieces * plane_rows + n // (X + 1) * plane_rows + places[n % (X + 1)]
                rows.append(weight_ref[pl.ds(pl.multiple_of(first, GRANULE), GRANULE), :])
            weights += rows[: 4 * pieces] + rows[4 * pieces :] * (HEAD // SHARE)
    weights = jnp.concatenate(weights, axis=0)
    for x in range(X):
        inputs = []
        for y in range(Y):
            for ref in (mine_ref, other_ref):
                inputs.append(ref[y, x * span : (x + 1) * span, :])
                fifth = ref[y, X * span :, :].astype(F32)
                inputs.append(jnp.where(share == x, fifth, 0.0).astype(BF16))
        total = jnp.dot(jnp.concatenate(inputs, axis=1), weights, preferred_element_type=F32)
        total = [total[r * SLOT : r * SLOT + length] for r, length in enumerate(LENGTHS)]
        out_ref[x] = jnp.concatenate(total, axis=0).astype(BF16)


def share_rows(granules):
    came = [granules[0]]
    for n in range(1, X):
        came.append(lax.ppermute(granules[n], "x", [(x, (x + n) % X) for x in range(X)]))
    return jnp.concatenate(came + [granules[X]], axis=0)


class Ring:
    def __init__(self, block):
        self.up, self.down = [block], [block]

    def step(self):
        if len(self.up) <= Z // 2:
            self.up.append(lax.ppermute(self.up[-1], "z", [(z, (z + 1) % Z) for z in range(Z)]))
        if len(self.down) < Z // 2:
            self.down.append(lax.ppermute(self.down[-1], "z", [(z, (z - 1) % Z) for z in range(Z)]))

    def meet(self, value):
        value, self.up[-1], self.down[-1] = lax.optimization_barrier((value, self.up[-1], self.down[-1]))
        return value

    def blocks(self):
        return self.up + self.down[1:]


def local(queries, keys_in, values, cluster_ids, out_weight):
    plane, side, core = lax.axis_index("z"), lax.axis_index("x"), lax.axis_index("c")
    third = lax.rem(plane, PARTS)
    width = out_weight.shape[1]

    send, granules = vmem_call(
        scatter_heads,
        56,
        [(Z, 3 * SLOT, HEAD), (X + 1, GRANULE, width)],
        queries,
        keys_in,
        values,
        cluster_ids.reshape(1, TOK),
        out_weight,
    )
    here = lax.all_to_all(send, "z", 0, 0, tiled=True)
    ring = Ring(share_rows(granules))
    ring.step()
    here = ring.meet(here)
    kv = here[:, SLOT:, :]
    turns = [
        [(PARTS * h + r, PARTS * h + (r + k) % PARTS) for h in range(HEADS_HERE) for r in range(PARTS)]
        for k in (1, 2)
    ]
    kv_others = [lax.ppermute(kv, "z", turn) for turn in turns]
    ring.step()
    query = jnp.broadcast_to(here[:, :SLOT, :].reshape(1, Z * SLOT, HEAD), (X, Z * SLOT, HEAD))
    query = lax.all_to_all(query, "x", 0, 0, tiled=True)

    home = (X * jnp.arange(Z, dtype=jnp.int32) + side) * TOK
    key_code = kv[:, ID_ROW, :].astype(F32) * POSITIONS + (
        home[:, None] + jnp.arange(HEAD, dtype=jnp.int32)[None, :]
    ).astype(F32)
    key_code = jnp.stack(
        [
            jnp.pad(
                key_code[:, start : start + length], ((0, 0), (0, SLOT - length)), constant_values=NEVER
            ).reshape(Z * SLOT)
            for start, length in zip(STARTS, LENGTHS)
        ]
    )
    (part,) = vmem_call(
        attend,
        32,
        [(X, (Z + 2) * SLOT, HEAD)],
        query,
        kv,
        kv_others[0],
        kv_others[1],
        key_code,
        scalars=third.reshape(1),
    )
    part = lax.all_to_all(ring.meet(part), "x", 0, 0, tiled=True)
    ring.step()
    ring.step()
    (joined,) = vmem_call(join, 8, [(Z, SLOT, HEAD)], part)
    joined = lax.all_to_all(ring.meet(joined), "z", 0, 0, tiled=True)
    ring.step()
    ring.step()
    (packed,) = vmem_call(assemble, 8, [(Y, (X + 1) * PARTS * SLOT, HEAD)], joined)
    packed = lax.all_to_all(ring.meet(packed), "y", 0, 0, tiled=True)
    ring.step()
    ring.step()
    packed = ring.meet(packed)
    others = lax.ppermute(packed, "c", [(0, 1), (1, 0)])
    (partial,) = vmem_call(
        project,
        24,
        [(X, TOK, width)],
        packed,
        others,
        *ring.blocks(),
        scalars=jnp.stack([core, side, plane]),
        scratch=[(Z * out_weight.shape[0], width)],
    )
    partial = lax.all_to_all(partial, "x", 0, 0, tiled=True)
    return jnp.sum(partial.astype(F32), axis=0).astype(BF16)


def solution(mesh):
    fine = Mesh(mesh.devices.reshape(Z, X, Y, C), ("z", "x", "y", "c"))
    both = P(("z", "x"), ("y", "c"))
    return jax.shard_map(
        local,
        mesh=fine,
        in_specs=(both, both, both, P(("z", "x"), None), both),
        out_specs=both,
        check_vma=False,
    )
```

```python
import functools

import jax
import jax.numpy as jnp
from jax import lax
from jax.experimental import pallas as pl
from jax.experimental.pallas import tpu as pltpu
from jax.sharding import Mesh
from jax.sharding import PartitionSpec as P

HEAD = 128
HEADS_HERE = 5
TOK = 128
Z, X, Y, C = 16, 4, 4, 2
PARTS = 3
STARTS = (0, 44, 88)
LENGTHS = (44, 44, 40)
SLOT = 48
ID_ROW = 46
POSITIONS = 8192
NEVER = 1e9
BLOCKED = -1e30
F32 = jnp.float32
BF16 = jnp.bfloat16
LOG2E = 1.4426950408889634
SHARE = 32
GRANULE = 16


def vmem_call(body, mebibytes, shapes, *operands, scalars=None, left=(), scratch=()):
    specs = [pl.BlockSpec(memory_space=pltpu.VMEM)] * len(operands)
    specs += [pl.BlockSpec(memory_space=pl.ANY)] * len(left)
    operands += tuple(left)
    if scalars is not None:
        specs = [pl.BlockSpec(memory_space=pltpu.SMEM)] + specs
        operands = (scalars,) + operands
    return pl.pallas_call(
        body,
        out_shape=[jax.ShapeDtypeStruct(shape, BF16) for shape in shapes],
        in_specs=specs,
        out_specs=[pl.BlockSpec(memory_space=pltpu.VMEM)] * len(shapes),
        scratch_shapes=list(scratch),
        compiler_params=pltpu.CompilerParams(vmem_limit_bytes=mebibytes * 1024 * 1024),
    )(*operands)


def scatter_heads(q_ref, k_ref, v_ref, ids_ref, weight_ref, out_ref, granules_ref):
    for n in range(X + 1):
        granules_ref[n] = weight_ref[n * GRANULE : (n + 1) * GRANULE, :]
    ids = ids_ref[...].astype(F32)
    lane = lax.broadcasted_iota(jnp.int32, (SLOT, HEAD), 1)
    row = lax.broadcasted_iota(jnp.int32, (SLOT, HEAD), 0)
    id_rows = []
    for start, length in zip(STARTS, LENGTHS):
        moved = ids if start == 0 else pltpu.roll(ids, TOK - start, 1)
        id_rows.append(jnp.where(lane < length, jnp.broadcast_to(moved, (SLOT, HEAD)), -1.0))
    every = jnp.broadcast_to(ids, (SLOT, HEAD))
    source = lax.broadcasted_iota(jnp.int32, (HEAD, HEAD), 0)
    to = lax.broadcasted_iota(jnp.int32, (HEAD, HEAD), 1)
    origin = (to % SHARE) // GRANULE * (X * GRANULE) + to // SHARE * GRANULE + to % GRANULE
    turn = jnp.where(source == origin, 1.0, 0.0).astype(BF16)
    for h in range(HEADS_HERE):
        for part, ref in enumerate((q_ref, k_ref, v_ref)):
            block = ref[:, h * HEAD : (h + 1) * HEAD]
            if part == 2:
                block = jnp.dot(block, turn, preferred_element_type=F32)
            block = jnp.concatenate([block.astype(F32), jnp.zeros((16, HEAD), F32)], axis=0)
            for r, (start, length) in enumerate(zip(STARTS, LENGTHS)):
                piece = jnp.where(row < length, block[start : start + SLOT], 0.0)
                if part == 0:
                    piece = jnp.where(row == ID_ROW, id_rows[r], piece)
                elif part == 1:
                    piece = jnp.where(row == ID_ROW, every, piece)
                out_ref[PARTS * h + r, part * SLOT : (part + 1) * SLOT, :] = piece.astype(BF16)
    out_ref[PARTS * HEADS_HERE] = jnp.zeros((3 * SLOT, HEAD), BF16)


def attend(third_ref, q_ref, kv0_ref, kv1_ref, kv2_ref, kcode_ref, out_ref):
    rows = Z * SLOT
    third = third_ref[0]
    order = [third, lax.rem(third + 2, PARTS), lax.rem(third + 1, PARTS)]
    key_codes = [kcode_ref[pl.ds(j, 1), :] for j in order]
    keys = [ref[:, :SLOT, :].reshape(rows, HEAD) for ref in (kv0_ref, kv1_ref, kv2_ref)]
    ones = jnp.ones((rows, HEAD), BF16)
    vals = [
        jnp.concatenate([ref[:, SLOT:, :].reshape(rows, HEAD), ones], axis=1)
        for ref in (kv0_ref, kv1_ref, kv2_ref)
    ]
    tile = 16
    at = ID_ROW % tile
    ids = jnp.concatenate(
        [
            q_ref[x, z * SLOT + ID_ROW - at : z * SLOT + ID_ROW - at + tile, :].astype(F32)[at : at + 1]
            for x in range(X)
            for z in range(Z)
        ],
        axis=0,
    )
    which = lax.broadcasted_iota(jnp.int32, (X * Z, HEAD), 0)
    home = (X * (which % Z) + which // Z) * TOK + third * STARTS[1]
    first = ids * POSITIONS
    last = first + (home + lax.broadcasted_iota(jnp.int32, (X * Z, HEAD), 1)).astype(F32)
    codes = jnp.concatenate([first, last], axis=0).T
    lane = lax.broadcasted_iota(jnp.int32, (SLOT, HEAD), 1)
    stats = [jnp.zeros((SLOT, HEAD), F32) for _ in range(2)]
    group = 4
    share = lax.broadcasted_iota(jnp.int32, (group * SLOT, HEAD), 1) // SHARE
    for g in range(Z // group):
        count = -(-(g + 1) * group * SLOT // HEAD) * HEAD
        zs = range(g * group, (g + 1) * group)
        slots = [jnp.zeros((group * SLOT, HEAD), F32) for _ in range(X)]
        for x in range(X):
            low_code = jnp.concatenate([codes[:SLOT, x * Z + z : x * Z + z + 1] for z in zs], axis=0)
            high_code = jnp.concatenate(
                [codes[:SLOT, (X + x) * Z + z : (X + x) * Z + z + 1] for z in zs], axis=0
            )
            query = q_ref[x, g * group * SLOT : (g + 1) * group * SLOT, :]
            scores = []
            for j in range(PARTS):
                score = lax.dot_general(
                    query, keys[j][:count], (((1,), (1,)), ((), ())), preferred_element_type=F32
                ) * (HEAD ** (-0.5) * LOG2E)
                key_code = key_codes[j][:, :count]
                allowed = (key_code <= high_code) & (key_code >= low_code)
                scores.append(jnp.where(allowed, score, BLOCKED))
            peak = functools.reduce(jnp.maximum, [jnp.max(s, axis=1, keepdims=True) for s in scores])
            output = jnp.zeros((group * SLOT, 2 * HEAD), F32)
            for j in range(PARTS):
                expo = jnp.exp2(scores[j] - peak)
                output = output + jnp.dot(
                    expo.astype(BF16), vals[j][:count], preferred_element_type=F32
                )
            normal = output[:, :HEAD] / output[:, HEAD:]
            for to in range(X):
                piece = normal if to == x else pltpu.roll(normal, (SHARE * (x - to)) % HEAD, 1)
                slots[to] = jnp.where(share == x, piece, slots[to])
            logsum = peak + jnp.log2(output[:, HEAD : HEAD + 1])
            high = logsum.astype(BF16).astype(F32)
            rest = logsum - high
            middle = rest.astype(BF16).astype(F32)
            low = rest - middle
            for n in range(group):
                for part, column in enumerate((high, middle, low)):
                    at = part * X * Z + x * Z + g * group + n
                    stats[at // HEAD] = jnp.where(
                        lane == at % HEAD, column[n * SLOT : (n + 1) * SLOT], stats[at // HEAD]
                    )
        for x in range(X):
            out_ref[x, g * group * SLOT : (g + 1) * group * SLOT, :] = slots[x].astype(BF16)
    for x in range(X):
        out_ref[x, rows : rows + SLOT, :] = stats[0].astype(BF16)
        out_ref[x, rows + SLOT :, :] = stats[1].astype(BF16)


def join(part_ref, out_ref):
    rows = Z * SLOT
    sums = []
    for x in range(X):
        stat = part_ref[x, rows : rows + SLOT, :].astype(F32)
        rest = part_ref[x, rows + SLOT :, :].astype(F32)
        sums.append(stat + pltpu.roll(stat, HEAD // 2, 1) + rest)
    peak = functools.reduce(jnp.maximum, sums)
    weights = [jnp.exp2(s - peak) for s in sums]
    total = functools.reduce(jnp.add, weights)
    weights = [w / total for w in weights]
    share = lax.broadcasted_iota(jnp.int32, (SLOT, HEAD), 1) // SHARE
    for z in range(Z):
        joined = functools.reduce(
            jnp.add,
            [
                jnp.take_along_axis(weights[x], share * Z + z, axis=1)
                * part_ref[x, z * SLOT : (z + 1) * SLOT, :].astype(F32)
                for x in range(X)
            ],
        )
        out_ref[z] = joined.astype(BF16)


def assemble(part_ref, out_ref):
    share = lax.broadcasted_iota(jnp.int32, (SLOT, HEAD), 1) // SHARE
    for r in range(PARTS):
        came = [part_ref[PARTS * h + r] for h in range(HEADS_HERE)]
        wide = [c.astype(F32) for c in came[:4]]
        for x in range(X):
            block = jnp.zeros((SLOT, HEAD), F32)
            for h in range(4):
                piece = wide[h] if h == x else pltpu.roll(wide[h], (SHARE * (h - x)) % HEAD, 1)
                block = jnp.where(share == h, piece, block)
            first = (x * PARTS + r) * SLOT
            for y in range(Y):
                out_ref[y, first : first + SLOT, :] = block.astype(BF16)
        first = (X * PARTS + r) * SLOT
        for y in range(Y):
            out_ref[y, first : first + SLOT, :] = came[4]


def project(place_ref, mine_ref, other_ref, *refs):
    half = Z // 2
    own, others, out_ref, weight_ref, sems = refs
    core, side, plane = place_ref[0], place_ref[1], place_ref[2]
    depth = weight_ref.shape[0] // Z
    way = 1 - 2 * core
    copies = []
    for n in range(half + 1):
        pairs = [(own.at[n], Z - way * n)]
        if 0 < n < half:
            pairs.append((others.at[n - 1], Z + way * n))
        for source, turn in pairs:
            first = pl.multiple_of(lax.rem(plane + turn, Z) * depth, GRANULE)
            place = weight_ref.at[pl.ds(first, depth), :]
            copies.append(pltpu.make_async_copy(source, place, sems.at[len(copies)]))
    for copy in copies:
        copy.start()
    for copy in copies:
        copy.wait()
    places = [lax.rem(side + (X + 1) - m, X + 1) * GRANULE for m in range(X + 1)]
    plane_rows = (X + 1) * GRANULE
    pieces = SHARE // GRANULE
    span = PARTS * SLOT
    share = lax.broadcasted_iota(jnp.int32, (span, HEAD), 1) // SHARE
    weights = []
    for y in range(Y):
        for which in (core, 1 - core):
            rows = []
            for n in range(HEADS_HERE * pieces):
                first = (C * y + which) * pieces * plane_rows + n // (X + 1) * plane_rows + places[n % (X + 1)]
                rows.append(weight_ref[pl.ds(pl.multiple_of(first, GRANULE), GRANULE), :])
            weights += rows[: 4 * pieces] + rows[4 * pieces :] * (HEAD // SHARE)
    weights = jnp.concatenate(weights, axis=0)
    for x in range(X):
        inputs = []
        for y in range(Y):
            for ref in (mine_ref, other_ref):
                inputs.append(ref[y, x * span : (x + 1) * span, :])
                fifth = ref[y, X * span :, :].astype(F32)
                inputs.append(jnp.where(share == x, fifth, 0.0).astype(BF16))
        total = jnp.dot(jnp.concatenate(inputs, axis=1), weights, preferred_element_type=F32)
        total = [total[r * SLOT : r * SLOT + length] for r, length in enumerate(LENGTHS)]
        out_ref[x] = jnp.concatenate(total, axis=0).astype(BF16)


def share_rows(granules):
    came = [granules[0]]
    for n in range(1, X):
        came.append(lax.ppermute(granules[n], "x", [(x, (x + n) % X) for x in range(X)]))
    return jnp.concatenate(came + [granules[X]], axis=0)


class Ring:
    def __init__(self, block):
        self.came = [jnp.stack([block, swap_cores(block)])]

    def step(self):
        turn = [(C * z + c, C * ((z + 1 - 2 * c) % Z) + c) for z in range(Z) for c in range(C)]
        self.came.append(lax.ppermute(self.came[-1], ("z", "c"), turn))

    def meet(self, value):
        value, self.came[-1] = lax.optimization_barrier((value, self.came[-1]))
        return value


def swap_cores(value):
    return lax.ppermute(value, "c", [(0, 1), (1, 0)])


def local(queries, keys_in, values, cluster_ids, out_weight):
    plane, side, core = lax.axis_index("z"), lax.axis_index("x"), lax.axis_index("c")
    third = lax.rem(plane, PARTS)
    width = out_weight.shape[1]

    send, granules = vmem_call(
        scatter_heads,
        56,
        [(Z, 3 * SLOT, HEAD), (X + 1, GRANULE, width)],
        queries,
        keys_in,
        values,
        cluster_ids.reshape(1, TOK),
        out_weight,
    )
    here = lax.all_to_all(send, "z", 0, 0, tiled=True)
    ring = Ring(share_rows(granules))
    ring.step()
    here = ring.meet(here)
    kv = here[:, SLOT:, :]
    turns = [
        [(PARTS * h + r, PARTS * h + (r + k) % PARTS) for h in range(HEADS_HERE) for r in range(PARTS)]
        for k in (1, 2)
    ]
    kv_others = [lax.ppermute(kv, "z", turn) for turn in turns]
    ring.step()
    ring.step()
    query = jnp.broadcast_to(here[:, :SLOT, :].reshape(1, Z * SLOT, HEAD), (X, Z * SLOT, HEAD))
    query = lax.all_to_all(query, "x", 0, 0, tiled=True)

    home = (X * jnp.arange(Z, dtype=jnp.int32) + side) * TOK
    key_code = kv[:, ID_ROW, :].astype(F32) * POSITIONS + (
        home[:, None] + jnp.arange(HEAD, dtype=jnp.int32)[None, :]
    ).astype(F32)
    key_code = jnp.stack(
        [
            jnp.pad(
                key_code[:, start : start + length], ((0, 0), (0, SLOT - length)), constant_values=NEVER
            ).reshape(Z * SLOT)
            for start, length in zip(STARTS, LENGTHS)
        ]
    )
    (part,) = vmem_call(
        attend,
        18,
        [(X, (Z + 2) * SLOT, HEAD)],
        query,
        kv,
        kv_others[0],
        kv_others[1],
        key_code,
        scalars=third.reshape(1),
    )
    part = lax.all_to_all(ring.meet(part), "x", 0, 0, tiled=True)
    ring.step()
    ring.step()
    (joined,) = vmem_call(join, 8, [(Z, SLOT, HEAD)], part)
    joined = lax.all_to_all(ring.meet(joined), "z", 0, 0, tiled=True)
    ring.step()
    ring.step()
    (packed,) = vmem_call(assemble, 8, [(Y, (X + 1) * PARTS * SLOT, HEAD)], joined)
    packed = lax.all_to_all(ring.meet(packed), "y", 0, 0, tiled=True)
    ring.step()
    rows = swap_cores(jnp.stack([block[1] for block in ring.came[1 : Z // 2]]))
    packed, rows = lax.optimization_barrier((packed, rows))
    packed = ring.meet(packed)
    others = swap_cores(packed)
    (partial,) = vmem_call(
        project,
        16,
        [(X, TOK, width)],
        packed,
        others,
        scalars=jnp.stack([core, side, plane]),
        left=[jnp.stack([block[0] for block in ring.came]), rows],
        scratch=[pltpu.VMEM((Z * out_weight.shape[0], width), BF16), pltpu.SemaphoreType.DMA((Z,))],
    )
    partial = lax.all_to_all(partial, "x", 0, 0, tiled=True)
    return jnp.sum(partial.astype(F32), axis=0).astype(BF16)


def solution(mesh):
    fine = Mesh(mesh.devices.reshape(Z, X, Y, C), ("z", "x", "y", "c"))
    both = P(("z", "x"), ("y", "c"))
    return jax.shard_map(
        local,
        mesh=fine,
        in_specs=(both, both, both, P(("z", "x"), None), both),
        out_specs=both,
        check_vma=False,
    )
```

```python
import functools

import jax
import jax.numpy as jnp
from jax import lax
from jax.experimental import pallas as pl
from jax.experimental.pallas import tpu as pltpu
from jax.sharding import Mesh
from jax.sharding import PartitionSpec as P

HEAD = 128
HEADS_HERE = 5
TOK = 128
Z, X, Y, C = 16, 4, 4, 2
PARTS = 3
STARTS = (0, 44, 88)
LENGTHS = (44, 44, 40)
SLOT = 48
ID_ROW = 46
POSITIONS = 8192
NEVER = 1e9
BLOCKED = -1e30
F32 = jnp.float32
BF16 = jnp.bfloat16
LOG2E = 1.4426950408889634
SHARE = 32
GRANULE = 16


def vmem_call(body, mebibytes, shapes, *operands, scalars=None, kind=BF16):
    specs = [pl.BlockSpec(memory_space=pltpu.VMEM)] * len(operands)
    if scalars is not None:
        specs = [pl.BlockSpec(memory_space=pltpu.SMEM)] + specs
        operands = (scalars,) + operands
    return pl.pallas_call(
        body,
        out_shape=[jax.ShapeDtypeStruct(shape, kind) for shape in shapes],
        in_specs=specs,
        out_specs=[pl.BlockSpec(memory_space=pltpu.VMEM)] * len(shapes),
        compiler_params=pltpu.CompilerParams(vmem_limit_bytes=mebibytes * 1024 * 1024),
    )(*operands)


def scatter_heads(q_ref, k_ref, v_ref, ids_ref, weight_ref, out_ref, granules_ref):
    for n in range(X + 1):
        granules_ref[n] = weight_ref[n * GRANULE : (n + 1) * GRANULE, :]
    ids = ids_ref[...].astype(F32)
    lane = lax.broadcasted_iota(jnp.int32, (SLOT, HEAD), 1)
    row = lax.broadcasted_iota(jnp.int32, (SLOT, HEAD), 0)
    id_rows = []
    for start, length in zip(STARTS, LENGTHS):
        moved = ids if start == 0 else pltpu.roll(ids, TOK - start, 1)
        id_rows.append(jnp.where(lane < length, jnp.broadcast_to(moved, (SLOT, HEAD)), -1.0))
    every = jnp.broadcast_to(ids, (SLOT, HEAD))
    source = lax.broadcasted_iota(jnp.int32, (HEAD, HEAD), 0)
    to = lax.broadcasted_iota(jnp.int32, (HEAD, HEAD), 1)
    origin = (to % SHARE) // GRANULE * (X * GRANULE) + to // SHARE * GRANULE + to % GRANULE
    turn = jnp.where(source == origin, 1.0, 0.0).astype(BF16)
    for h in range(HEADS_HERE):
        for part, ref in enumerate((q_ref, k_ref, v_ref)):
            block = ref[:, h * HEAD : (h + 1) * HEAD]
            if part == 2:
                block = jnp.dot(block, turn, preferred_element_type=F32)
            block = jnp.concatenate([block.astype(F32), jnp.zeros((16, HEAD), F32)], axis=0)
            for r, (start, length) in enumerate(zip(STARTS, LENGTHS)):
                piece = jnp.where(row < length, block[start : start + SLOT], 0.0)
                if part == 0:
                    piece = jnp.where(row == ID_ROW, id_rows[r], piece)
                elif part == 1:
                    piece = jnp.where(row == ID_ROW, every, piece)
                out_ref[PARTS * h + r, part * SLOT : (part + 1) * SLOT, :] = piece.astype(BF16)
    out_ref[PARTS * HEADS_HERE] = jnp.zeros((3 * SLOT, HEAD), BF16)


GROUP = 4


def query_codes(third, q_ref):
    tile = 16
    at = ID_ROW % tile
    ids = jnp.concatenate(
        [
            q_ref[x, z * SLOT + ID_ROW - at : z * SLOT + ID_ROW - at + tile, :].astype(F32)[at : at + 1]
            for x in range(X)
            for z in range(Z)
        ],
        axis=0,
    )
    which = lax.broadcasted_iota(jnp.int32, (X * Z, HEAD), 0)
    home = (X * (which % Z) + which // Z) * TOK + third * STARTS[1]
    first = ids * POSITIONS
    last = first + (home + lax.broadcasted_iota(jnp.int32, (X * Z, HEAD), 1)).astype(F32)
    return jnp.concatenate([first, last], axis=0).T


def columns(table, first):
    return jnp.concatenate([table[:SLOT, first + n : first + n + 1] for n in range(GROUP)], axis=0)


def masked_scores(query, keys, key_code, low_code, high_code):
    score = lax.dot_general(query, keys, (((1,), (1,)), ((), ())), preferred_element_type=F32)
    allowed = (key_code <= high_code) & (key_code >= low_code)
    return jnp.where(allowed, score * (HEAD ** (-0.5) * LOG2E), BLOCKED)


def keys_values(kv_ref):
    rows = Z * SLOT
    values = kv_ref[:, SLOT:, :].reshape(rows, HEAD)
    return kv_ref[:, :SLOT, :].reshape(rows, HEAD), jnp.concatenate([values, jnp.ones((rows, HEAD), BF16)], axis=1)


def attend_first(third_ref, q_ref, kv0_ref, kv1_ref, kcode_ref, sum_ref, stat_ref):
    third = third_ref[0]
    key_codes = [kcode_ref[pl.ds(j, 1), :] for j in (third, lax.rem(third + 2, PARTS))]
    pairs = [keys_values(ref) for ref in (kv0_ref, kv1_ref)]
    codes = query_codes(third, q_ref)
    lane = lax.broadcasted_iota(jnp.int32, (SLOT, HEAD), 1)
    stats = [jnp.zeros((SLOT, HEAD), F32) for _ in range(2)]
    for g in range(Z // GROUP):
        span = slice(g * GROUP * SLOT, (g + 1) * GROUP * SLOT)
        count = -(-(g + 1) * GROUP * SLOT // HEAD) * HEAD
        for x in range(X):
            low_code = columns(codes, x * Z + g * GROUP)
            high_code = columns(codes, (X + x) * Z + g * GROUP)
            scores = [
                masked_scores(q_ref[x, span, :], keys[:count], code[:, :count], low_code, high_code)
                for (keys, _), code in zip(pairs, key_codes)
            ]
            peak = functools.reduce(jnp.maximum, [jnp.max(s, axis=1, keepdims=True) for s in scores])
            output = functools.reduce(
                jnp.add,
                [
                    jnp.dot(jnp.exp2(s - peak).astype(BF16), values[:count], preferred_element_type=F32)
                    for s, (_, values) in zip(scores, pairs)
                ],
            )
            sum_ref[x, span, :] = output[:, :HEAD]
            for n in range(GROUP):
                for at, column in enumerate((peak, output[:, HEAD : HEAD + 1])):
                    stats[at] = jnp.where(
                        lane == x * Z + g * GROUP + n, column[n * SLOT : (n + 1) * SLOT], stats[at]
                    )
    for at in range(2):
        stat_ref[at] = stats[at]


def attend_last(third_ref, q_ref, kv_ref, kcode_ref, sum_ref, stat_ref, out_ref):
    rows = Z * SLOT
    third = third_ref[0]
    key_code = kcode_ref[pl.ds(lax.rem(third + 1, PARTS), 1), :]
    keys, values = keys_values(kv_ref)
    codes = query_codes(third, q_ref)
    peaks, totals = stat_ref[0], stat_ref[1]
    lane = lax.broadcasted_iota(jnp.int32, (SLOT, HEAD), 1)
    stats = [jnp.zeros((SLOT, HEAD), F32) for _ in range(2)]
    share = lax.broadcasted_iota(jnp.int32, (GROUP * SLOT, HEAD), 1) // SHARE
    for g in range(Z // GROUP):
        span = slice(g * GROUP * SLOT, (g + 1) * GROUP * SLOT)
        count = -(-(g + 1) * GROUP * SLOT // HEAD) * HEAD
        slots = [jnp.zeros((GROUP * SLOT, HEAD), F32) for _ in range(X)]
        for x in range(X):
            first = x * Z + g * GROUP
            score = masked_scores(
                q_ref[x, span, :],
                keys[:count],
                key_code[:, :count],
                columns(codes, first),
                columns(codes, X * Z + first),
            )
            before = columns(peaks, first)
            peak = jnp.maximum(before, jnp.max(score, axis=1, keepdims=True))
            kept = jnp.exp2(before - peak)
            output = jnp.dot(
                jnp.exp2(score - peak).astype(BF16), values[:count], preferred_element_type=F32
            )
            total = output[:, HEAD : HEAD + 1] + kept * columns(totals, first)
            normal = (output[:, :HEAD] + kept * sum_ref[x, span, :]) / total
            for to in range(X):
                piece = normal if to == x else pltpu.roll(normal, (SHARE * (x - to)) % HEAD, 1)
                slots[to] = jnp.where(share == x, piece, slots[to])
            logsum = peak + jnp.log2(total)
            high = logsum.astype(BF16).astype(F32)
            rest = logsum - high
            middle = rest.astype(BF16).astype(F32)
            low = rest - middle
            for n in range(GROUP):
                for part, column in enumerate((high, middle, low)):
                    at = part * X * Z + first + n
                    stats[at // HEAD] = jnp.where(
                        lane == at % HEAD, column[n * SLOT : (n + 1) * SLOT], stats[at // HEAD]
                    )
        for x in range(X):
            out_ref[x, span, :] = slots[x].astype(BF16)
    for x in range(X):
        out_ref[x, rows : rows + SLOT, :] = stats[0].astype(BF16)
        out_ref[x, rows + SLOT :, :] = stats[1].astype(BF16)


def join(part_ref, out_ref):
    rows = Z * SLOT
    sums = []
    for x in range(X):
        stat = part_ref[x, rows : rows + SLOT, :].astype(F32)
        rest = part_ref[x, rows + SLOT :, :].astype(F32)
        sums.append(stat + pltpu.roll(stat, HEAD // 2, 1) + rest)
    peak = functools.reduce(jnp.maximum, sums)
    weights = [jnp.exp2(s - peak) for s in sums]
    total = functools.reduce(jnp.add, weights)
    weights = [w / total for w in weights]
    share = lax.broadcasted_iota(jnp.int32, (SLOT, HEAD), 1) // SHARE
    for z in range(Z):
        joined = functools.reduce(
            jnp.add,
            [
                jnp.take_along_axis(weights[x], share * Z + z, axis=1)
                * part_ref[x, z * SLOT : (z + 1) * SLOT, :].astype(F32)
                for x in range(X)
            ],
        )
        out_ref[z] = joined.astype(BF16)


def assemble(part_ref, out_ref):
    share = lax.broadcasted_iota(jnp.int32, (SLOT, HEAD), 1) // SHARE
    for r in range(PARTS):
        came = [part_ref[PARTS * h + r] for h in range(HEADS_HERE)]
        wide = [c.astype(F32) for c in came[:4]]
        for x in range(X):
            block = jnp.zeros((SLOT, HEAD), F32)
            for h in range(4):
                piece = wide[h] if h == x else pltpu.roll(wide[h], (SHARE * (h - x)) % HEAD, 1)
                block = jnp.where(share == h, piece, block)
            first = (x * PARTS + r) * SLOT
            for y in range(Y):
                out_ref[y, first : first + SLOT, :] = block.astype(BF16)
        first = (X * PARTS + r) * SLOT
        for y in range(Y):
            out_ref[y, first : first + SLOT, :] = came[4]


def project(place_ref, mine_ref, other_ref, weight_ref, out_ref):
    core, side = place_ref[0], place_ref[1]
    places = [lax.rem(side + (X + 1) - m, X + 1) * GRANULE for m in range(X + 1)]
    plane_rows = (X + 1) * GRANULE
    pieces = SHARE // GRANULE
    span = PARTS * SLOT
    share = lax.broadcasted_iota(jnp.int32, (span, HEAD), 1) // SHARE
    weights = []
    for y in range(Y):
        for which in (core, 1 - core):
            rows = []
            for n in range(HEADS_HERE * pieces):
                first = (C * y + which) * pieces * plane_rows + n // (X + 1) * plane_rows + places[n % (X + 1)]
                rows.append(weight_ref[pl.ds(pl.multiple_of(first, GRANULE), GRANULE), :])
            weights += rows[: 4 * pieces] + rows[4 * pieces :] * (HEAD // SHARE)
    weights = jnp.concatenate(weights, axis=0)
    for x in range(X):
        inputs = []
        for y in range(Y):
            for ref in (mine_ref, other_ref):
                inputs.append(ref[y, x * span : (x + 1) * span, :])
                fifth = ref[y, X * span :, :].astype(F32)
                inputs.append(jnp.where(share == x, fifth, 0.0).astype(BF16))
        total = jnp.dot(jnp.concatenate(inputs, axis=1), weights, preferred_element_type=F32)
        total = [total[r * SLOT : r * SLOT + length] for r, length in enumerate(LENGTHS)]
        out_ref[x] = jnp.concatenate(total, axis=0).astype(BF16)


def share_rows(granules):
    came = [granules[0]]
    for n in range(1, X):
        came.append(lax.ppermute(granules[n], "x", [(x, (x + n) % X) for x in range(X)]))
    return jnp.concatenate(came + [granules[X]], axis=0)


def local(queries, keys_in, values, cluster_ids, out_weight):
    plane, side, core = lax.axis_index("z"), lax.axis_index("x"), lax.axis_index("c")
    third = lax.rem(plane, PARTS)
    width = out_weight.shape[1]

    send, granules = vmem_call(
        scatter_heads,
        56,
        [(Z, 3 * SLOT, HEAD), (X + 1, GRANULE, width)],
        queries,
        keys_in,
        values,
        cluster_ids.reshape(1, TOK),
        out_weight,
    )
    here = lax.all_to_all(send, "z", 0, 0, tiled=True)
    weight = lax.all_gather(share_rows(granules), "z", axis=0, tiled=True)
    kv = here[:, SLOT:, :]
    turns = [
        [(PARTS * h + r, PARTS * h + (r + k) % PARTS) for h in range(HEADS_HERE) for r in range(PARTS)]
        for k in (1, 2)
    ]
    kv_others = [lax.ppermute(kv, "z", turn) for turn in turns]
    query = jnp.broadcast_to(here[:, :SLOT, :].reshape(1, Z * SLOT, HEAD), (X, Z * SLOT, HEAD))
    query = lax.all_to_all(query, "x", 0, 0, tiled=True)

    home = (X * jnp.arange(Z, dtype=jnp.int32) + side) * TOK
    key_code = kv[:, ID_ROW, :].astype(F32) * POSITIONS + (
        home[:, None] + jnp.arange(HEAD, dtype=jnp.int32)[None, :]
    ).astype(F32)
    key_code = jnp.stack(
        [
            jnp.pad(
                key_code[:, start : start + length], ((0, 0), (0, SLOT - length)), constant_values=NEVER
            ).reshape(Z * SLOT)
            for start, length in zip(STARTS, LENGTHS)
        ]
    )
    third = third.reshape(1)
    sums, stats = vmem_call(
        attend_first,
        18,
        [(X, Z * SLOT, HEAD), (2, SLOT, HEAD)],
        query,
        kv,
        kv_others[0],
        key_code,
        scalars=third,
        kind=F32,
    )
    (part,) = vmem_call(
        attend_last,
        18,
        [(X, (Z + 2) * SLOT, HEAD)],
        query,
        kv_others[1],
        key_code,
        sums,
        stats,
        scalars=third,
    )
    part = lax.all_to_all(part, "x", 0, 0, tiled=True)
    (joined,) = vmem_call(join, 8, [(Z, SLOT, HEAD)], part)
    joined = lax.all_to_all(joined, "z", 0, 0, tiled=True)
    (packed,) = vmem_call(assemble, 8, [(Y, (X + 1) * PARTS * SLOT, HEAD)], joined)
    packed = lax.all_to_all(packed, "y", 0, 0, tiled=True)
    others = lax.ppermute(packed, "c", [(0, 1), (1, 0)])
    (partial,) = vmem_call(
        project, 24, [(X, TOK, width)], packed, others, weight, scalars=jnp.stack([core, side])
    )
    partial = lax.all_to_all(partial, "x", 0, 0, tiled=True)
    return jnp.sum(partial.astype(F32), axis=0).astype(BF16)


def solution(mesh):
    fine = Mesh(mesh.devices.reshape(Z, X, Y, C), ("z", "x", "y", "c"))
    both = P(("z", "x"), ("y", "c"))
    return jax.shard_map(
        local,
        mesh=fine,
        in_specs=(both, both, both, P(("z", "x"), None), both),
        out_specs=both,
        check_vma=False,
    )
```

```python
import functools

import jax
import jax.numpy as jnp
from jax import lax
from jax.experimental import pallas as pl
from jax.experimental.pallas import tpu as pltpu
from jax.sharding import Mesh
from jax.sharding import PartitionSpec as P

HEAD = 128
HEADS_HERE = 5
TOK = 128
Z, X, Y, C = 16, 4, 4, 2
PARTS = 3
STARTS = (0, 44, 88)
LENGTHS = (44, 44, 40)
SLOT = 48
ID_ROW = 46
POSITIONS = 8192
NEVER = 1e9
BLOCKED = -1e30
F32 = jnp.float32
BF16 = jnp.bfloat16
LOG2E = 1.4426950408889634
PAIR = 2
SHARE = 64
GRANULE = 16


def vmem_call(body, mebibytes, shapes, *operands, scalars=None, left=(), scratch=(), kinds=None, cost=None):
    specs = [pl.BlockSpec(memory_space=pltpu.VMEM)] * len(operands)
    specs += [pl.BlockSpec(memory_space=pltpu.HBM)] * len(left)
    operands += tuple(left)
    kinds = kinds or [BF16] * len(shapes)
    if scalars is not None:
        specs = [pl.BlockSpec(memory_space=pltpu.SMEM)] + specs
        operands = (scalars,) + operands
    return pl.pallas_call(
        body,
        out_shape=[jax.ShapeDtypeStruct(shape, kind) for shape, kind in zip(shapes, kinds)],
        in_specs=specs,
        out_specs=[pl.BlockSpec(memory_space=pltpu.VMEM)] * len(shapes),
        scratch_shapes=list(scratch),
        cost_estimate=cost,
        compiler_params=pltpu.CompilerParams(vmem_limit_bytes=mebibytes * 1024 * 1024),
    )(*operands)


def scatter_heads(q_ref, k_ref, v_ref, ids_ref, weight_ref, out_ref, granules_ref):
    for n in range(X + 1):
        granules_ref[n] = weight_ref[n * GRANULE : (n + 1) * GRANULE, :]
    ids = ids_ref[...].astype(F32)
    lane = lax.broadcasted_iota(jnp.int32, (SLOT, HEAD), 1)
    row = lax.broadcasted_iota(jnp.int32, (SLOT, HEAD), 0)
    id_rows = []
    for start, length in zip(STARTS, LENGTHS):
        moved = ids if start == 0 else pltpu.roll(ids, TOK - start, 1)
        id_rows.append(jnp.where(lane < length, jnp.broadcast_to(moved, (SLOT, HEAD)), -1.0))
    every = jnp.broadcast_to(ids, (SLOT, HEAD))
    source = lax.broadcasted_iota(jnp.int32, (HEAD, HEAD), 0)
    to = lax.broadcasted_iota(jnp.int32, (HEAD, HEAD), 1)
    origin = (to % SHARE) // GRANULE * (PAIR * GRANULE) + to // SHARE * GRANULE + to % GRANULE
    turn = jnp.where(source == origin, 1.0, 0.0).astype(BF16)
    for h in range(HEADS_HERE):
        for part, ref in enumerate((q_ref, k_ref, v_ref)):
            block = ref[:, h * HEAD : (h + 1) * HEAD]
            if part == 2:
                block = jnp.dot(block, turn, preferred_element_type=F32)
            block = jnp.concatenate([block.astype(F32), jnp.zeros((16, HEAD), F32)], axis=0)
            for r, (start, length) in enumerate(zip(STARTS, LENGTHS)):
                piece = jnp.where(row < length, block[start : start + SLOT], 0.0)
                if part == 0:
                    piece = jnp.where(row == ID_ROW, id_rows[r], piece)
                elif part == 1:
                    piece = jnp.where(row == ID_ROW, every, piece)
                out_ref[PARTS * h + r, part * SLOT : (part + 1) * SLOT, :] = piece.astype(BF16)
    out_ref[PARTS * HEADS_HERE] = jnp.zeros((3 * SLOT, HEAD), BF16)


def attend(third_ref, q_ref, kv0_ref, kv1_ref, kv2_ref, kcode_ref, out_ref):
    rows = Z * SLOT
    third = third_ref[0]
    order = [third, lax.rem(third + 2, PARTS), lax.rem(third + 1, PARTS)]
    key_codes = [kcode_ref[pl.ds(j, 1), :] for j in order]
    keys = [ref[:, :SLOT, :].reshape(rows, HEAD) for ref in (kv0_ref, kv1_ref, kv2_ref)]
    ones = jnp.ones((rows, HEAD), BF16)
    vals = [
        jnp.concatenate([ref[:, SLOT:, :].reshape(rows, HEAD), ones], axis=1)
        for ref in (kv0_ref, kv1_ref, kv2_ref)
    ]
    tile = 16
    at = ID_ROW % tile
    ids = jnp.concatenate(
        [
            q_ref[x, z * SLOT + ID_ROW - at : z * SLOT + ID_ROW - at + tile, :].astype(F32)[at : at + 1]
            for x in range(X)
            for z in range(Z)
        ],
        axis=0,
    )
    which = lax.broadcasted_iota(jnp.int32, (X * Z, HEAD), 0)
    home = (X * (which % Z) + which // Z) * TOK + third * STARTS[1]
    first = ids * POSITIONS
    last = first + (home + lax.broadcasted_iota(jnp.int32, (X * Z, HEAD), 1)).astype(F32)
    codes = jnp.concatenate([first, last], axis=0).T
    lane = lax.broadcasted_iota(jnp.int32, (SLOT, HEAD), 1)
    group = 4
    halves = lax.broadcasted_iota(jnp.int32, (group * SLOT, HEAD), 1) < SHARE
    stats = [jnp.zeros((SLOT, HEAD), F32) for _ in range(X // PAIR)]
    for g in range(Z // group):
        count = -(-(g + 1) * group * SLOT // HEAD) * HEAD
        zs = range(g * group, (g + 1) * group)
        normals = []
        for x in range(X):
            low_code = jnp.concatenate([codes[:SLOT, x * Z + z : x * Z + z + 1] for z in zs], axis=0)
            high_code = jnp.concatenate(
                [codes[:SLOT, (X + x) * Z + z : (X + x) * Z + z + 1] for z in zs], axis=0
            )
            query = q_ref[x, g * group * SLOT : (g + 1) * group * SLOT, :]
            scores = []
            for j in range(PARTS):
                score = lax.dot_general(
                    query, keys[j][:count], (((1,), (1,)), ((), ())), preferred_element_type=F32
                ) * (HEAD ** (-0.5) * LOG2E)
                key_code = key_codes[j][:, :count]
                allowed = (key_code <= high_code) & (key_code >= low_code)
                scores.append(jnp.where(allowed, score, BLOCKED))
            peak = functools.reduce(jnp.maximum, [jnp.max(s, axis=1, keepdims=True) for s in scores])
            output = jnp.zeros((group * SLOT, 2 * HEAD), F32)
            for j in range(PARTS):
                expo = jnp.exp2(scores[j] - peak)
                output = output + jnp.dot(
                    expo.astype(BF16), vals[j][:count], preferred_element_type=F32
                )
            normals.append(output[:, :HEAD] / output[:, HEAD:])
            logsum = peak + jnp.log2(output[:, HEAD:])
            for n in range(group):
                at = x % PAIR * Z + g * group + n
                stats[x // PAIR] = jnp.where(lane == at, logsum[n * SLOT : (n + 1) * SLOT], stats[x // PAIR])
        for first in range(0, X, PAIR):
            one, two = normals[first : first + PAIR]
            span = slice(g * group * SLOT, (g + 1) * group * SLOT)
            out_ref[first, span, :] = jnp.where(halves, one, pltpu.roll(two, SHARE, 1)).astype(BF16)
            out_ref[first + 1, span, :] = jnp.where(halves, pltpu.roll(one, SHARE, 1), two).astype(BF16)
    for pair, logsum in enumerate(stats):
        high = logsum.astype(BF16).astype(F32)
        rest = logsum - high
        middle = rest.astype(BF16).astype(F32)
        low = rest - middle
        table = high + pltpu.roll(middle, PAIR * Z, 1) + pltpu.roll(low, 2 * PAIR * Z, 1)
        for x in range(PAIR):
            out_ref[PAIR * pair + x, rows:, :] = table.astype(BF16)


def join(part_ref, out_ref):
    rows = Z * SLOT
    sums = []
    for x in range(X):
        stat = part_ref[x, rows:, :].astype(F32)
        sums.append(stat + pltpu.roll(stat, HEAD - PAIR * Z, 1) + pltpu.roll(stat, HEAD - 2 * PAIR * Z, 1))
    peak = functools.reduce(jnp.maximum, sums)
    weights = [jnp.exp2(s - peak) for s in sums]
    total = functools.reduce(jnp.add, weights)
    weights = [w / total for w in weights]
    half = lax.broadcasted_iota(jnp.int32, (SLOT, HEAD), 1) // SHARE
    for z in range(Z):
        joined = functools.reduce(
            jnp.add,
            [
                jnp.take_along_axis(weights[x], half * Z + z, axis=1)
                * part_ref[x, z * SLOT : (z + 1) * SLOT, :].astype(F32)
                for x in range(X)
            ],
        )
        out_ref[z] = joined.astype(BF16)


def assemble(part_ref, out_ref):
    halves = lax.broadcasted_iota(jnp.int32, (SLOT, HEAD), 1) < SHARE
    for r in range(PARTS):
        for two in range(2):
            one, other = [part_ref[PARTS * (2 * two + n) + r].astype(F32) for n in range(2)]
            blocks = (
                jnp.where(halves, one, pltpu.roll(other, SHARE, 1)),
                jnp.where(halves, pltpu.roll(one, SHARE, 1), other),
            )
            for x, block in enumerate(blocks):
                first = ((2 * x + two) * PARTS + r) * SLOT
                for y in range(Y):
                    out_ref[y, first : first + SLOT, :] = block.astype(BF16)
        first = (2 * PAIR * PARTS + r) * SLOT
        for y in range(Y):
            out_ref[y, first : first + SLOT, :] = part_ref[PARTS * (HEADS_HERE - 1) + r]


def project(place_ref, mine_ref, other_ref, hbm_ref, own_ref, send_ref, weight_ref, sems):
    core, side = place_ref[0], place_ref[1]
    depth = weight_ref.shape[0] // Z
    copies = [
        pltpu.make_async_copy(
            hbm_ref.at[pl.ds(z * depth, depth), :], weight_ref.at[pl.ds(z * depth, depth), :], sems.at[z]
        )
        for z in range(Z)
    ]
    for copy in copies:
        copy.start()
    member = lax.rem(side, PAIR)
    places = []
    for m in range(depth // GRANULE):
        number = 2 * m + member
        holder, n = lax.div(number, X + 1), lax.rem(number, X + 1)
        away = lax.rem(holder + X - side, X)
        base = jnp.where(away == 0, 0, jnp.where(away == 1, 8, jnp.where(away == 2, 3, 6)))
        places.append((base + lax.div(n, 2)) * GRANULE)
    span = PARTS * SLOT
    halves = lax.broadcasted_iota(jnp.int32, (span, HEAD), 1) < SHARE
    per_head = SHARE // GRANULE
    inputs = [[] for _ in range(PAIR)]
    for y in range(Y):
        for ref in (mine_ref, other_ref):
            fifth = ref[y, 2 * PAIR * span :, :].astype(F32)
            for x in range(PAIR):
                inputs[x] += [ref[y, (2 * x + two) * span : (2 * x + two + 1) * span, :] for two in range(2)]
                inputs[x].append(jnp.where(halves == (x == 0), fifth, 0.0).astype(BF16))
    inputs = [jnp.concatenate(blocks, axis=1) for blocks in inputs]
    for copy in copies:
        copy.wait()
    weights = []
    for y in range(Y):
        for which in (core, 1 - core):
            rows = []
            for n in range(HEADS_HERE * per_head):
                first = ((C * y + which) * 2 + n // len(places)) * depth + places[n % len(places)]
                rows.append(weight_ref[pl.ds(pl.multiple_of(first, GRANULE), GRANULE), :])
            weights += rows + rows[4 * per_head :]
    weights = jnp.concatenate(weights, axis=0)
    totals = []
    for x in range(PAIR):
        total = jnp.dot(inputs[x], weights, preferred_element_type=F32)
        total = [total[r * SLOT : r * SLOT + length] for r, length in enumerate(LENGTHS)]
        totals.append(jnp.concatenate(total, axis=0))
    own_ref[...] = jnp.where(member == 0, totals[0], totals[1])
    send_ref[...] = jnp.where(member == 0, totals[1], totals[0]).astype(BF16)


def share_rows(granules):
    even = jnp.concatenate([granules[n] for n in range(0, X + 1, 2)], axis=0)
    odd = jnp.concatenate([granules[n] for n in range(1, X + 1, 2)], axis=0)
    blocks = [even]
    for block, away in ((even, 2), (odd, 1), (odd, X - 1)):
        blocks.append(lax.ppermute(block, "x", [(x, (x + away) % X) for x in range(X)]))
    return jnp.concatenate(blocks, axis=0)


def local(queries, keys_in, values, cluster_ids, out_weight):
    plane, side, core = lax.axis_index("z"), lax.axis_index("x"), lax.axis_index("c")
    third = lax.rem(plane, PARTS)
    width = out_weight.shape[1]

    send, granules = vmem_call(
        scatter_heads,
        56,
        [(Z, 3 * SLOT, HEAD), (X + 1, GRANULE, width)],
        queries,
        keys_in,
        values,
        cluster_ids.reshape(1, TOK),
        out_weight,
    )
    here = lax.all_to_all(send, "z", 0, 0, tiled=True)
    weight = lax.all_gather(share_rows(granules), "z", axis=0, tiled=True)
    kv = here[:, SLOT:, :]
    turns = [
        [(PARTS * h + r, PARTS * h + (r + k) % PARTS) for h in range(HEADS_HERE) for r in range(PARTS)]
        for k in (1, 2)
    ]
    kv_others = [lax.ppermute(kv, "z", turn) for turn in turns]
    query = jnp.broadcast_to(here[:, :SLOT, :].reshape(1, Z * SLOT, HEAD), (X, Z * SLOT, HEAD))
    query = lax.all_to_all(query, "x", 0, 0, tiled=True)

    home = (X * jnp.arange(Z, dtype=jnp.int32) + side) * TOK
    key_code = kv[:, ID_ROW, :].astype(F32) * POSITIONS + (
        home[:, None] + jnp.arange(HEAD, dtype=jnp.int32)[None, :]
    ).astype(F32)
    key_code = jnp.stack(
        [
            jnp.pad(
                key_code[:, start : start + length], ((0, 0), (0, SLOT - length)), constant_values=NEVER
            ).reshape(Z * SLOT)
            for start, length in zip(STARTS, LENGTHS)
        ]
    )
    (part,) = vmem_call(
        attend,
        20,
        [(X, (Z + 1) * SLOT, HEAD)],
        query,
        kv,
        kv_others[0],
        kv_others[1],
        key_code,
        scalars=third.reshape(1),
        cost=pl.CostEstimate(flops=1 << 36, bytes_accessed=1 << 22, transcendentals=1 << 22),
    )
    part = lax.all_to_all(part, "x", 0, 0, tiled=True)
    (joined,) = vmem_call(join, 8, [(Z, SLOT, HEAD)], part)
    joined = lax.all_to_all(joined, "z", 0, 0, tiled=True)
    (packed,) = vmem_call(assemble, 8, [(Y, (2 * PAIR + 1) * PARTS * SLOT, HEAD)], joined)
    packed = lax.all_to_all(packed, "y", 0, 0, tiled=True)
    others = lax.ppermute(packed, "c", [(0, 1), (1, 0)])
    own, send = vmem_call(
        project,
        24,
        [(TOK, width), (TOK, width)],
        packed,
        others,
        scalars=jnp.stack([core, side]),
        left=[weight],
        scratch=[pltpu.VMEM(weight.shape, BF16), pltpu.SemaphoreType.DMA((Z,))],
        kinds=[F32, BF16],
    )
    came = lax.ppermute(send, "x", [(x, x + 1 - 2 * (x % PAIR)) for x in range(X)])
    return (own + came.astype(F32)).astype(BF16)


def solution(mesh):
    fine = Mesh(mesh.devices.reshape(Z, X, Y, C), ("z", "x", "y", "c"))
    both = P(("z", "x"), ("y", "c"))
    return jax.shard_map(
        local,
        mesh=fine,
        in_specs=(both, both, both, P(("z", "x"), None), both),
        out_specs=both,
        check_vma=False,
    )
```

```python
import functools

import jax
import jax.numpy as jnp
from jax import lax
from jax.experimental import pallas as pl
from jax.experimental.pallas import tpu as pltpu
from jax.sharding import Mesh
from jax.sharding import PartitionSpec as P

HEAD = 128
HEADS_HERE = 5
TOK = 128
Z, X, Y, C = 16, 4, 4, 2
PARTS = 3
STARTS = (0, 44, 88)
LENGTHS = (44, 44, 40)
SLOT = 48
ID_ROW = 46
POSITIONS = 8192
NEVER = 1e9
BLOCKED = -1e30
F32 = jnp.float32
BF16 = jnp.bfloat16
LOG2E = 1.4426950408889634
PAIR = 2
SHARE = 64
GRANULE = 16


def vmem_call(body, mebibytes, shapes, *operands, scalars=None, kinds=None, cost=None):
    specs = [pl.BlockSpec(memory_space=pltpu.VMEM)] * len(operands)
    if scalars is not None:
        specs = [pl.BlockSpec(memory_space=pltpu.SMEM)] + specs
        operands = (scalars,) + operands
    kinds = kinds or [BF16] * len(shapes)
    return pl.pallas_call(
        body,
        out_shape=[jax.ShapeDtypeStruct(shape, kind) for shape, kind in zip(shapes, kinds)],
        in_specs=specs,
        out_specs=[pl.BlockSpec(memory_space=pltpu.VMEM)] * len(shapes),
        cost_estimate=cost,
        compiler_params=pltpu.CompilerParams(vmem_limit_bytes=mebibytes * 1024 * 1024),
    )(*operands)


def scatter_heads(q_ref, k_ref, v_ref, ids_ref, weight_ref, out_ref, granules_ref):
    for n in range(X + 1):
        granules_ref[n] = weight_ref[n * GRANULE : (n + 1) * GRANULE, :]
    ids = ids_ref[...].astype(F32)
    lane = lax.broadcasted_iota(jnp.int32, (SLOT, HEAD), 1)
    row = lax.broadcasted_iota(jnp.int32, (SLOT, HEAD), 0)
    id_rows = []
    for start, length in zip(STARTS, LENGTHS):
        moved = ids if start == 0 else pltpu.roll(ids, TOK - start, 1)
        id_rows.append(jnp.where(lane < length, jnp.broadcast_to(moved, (SLOT, HEAD)), -1.0))
    every = jnp.broadcast_to(ids, (SLOT, HEAD))
    source = lax.broadcasted_iota(jnp.int32, (HEAD, HEAD), 0)
    to = lax.broadcasted_iota(jnp.int32, (HEAD, HEAD), 1)
    origin = (to % SHARE) // GRANULE * (PAIR * GRANULE) + to // SHARE * GRANULE + to % GRANULE
    turn = jnp.where(source == origin, 1.0, 0.0).astype(BF16)
    for h in range(HEADS_HERE):
        for part, ref in enumerate((q_ref, k_ref, v_ref)):
            block = ref[:, h * HEAD : (h + 1) * HEAD]
            if part == 2:
                block = jnp.dot(block, turn, preferred_element_type=F32)
            block = jnp.concatenate([block.astype(F32), jnp.zeros((16, HEAD), F32)], axis=0)
            for r, (start, length) in enumerate(zip(STARTS, LENGTHS)):
                piece = jnp.where(row < length, block[start : start + SLOT], 0.0)
                if part == 0:
                    piece = jnp.where(row == ID_ROW, id_rows[r], piece)
                elif part == 1:
                    piece = jnp.where(row == ID_ROW, every, piece)
                out_ref[PARTS * h + r, part * SLOT : (part + 1) * SLOT, :] = piece.astype(BF16)
    out_ref[PARTS * HEADS_HERE] = jnp.zeros((3 * SLOT, HEAD), BF16)


def attend(third_ref, q_ref, kv0_ref, kv1_ref, kv2_ref, kcode_ref, out_ref):
    rows = Z * SLOT
    third = third_ref[0]
    order = [third, lax.rem(third + 2, PARTS), lax.rem(third + 1, PARTS)]
    key_codes = [kcode_ref[pl.ds(j, 1), :] for j in order]
    keys = [ref[:, :SLOT, :].reshape(rows, HEAD) for ref in (kv0_ref, kv1_ref, kv2_ref)]
    ones = jnp.ones((rows, HEAD), BF16)
    vals = [
        jnp.concatenate([ref[:, SLOT:, :].reshape(rows, HEAD), ones], axis=1)
        for ref in (kv0_ref, kv1_ref, kv2_ref)
    ]
    tile = 16
    at = ID_ROW % tile
    ids = jnp.concatenate(
        [
            q_ref[x, z * SLOT + ID_ROW - at : z * SLOT + ID_ROW - at + tile, :].astype(F32)[at : at + 1]
            for x in range(X)
            for z in range(Z)
        ],
        axis=0,
    )
    which = lax.broadcasted_iota(jnp.int32, (X * Z, HEAD), 0)
    home = (X * (which % Z) + which // Z) * TOK + third * STARTS[1]
    first = ids * POSITIONS
    last = first + (home + lax.broadcasted_iota(jnp.int32, (X * Z, HEAD), 1)).astype(F32)
    codes = jnp.concatenate([first, last], axis=0).T
    lane = lax.broadcasted_iota(jnp.int32, (SLOT, HEAD), 1)
    group = 4
    halves = lax.broadcasted_iota(jnp.int32, (group * SLOT, HEAD), 1) < SHARE
    stats = [jnp.zeros((SLOT, HEAD), F32) for _ in range(X // PAIR)]
    for g in range(Z // group):
        count = -(-(g + 1) * group * SLOT // HEAD) * HEAD
        zs = range(g * group, (g + 1) * group)
        normals = []
        for x in range(X):
            low_code = jnp.concatenate([codes[:SLOT, x * Z + z : x * Z + z + 1] for z in zs], axis=0)
            high_code = jnp.concatenate(
                [codes[:SLOT, (X + x) * Z + z : (X + x) * Z + z + 1] for z in zs], axis=0
            )
            query = q_ref[x, g * group * SLOT : (g + 1) * group * SLOT, :]
            scores = []
            for j in range(PARTS):
                score = lax.dot_general(
                    query, keys[j][:count], (((1,), (1,)), ((), ())), preferred_element_type=F32
                ) * (HEAD ** (-0.5) * LOG2E)
                key_code = key_codes[j][:, :count]
                allowed = (key_code <= high_code) & (key_code >= low_code)
                scores.append(jnp.where(allowed, score, BLOCKED))
            peak = functools.reduce(jnp.maximum, [jnp.max(s, axis=1, keepdims=True) for s in scores])
            output = jnp.zeros((group * SLOT, 2 * HEAD), F32)
            for j in range(PARTS):
                expo = jnp.exp2(scores[j] - peak)
                output = output + jnp.dot(
                    expo.astype(BF16), vals[j][:count], preferred_element_type=F32
                )
            normals.append(output[:, :HEAD] / output[:, HEAD:])
            logsum = peak + jnp.log2(output[:, HEAD:])
            for n in range(group):
                at = x % PAIR * Z + g * group + n
                stats[x // PAIR] = jnp.where(lane == at, logsum[n * SLOT : (n + 1) * SLOT], stats[x // PAIR])
        for first in range(0, X, PAIR):
            one, two = normals[first : first + PAIR]
            span = slice(g * group * SLOT, (g + 1) * group * SLOT)
            out_ref[first, span, :] = jnp.where(halves, one, pltpu.roll(two, SHARE, 1)).astype(BF16)
            out_ref[first + 1, span, :] = jnp.where(halves, pltpu.roll(one, SHARE, 1), two).astype(BF16)
    for pair, logsum in enumerate(stats):
        high = logsum.astype(BF16).astype(F32)
        rest = logsum - high
        middle = rest.astype(BF16).astype(F32)
        low = rest - middle
        table = high + pltpu.roll(middle, PAIR * Z, 1) + pltpu.roll(low, 2 * PAIR * Z, 1)
        for x in range(PAIR):
            out_ref[PAIR * pair + x, rows:, :] = table.astype(BF16)


def join(part_ref, out_ref):
    rows = Z * SLOT
    sums = []
    for x in range(X):
        stat = part_ref[x, rows:, :].astype(F32)
        sums.append(stat + pltpu.roll(stat, HEAD - PAIR * Z, 1) + pltpu.roll(stat, HEAD - 2 * PAIR * Z, 1))
    peak = functools.reduce(jnp.maximum, sums)
    weights = [jnp.exp2(s - peak) for s in sums]
    total = functools.reduce(jnp.add, weights)
    weights = [w / total for w in weights]
    half = lax.broadcasted_iota(jnp.int32, (SLOT, HEAD), 1) // SHARE
    for z in range(Z):
        joined = functools.reduce(
            jnp.add,
            [
                jnp.take_along_axis(weights[x], half * Z + z, axis=1)
                * part_ref[x, z * SLOT : (z + 1) * SLOT, :].astype(F32)
                for x in range(X)
            ],
        )
        out_ref[z] = joined.astype(BF16)


def assemble(part_ref, out_ref):
    halves = lax.broadcasted_iota(jnp.int32, (SLOT, HEAD), 1) < SHARE
    for r in range(PARTS):
        for two in range(2):
            one, other = [part_ref[PARTS * (2 * two + n) + r].astype(F32) for n in range(2)]
            blocks = (
                jnp.where(halves, one, pltpu.roll(other, SHARE, 1)),
                jnp.where(halves, pltpu.roll(one, SHARE, 1), other),
            )
            for x, block in enumerate(blocks):
                first = ((2 * x + two) * PARTS + r) * SLOT
                for y in range(Y):
                    out_ref[y, first : first + SLOT, :] = block.astype(BF16)
        first = (2 * PAIR * PARTS + r) * SLOT
        for y in range(Y):
            out_ref[y, first : first + SLOT, :] = part_ref[PARTS * (HEADS_HERE - 1) + r]


def multiply(core, side, packed_ref, weight_ref):
    depth = weight_ref.shape[0] // Z
    member = lax.rem(side, PAIR)
    places = []
    for m in range(depth // GRANULE):
        number = 2 * m + member
        holder, n = lax.div(number, X + 1), lax.rem(number, X + 1)
        away = lax.rem(holder + X - side, X)
        base = jnp.where(away == 0, 0, jnp.where(away == 1, 8, jnp.where(away == 2, 3, 6)))
        places.append((base + lax.div(n, 2)) * GRANULE)
    span = PARTS * SLOT
    halves = lax.broadcasted_iota(jnp.int32, (span, HEAD), 1) < SHARE
    per_head = SHARE // GRANULE
    inputs = [[] for _ in range(PAIR)]
    weights = []
    for y in range(Y):
        fifth = packed_ref[y, 2 * PAIR * span :, :].astype(F32)
        for x in range(PAIR):
            inputs[x] += [packed_ref[y, (2 * x + two) * span : (2 * x + two + 1) * span, :] for two in range(2)]
            inputs[x].append(jnp.where(halves == (x == 0), fifth, 0.0).astype(BF16))
        rows = []
        for n in range(HEADS_HERE * per_head):
            first = ((C * y + core) * 2 + n // len(places)) * depth + places[n % len(places)]
            rows.append(weight_ref[pl.ds(pl.multiple_of(first, GRANULE), GRANULE), :])
        weights += rows + rows[4 * per_head :]
    weights = jnp.concatenate(weights, axis=0)
    return [
        jnp.dot(jnp.concatenate(blocks, axis=1), weights, preferred_element_type=F32) for blocks in inputs
    ]


def project_mine(place_ref, packed_ref, weight_ref, sum_ref):
    for x, total in enumerate(multiply(place_ref[0], place_ref[1], packed_ref, weight_ref)):
        sum_ref[x] = total


def project_other(place_ref, packed_ref, weight_ref, sum_ref, own_ref, send_ref):
    side = place_ref[1]
    totals = []
    for x, total in enumerate(multiply(1 - place_ref[0], side, packed_ref, weight_ref)):
        total = total + sum_ref[x]
        total = [total[r * SLOT : r * SLOT + length] for r, length in enumerate(LENGTHS)]
        totals.append(jnp.concatenate(total, axis=0))
    first = lax.rem(side, PAIR) == 0
    own_ref[...] = jnp.where(first, totals[0], totals[1])
    send_ref[...] = jnp.where(first, totals[1], totals[0]).astype(BF16)


def share_rows(granules):
    even = jnp.concatenate([granules[n] for n in range(0, X + 1, 2)], axis=0)
    odd = jnp.concatenate([granules[n] for n in range(1, X + 1, 2)], axis=0)
    blocks = [even]
    for block, away in ((even, 2), (odd, 1), (odd, X - 1)):
        blocks.append(lax.ppermute(block, "x", [(x, (x + away) % X) for x in range(X)]))
    return jnp.concatenate(blocks, axis=0)


def local(queries, keys_in, values, cluster_ids, out_weight):
    plane, side, core = lax.axis_index("z"), lax.axis_index("x"), lax.axis_index("c")
    third = lax.rem(plane, PARTS)
    width = out_weight.shape[1]

    send, granules = vmem_call(
        scatter_heads,
        56,
        [(Z, 3 * SLOT, HEAD), (X + 1, GRANULE, width)],
        queries,
        keys_in,
        values,
        cluster_ids.reshape(1, TOK),
        out_weight,
    )
    here = lax.all_to_all(send, "z", 0, 0, tiled=True)
    weight = lax.all_gather(share_rows(granules), "z", axis=0, tiled=True)
    kv = here[:, SLOT:, :]
    turns = [
        [(PARTS * h + r, PARTS * h + (r + k) % PARTS) for h in range(HEADS_HERE) for r in range(PARTS)]
        for k in (1, 2)
    ]
    kv_others = [lax.ppermute(kv, "z", turn) for turn in turns]
    query = jnp.broadcast_to(here[:, :SLOT, :].reshape(1, Z * SLOT, HEAD), (X, Z * SLOT, HEAD))
    query = lax.all_to_all(query, "x", 0, 0, tiled=True)

    home = (X * jnp.arange(Z, dtype=jnp.int32) + side) * TOK
    key_code = kv[:, ID_ROW, :].astype(F32) * POSITIONS + (
        home[:, None] + jnp.arange(HEAD, dtype=jnp.int32)[None, :]
    ).astype(F32)
    key_code = jnp.stack(
        [
            jnp.pad(
                key_code[:, start : start + length], ((0, 0), (0, SLOT - length)), constant_values=NEVER
            ).reshape(Z * SLOT)
            for start, length in zip(STARTS, LENGTHS)
        ]
    )
    (part,) = vmem_call(
        attend,
        20,
        [(X, (Z + 1) * SLOT, HEAD)],
        query,
        kv,
        kv_others[0],
        kv_others[1],
        key_code,
        scalars=third.reshape(1),
        cost=pl.CostEstimate(flops=1 << 36, bytes_accessed=1 << 22, transcendentals=1 << 22),
    )
    part = lax.all_to_all(part, "x", 0, 0, tiled=True)
    (joined,) = vmem_call(join, 8, [(Z, SLOT, HEAD)], part)
    joined = lax.all_to_all(joined, "z", 0, 0, tiled=True)
    (packed,) = vmem_call(assemble, 8, [(Y, (2 * PAIR + 1) * PARTS * SLOT, HEAD)], joined)
    packed = lax.all_to_all(packed, "y", 0, 0, tiled=True)
    others = lax.ppermute(packed, "c", [(0, 1), (1, 0)])
    place = jnp.stack([core, side])
    (sums,) = vmem_call(
        project_mine,
        16,
        [(PAIR, PARTS * SLOT, width)],
        packed,
        weight,
        scalars=place,
        kinds=[F32],
        cost=pl.CostEstimate(flops=1 << 31, bytes_accessed=1 << 23, transcendentals=0),
    )
    own, send = vmem_call(
        project_other,
        16,
        [(TOK, width), (TOK, width)],
        others,
        weight,
        sums,
        scalars=place,
        kinds=[F32, BF16],
    )
    came = lax.ppermute(send, "x", [(x, x + 1 - 2 * (x % PAIR)) for x in range(X)])
    return (own + came.astype(F32)).astype(BF16)


def solution(mesh):
    fine = Mesh(mesh.devices.reshape(Z, X, Y, C), ("z", "x", "y", "c"))
    both = P(("z", "x"), ("y", "c"))
    return jax.shard_map(
        local,
        mesh=fine,
        in_specs=(both, both, both, P(("z", "x"), None), both),
        out_specs=both,
        check_vma=False,
    )
```

```python
import functools

import jax
import jax.numpy as jnp
from jax import lax
from jax.experimental import pallas as pl
from jax.experimental.pallas import tpu as pltpu
from jax.sharding import Mesh
from jax.sharding import PartitionSpec as P

HEAD = 128
HEADS_HERE = 5
TOK = 128
Z, X, Y, C = 16, 4, 4, 2
PARTS = 3
STARTS = (0, 44, 88)
LENGTHS = (44, 44, 40)
SLOT = 48
ROWS = 44
ID_ROW = 46
POSITIONS = 8192
NEVER = 1e9
BLOCKED = -1e30
F32 = jnp.float32
BF16 = jnp.bfloat16
LOG2E = 1.4426950408889634
PAIR = 2
SHARE = 64
GRANULE = 16


def vmem_call(body, mebibytes, shapes, *operands, scalars=None, kinds=None, cost=None):
    specs = [pl.BlockSpec(memory_space=pltpu.VMEM)] * len(operands)
    if scalars is not None:
        specs = [pl.BlockSpec(memory_space=pltpu.SMEM)] + specs
        operands = (scalars,) + operands
    kinds = kinds or [BF16] * len(shapes)
    return pl.pallas_call(
        body,
        out_shape=[jax.ShapeDtypeStruct(shape, kind) for shape, kind in zip(shapes, kinds)],
        in_specs=specs,
        out_specs=[pl.BlockSpec(memory_space=pltpu.VMEM)] * len(shapes),
        cost_estimate=cost,
        compiler_params=pltpu.CompilerParams(vmem_limit_bytes=mebibytes * 1024 * 1024),
    )(*operands)


def scatter_heads(q_ref, k_ref, v_ref, ids_ref, weight_ref, out_ref, granules_ref):
    for n in range(X + 1):
        granules_ref[n] = weight_ref[n * GRANULE : (n + 1) * GRANULE, :]
    ids = ids_ref[...].astype(F32)
    lane = lax.broadcasted_iota(jnp.int32, (SLOT, HEAD), 1)
    row = lax.broadcasted_iota(jnp.int32, (SLOT, HEAD), 0)
    id_rows = []
    for start, length in zip(STARTS, LENGTHS):
        moved = ids if start == 0 else pltpu.roll(ids, TOK - start, 1)
        id_rows.append(jnp.where(lane < length, jnp.broadcast_to(moved, (SLOT, HEAD)), -1.0))
    every = jnp.broadcast_to(ids, (SLOT, HEAD))
    source = lax.broadcasted_iota(jnp.int32, (HEAD, HEAD), 0)
    to = lax.broadcasted_iota(jnp.int32, (HEAD, HEAD), 1)
    origin = (to % SHARE) // GRANULE * (PAIR * GRANULE) + to // SHARE * GRANULE + to % GRANULE
    turn = jnp.where(source == origin, 1.0, 0.0).astype(BF16)
    for h in range(HEADS_HERE):
        blocks = []
        for part, ref in enumerate((q_ref, k_ref, v_ref)):
            block = ref[:, h * HEAD : (h + 1) * HEAD]
            if part == 2:
                block = jnp.dot(block, turn, preferred_element_type=F32)
            blocks.append(jnp.concatenate([block.astype(F32), jnp.zeros((16, HEAD), F32)], axis=0))
        for r, (start, length) in enumerate(zip(STARTS, LENGTHS)):
            query, key, value = [
                jnp.where(row < length, block[start : start + SLOT], 0.0) for block in blocks
            ]
            query = jnp.where(row == ID_ROW, id_rows[r], query)
            query = jnp.where(row == ID_ROW + 1, every, query)
            slot = jnp.concatenate([query, key[:ROWS], value[:ROWS]], axis=0)
            out_ref[PARTS * h + r] = slot.astype(BF16)
    out_ref[PARTS * HEADS_HERE] = jnp.zeros((SLOT + 2 * ROWS, HEAD), BF16)


def attend(third_ref, q_ref, kv0_ref, kv1_ref, kv2_ref, kcode_ref, out_ref):
    rows = Z * SLOT
    third = third_ref[0]
    order = [third, lax.rem(third + 2, PARTS), lax.rem(third + 1, PARTS)]
    key_codes = [kcode_ref[pl.ds(j, 1), :] for j in order]
    parts = [ref[...].astype(F32) for ref in (kv0_ref, kv1_ref, kv2_ref)]
    keys = [part[:, :SLOT].astype(BF16).reshape(rows, HEAD) for part in parts]
    ones = jnp.ones((rows, HEAD), BF16)
    vals = []
    for part in parts:
        turned = [pltpu.roll(part[z, 2 * ROWS - SLOT :], ROWS, 0) for z in range(Z)]
        vals.append(jnp.concatenate([jnp.concatenate(turned, axis=0).astype(BF16), ones], axis=1))
    tile = 16
    at = ID_ROW % tile
    ids = jnp.concatenate(
        [
            q_ref[x, z * SLOT + ID_ROW - at : z * SLOT + ID_ROW - at + tile, :].astype(F32)[at : at + 1]
            for x in range(X)
            for z in range(Z)
        ],
        axis=0,
    )
    which = lax.broadcasted_iota(jnp.int32, (X * Z, HEAD), 0)
    home = (X * (which % Z) + which // Z) * TOK + third * STARTS[1]
    first = ids * POSITIONS
    last = first + (home + lax.broadcasted_iota(jnp.int32, (X * Z, HEAD), 1)).astype(F32)
    codes = jnp.concatenate([first, last], axis=0).T
    lane = lax.broadcasted_iota(jnp.int32, (SLOT, HEAD), 1)
    group = 4
    halves = lax.broadcasted_iota(jnp.int32, (group * SLOT, HEAD), 1) < SHARE
    stats = [jnp.zeros((SLOT, HEAD), F32) for _ in range(X // PAIR)]
    for g in range(Z // group):
        count = -(-(g + 1) * group * SLOT // HEAD) * HEAD
        zs = range(g * group, (g + 1) * group)
        normals = []
        for x in range(X):
            low_code = jnp.concatenate([codes[:SLOT, x * Z + z : x * Z + z + 1] for z in zs], axis=0)
            high_code = jnp.concatenate(
                [codes[:SLOT, (X + x) * Z + z : (X + x) * Z + z + 1] for z in zs], axis=0
            )
            query = q_ref[x, g * group * SLOT : (g + 1) * group * SLOT, :]
            scores = []
            for j in range(PARTS):
                score = lax.dot_general(
                    query, keys[j][:count], (((1,), (1,)), ((), ())), preferred_element_type=F32
                ) * (HEAD ** (-0.5) * LOG2E)
                key_code = key_codes[j][:, :count]
                allowed = (key_code <= high_code) & (key_code >= low_code)
                scores.append(jnp.where(allowed, score, BLOCKED))
            peak = functools.reduce(jnp.maximum, [jnp.max(s, axis=1, keepdims=True) for s in scores])
            output = jnp.zeros((group * SLOT, 2 * HEAD), F32)
            for j in range(PARTS):
                expo = jnp.exp2(scores[j] - peak)
                output = output + jnp.dot(
                    expo.astype(BF16), vals[j][:count], preferred_element_type=F32
                )
            normals.append(output[:, :HEAD] / output[:, HEAD:])
            logsum = peak + jnp.log2(output[:, HEAD:])
            for n in range(group):
                at = x % PAIR * Z + g * group + n
                stats[x // PAIR] = jnp.where(lane == at, logsum[n * SLOT : (n + 1) * SLOT], stats[x // PAIR])
        for first in range(0, X, PAIR):
            one, two = normals[first : first + PAIR]
            span = slice(g * group * SLOT, (g + 1) * group * SLOT)
            out_ref[first, span, :] = jnp.where(halves, one, pltpu.roll(two, SHARE, 1)).astype(BF16)
            out_ref[first + 1, span, :] = jnp.where(halves, pltpu.roll(one, SHARE, 1), two).astype(BF16)
    for pair, logsum in enumerate(stats):
        high = logsum.astype(BF16).astype(F32)
        rest = logsum - high
        middle = rest.astype(BF16).astype(F32)
        low = rest - middle
        table = high + pltpu.roll(middle, PAIR * Z, 1) + pltpu.roll(low, 2 * PAIR * Z, 1)
        for x in range(PAIR):
            out_ref[PAIR * pair + x, rows:, :] = table.astype(BF16)


def join(part_ref, out_ref):
    rows = Z * SLOT
    sums = []
    for x in range(X):
        stat = part_ref[x, rows:, :].astype(F32)
        sums.append(stat + pltpu.roll(stat, HEAD - PAIR * Z, 1) + pltpu.roll(stat, HEAD - 2 * PAIR * Z, 1))
    peak = functools.reduce(jnp.maximum, sums)
    weights = [jnp.exp2(s - peak) for s in sums]
    total = functools.reduce(jnp.add, weights)
    weights = [w / total for w in weights]
    half = lax.broadcasted_iota(jnp.int32, (SLOT, HEAD), 1) // SHARE
    for z in range(Z):
        joined = functools.reduce(
            jnp.add,
            [
                jnp.take_along_axis(weights[x], half * Z + z, axis=1)
                * part_ref[x, z * SLOT : (z + 1) * SLOT, :].astype(F32)
                for x in range(X)
            ],
        )
        out_ref[z] = joined.astype(BF16)


def assemble(part_ref, out_ref):
    halves = lax.broadcasted_iota(jnp.int32, (SLOT, HEAD), 1) < SHARE
    for r in range(PARTS):
        for two in range(2):
            one, other = [part_ref[PARTS * (2 * two + n) + r].astype(F32) for n in range(2)]
            blocks = (
                jnp.where(halves, one, pltpu.roll(other, SHARE, 1)),
                jnp.where(halves, pltpu.roll(one, SHARE, 1), other),
            )
            for x, block in enumerate(blocks):
                first = ((2 * x + two) * PARTS + r) * SLOT
                for y in range(Y):
                    out_ref[y, first : first + SLOT, :] = block.astype(BF16)
        first = (2 * PAIR * PARTS + r) * SLOT
        for y in range(Y):
            out_ref[y, first : first + SLOT, :] = part_ref[PARTS * (HEADS_HERE - 1) + r]


def multiply(core, side, packed_ref, weight_ref):
    depth = weight_ref.shape[0] // Z
    member = lax.rem(side, PAIR)
    places = []
    for m in range(depth // GRANULE):
        number = 2 * m + member
        holder, n = lax.div(number, X + 1), lax.rem(number, X + 1)
        away = lax.rem(holder + X - side, X)
        base = jnp.where(away == 0, 0, jnp.where(away == 1, 8, jnp.where(away == 2, 3, 6)))
        places.append((base + lax.div(n, 2)) * GRANULE)
    span = PARTS * SLOT
    halves = lax.broadcasted_iota(jnp.int32, (span, HEAD), 1) < SHARE
    per_head = SHARE // GRANULE
    inputs = [[] for _ in range(PAIR)]
    weights = []
    for y in range(Y):
        fifth = packed_ref[y, 2 * PAIR * span :, :].astype(F32)
        for x in range(PAIR):
            inputs[x] += [packed_ref[y, (2 * x + two) * span : (2 * x + two + 1) * span, :] for two in range(2)]
            inputs[x].append(jnp.where(halves == (x == 0), fifth, 0.0).astype(BF16))
        rows = []
        for n in range(HEADS_HERE * per_head):
            first = ((C * y + core) * 2 + n // len(places)) * depth + places[n % len(places)]
            rows.append(weight_ref[pl.ds(pl.multiple_of(first, GRANULE), GRANULE), :])
        weights += rows + rows[4 * per_head :]
    weights = jnp.concatenate(weights, axis=0)
    return [
        jnp.dot(jnp.concatenate(blocks, axis=1), weights, preferred_element_type=F32) for blocks in inputs
    ]


def project_mine(place_ref, packed_ref, weight_ref, sum_ref):
    for x, total in enumerate(multiply(place_ref[0], place_ref[1], packed_ref, weight_ref)):
        sum_ref[x] = total


def project_other(place_ref, packed_ref, weight_ref, sum_ref, own_ref, send_ref):
    side = place_ref[1]
    totals = []
    for x, total in enumerate(multiply(1 - place_ref[0], side, packed_ref, weight_ref)):
        total = total + sum_ref[x]
        total = [total[r * SLOT : r * SLOT + length] for r, length in enumerate(LENGTHS)]
        totals.append(jnp.concatenate(total, axis=0))
    first = lax.rem(side, PAIR) == 0
    own_ref[...] = jnp.where(first, totals[0], totals[1])
    send_ref[...] = jnp.where(first, totals[1], totals[0]).astype(BF16)


def share_rows(granules):
    even = jnp.concatenate([granules[n] for n in range(0, X + 1, 2)], axis=0)
    odd = jnp.concatenate([granules[n] for n in range(1, X + 1, 2)], axis=0)
    blocks = [even]
    for block, away in ((even, 2), (odd, 1), (odd, X - 1)):
        blocks.append(lax.ppermute(block, "x", [(x, (x + away) % X) for x in range(X)]))
    return jnp.concatenate(blocks, axis=0)


def local(queries, keys_in, values, cluster_ids, out_weight):
    plane, side, core = lax.axis_index("z"), lax.axis_index("x"), lax.axis_index("c")
    third = lax.rem(plane, PARTS)
    width = out_weight.shape[1]

    send, granules = vmem_call(
        scatter_heads,
        56,
        [(Z, SLOT + 2 * ROWS, HEAD), (X + 1, GRANULE, width)],
        queries,
        keys_in,
        values,
        cluster_ids.reshape(1, TOK),
        out_weight,
    )
    here = lax.all_to_all(send, "z", 0, 0, tiled=True)
    weight = lax.all_gather(share_rows(granules), "z", axis=0, tiled=True)
    kv = here[:, SLOT:, :]
    turns = [
        [(PARTS * h + r, PARTS * h + (r + k) % PARTS) for h in range(HEADS_HERE) for r in range(PARTS)]
        for k in (1, 2)
    ]
    kv_others = [lax.ppermute(kv, "z", turn) for turn in turns]
    query = jnp.broadcast_to(here[:, :SLOT, :].reshape(1, Z * SLOT, HEAD), (X, Z * SLOT, HEAD))
    query = lax.all_to_all(query, "x", 0, 0, tiled=True)

    home = (X * jnp.arange(Z, dtype=jnp.int32) + side) * TOK
    key_code = here[:, ID_ROW + 1, :].astype(F32) * POSITIONS + (
        home[:, None] + jnp.arange(HEAD, dtype=jnp.int32)[None, :]
    ).astype(F32)
    key_code = jnp.stack(
        [
            jnp.pad(
                key_code[:, start : start + length], ((0, 0), (0, SLOT - length)), constant_values=NEVER
            ).reshape(Z * SLOT)
            for start, length in zip(STARTS, LENGTHS)
        ]
    )
    (part,) = vmem_call(
        attend,
        20,
        [(X, (Z + 1) * SLOT, HEAD)],
        query,
        kv,
        kv_others[0],
        kv_others[1],
        key_code,
        scalars=third.reshape(1),
        cost=pl.CostEstimate(flops=1 << 36, bytes_accessed=1 << 22, transcendentals=1 << 22),
    )
    part = lax.all_to_all(part, "x", 0, 0, tiled=True)
    (joined,) = vmem_call(join, 8, [(Z, SLOT, HEAD)], part)
    joined = lax.all_to_all(joined, "z", 0, 0, tiled=True)
    (packed,) = vmem_call(assemble, 8, [(Y, (2 * PAIR + 1) * PARTS * SLOT, HEAD)], joined)
    packed = lax.all_to_all(packed, "y", 0, 0, tiled=True)
    others = lax.ppermute(packed, "c", [(0, 1), (1, 0)])
    place = jnp.stack([core, side])
    (sums,) = vmem_call(
        project_mine,
        16,
        [(PAIR, PARTS * SLOT, width)],
        packed,
        weight,
        scalars=place,
        kinds=[F32],
        cost=pl.CostEstimate(flops=1 << 31, bytes_accessed=1 << 23, transcendentals=0),
    )
    own, send = vmem_call(
        project_other,
        16,
        [(TOK, width), (TOK, width)],
        others,
        weight,
        sums,
        scalars=place,
        kinds=[F32, BF16],
    )
    came = lax.ppermute(send, "x", [(x, x + 1 - 2 * (x % PAIR)) for x in range(X)])
    return (own + came.astype(F32)).astype(BF16)


def solution(mesh):
    fine = Mesh(mesh.devices.reshape(Z, X, Y, C), ("z", "x", "y", "c"))
    both = P(("z", "x"), ("y", "c"))
    return jax.shard_map(
        local,
        mesh=fine,
        in_specs=(both, both, both, P(("z", "x"), None), both),
        out_specs=both,
        check_vma=False,
    )
```

```python
import functools

import jax
import jax.numpy as jnp
from jax import lax
from jax.experimental import pallas as pl
from jax.experimental.pallas import tpu as pltpu
from jax.sharding import Mesh
from jax.sharding import PartitionSpec as P

HEAD = 128
HEADS_HERE = 5
TOK = 128
Z, X, Y, C = 16, 4, 4, 2
PARTS = 3
STARTS = (0, 44, 88)
LENGTHS = (44, 44, 40)
SLOT = 48
ROWS = 44
ID_ROW = 46
POSITIONS = 8192
NEVER = 1e9
BLOCKED = -1e30
F32 = jnp.float32
BF16 = jnp.bfloat16
LOG2E = 1.4426950408889634
PAIR = 2
SHARE = 64
GRANULE = 16


def vmem_call(body, mebibytes, shapes, *operands, scalars=None, kinds=None, cost=None):
    specs = [pl.BlockSpec(memory_space=pltpu.VMEM)] * len(operands)
    if scalars is not None:
        specs = [pl.BlockSpec(memory_space=pltpu.SMEM)] + specs
        operands = (scalars,) + operands
    kinds = kinds or [BF16] * len(shapes)
    return pl.pallas_call(
        body,
        out_shape=[jax.ShapeDtypeStruct(shape, kind) for shape, kind in zip(shapes, kinds)],
        in_specs=specs,
        out_specs=[pl.BlockSpec(memory_space=pltpu.VMEM)] * len(shapes),
        cost_estimate=cost,
        compiler_params=pltpu.CompilerParams(vmem_limit_bytes=mebibytes * 1024 * 1024),
    )(*operands)


def scatter_heads(q_ref, k_ref, v_ref, ids_ref, weight_ref, out_ref, granules_ref):
    for n in range(X + 1):
        granules_ref[n] = weight_ref[n * GRANULE : (n + 1) * GRANULE, :]
    ids = ids_ref[...].astype(F32)
    lane = lax.broadcasted_iota(jnp.int32, (SLOT, HEAD), 1)
    row = lax.broadcasted_iota(jnp.int32, (SLOT, HEAD), 0)
    id_rows = []
    for start, length in zip(STARTS, LENGTHS):
        moved = ids if start == 0 else pltpu.roll(ids, TOK - start, 1)
        id_rows.append(jnp.where(lane < length, jnp.broadcast_to(moved, (SLOT, HEAD)), -1.0))
    every = jnp.broadcast_to(ids, (SLOT, HEAD))
    source = lax.broadcasted_iota(jnp.int32, (HEAD, HEAD), 0)
    to = lax.broadcasted_iota(jnp.int32, (HEAD, HEAD), 1)
    origin = (to % SHARE) // GRANULE * (PAIR * GRANULE) + to // SHARE * GRANULE + to % GRANULE
    turn = jnp.where(source == origin, 1.0, 0.0).astype(BF16)
    for h in range(HEADS_HERE):
        blocks = []
        for part, ref in enumerate((q_ref, k_ref, v_ref)):
            block = ref[:, h * HEAD : (h + 1) * HEAD]
            if part == 2:
                block = jnp.dot(block, turn, preferred_element_type=F32)
            blocks.append(jnp.concatenate([block.astype(F32), jnp.zeros((16, HEAD), F32)], axis=0))
        for r, (start, length) in enumerate(zip(STARTS, LENGTHS)):
            query, key, value = [
                jnp.where(row < length, block[start : start + SLOT], 0.0) for block in blocks
            ]
            query = jnp.where(row == ID_ROW, id_rows[r], query)
            query = jnp.where(row == ID_ROW + 1, every, query)
            slot = jnp.concatenate([query, key[:ROWS], value[:ROWS]], axis=0)
            out_ref[PARTS * h + r] = slot.astype(BF16)
    out_ref[PARTS * HEADS_HERE] = jnp.zeros((SLOT + 2 * ROWS, HEAD), BF16)


def attend(third_ref, q_ref, kv0_ref, kv1_ref, kv2_ref, kcode_ref, out_ref):
    rows = Z * SLOT
    third = third_ref[0]
    order = [third, lax.rem(third + 2, PARTS), lax.rem(third + 1, PARTS)]
    key_codes = [kcode_ref[pl.ds(j, 1), :] for j in order]
    parts = [ref[...].astype(F32) for ref in (kv0_ref, kv1_ref, kv2_ref)]
    keys = [part[:, :SLOT].astype(BF16).reshape(rows, HEAD) for part in parts]
    ones = jnp.ones((rows, HEAD), BF16)
    vals = []
    for part in parts:
        turned = [pltpu.roll(part[z, 2 * ROWS - SLOT :], ROWS, 0) for z in range(Z)]
        vals.append(jnp.concatenate([jnp.concatenate(turned, axis=0).astype(BF16), ones], axis=1))
    tile = 16
    at = ID_ROW % tile
    ids = jnp.concatenate(
        [
            q_ref[x, z * SLOT + ID_ROW - at : z * SLOT + ID_ROW - at + tile, :].astype(F32)[at : at + 1]
            for x in range(X)
            for z in range(Z)
        ],
        axis=0,
    )
    which = lax.broadcasted_iota(jnp.int32, (X * Z, HEAD), 0)
    home = (X * (which % Z) + which // Z) * TOK + third * STARTS[1]
    first = ids * POSITIONS
    last = first + (home + lax.broadcasted_iota(jnp.int32, (X * Z, HEAD), 1)).astype(F32)
    codes = jnp.concatenate([first, last], axis=0).T
    lane = lax.broadcasted_iota(jnp.int32, (SLOT, HEAD), 1)
    group = 4
    halves = lax.broadcasted_iota(jnp.int32, (group * SLOT, HEAD), 1) < SHARE
    stats = [jnp.zeros((SLOT, HEAD), F32) for _ in range(X // PAIR)]
    for g in range(Z // group):
        count = -(-(g + 1) * group * SLOT // HEAD) * HEAD
        zs = range(g * group, (g + 1) * group)
        normals = []
        for x in range(X):
            low_code = jnp.concatenate([codes[:SLOT, x * Z + z : x * Z + z + 1] for z in zs], axis=0)
            high_code = jnp.concatenate(
                [codes[:SLOT, (X + x) * Z + z : (X + x) * Z + z + 1] for z in zs], axis=0
            )
            query = q_ref[x, g * group * SLOT : (g + 1) * group * SLOT, :]
            scores = []
            for j in range(PARTS):
                score = lax.dot_general(
                    query, keys[j][:count], (((1,), (1,)), ((), ())), preferred_element_type=F32
                ) * (HEAD ** (-0.5) * LOG2E)
                key_code = key_codes[j][:, :count]
                allowed = (key_code <= high_code) & (key_code >= low_code)
                scores.append(jnp.where(allowed, score, BLOCKED))
            peak = functools.reduce(jnp.maximum, [jnp.max(s, axis=1, keepdims=True) for s in scores])
            output = jnp.zeros((group * SLOT, 2 * HEAD), F32)
            for j in range(PARTS):
                expo = jnp.exp2(scores[j] - peak)
                output = output + jnp.dot(
                    expo.astype(BF16), vals[j][:count], preferred_element_type=F32
                )
            normals.append(output[:, :HEAD] / output[:, HEAD:])
            logsum = peak + jnp.log2(output[:, HEAD:])
            for n in range(group):
                at = x % PAIR * Z + g * group + n
                stats[x // PAIR] = jnp.where(lane == at, logsum[n * SLOT : (n + 1) * SLOT], stats[x // PAIR])
        for first in range(0, X, PAIR):
            one, two = normals[first : first + PAIR]
            span = slice(g * group * SLOT, (g + 1) * group * SLOT)
            out_ref[first, span, :] = jnp.where(halves, one, pltpu.roll(two, SHARE, 1)).astype(BF16)
            out_ref[first + 1, span, :] = jnp.where(halves, pltpu.roll(one, SHARE, 1), two).astype(BF16)
    for pair, logsum in enumerate(stats):
        high = logsum.astype(BF16).astype(F32)
        rest = logsum - high
        middle = rest.astype(BF16).astype(F32)
        low = rest - middle
        table = high + pltpu.roll(middle, PAIR * Z, 1) + pltpu.roll(low, 2 * PAIR * Z, 1)
        for x in range(PAIR):
            out_ref[PAIR * pair + x, rows:, :] = table.astype(BF16)


def join(part_ref, out_ref):
    rows = Z * SLOT
    sums = []
    for x in range(X):
        stat = part_ref[x, rows:, :].astype(F32)
        sums.append(stat + pltpu.roll(stat, HEAD - PAIR * Z, 1) + pltpu.roll(stat, HEAD - 2 * PAIR * Z, 1))
    peak = functools.reduce(jnp.maximum, sums)
    weights = [jnp.exp2(s - peak) for s in sums]
    total = functools.reduce(jnp.add, weights)
    weights = [w / total for w in weights]
    half = lax.broadcasted_iota(jnp.int32, (SLOT, HEAD), 1) // SHARE
    for z in range(Z):
        joined = functools.reduce(
            jnp.add,
            [
                jnp.take_along_axis(weights[x], half * Z + z, axis=1)
                * part_ref[x, z * SLOT : (z + 1) * SLOT, :].astype(F32)
                for x in range(X)
            ],
        )
        out_ref[z] = joined.astype(BF16)


def assemble(part_ref, out_ref):
    halves = lax.broadcasted_iota(jnp.int32, (SLOT, HEAD), 1) < SHARE
    for r in range(PARTS):
        for two in range(2):
            one, other = [part_ref[PARTS * (2 * two + n) + r].astype(F32) for n in range(2)]
            blocks = (
                jnp.where(halves, one, pltpu.roll(other, SHARE, 1)),
                jnp.where(halves, pltpu.roll(one, SHARE, 1), other),
            )
            for x, block in enumerate(blocks):
                first = ((2 * x + two) * PARTS + r) * SLOT
                for y in range(Y):
                    out_ref[y, first : first + SLOT, :] = block.astype(BF16)
        first = (2 * PAIR * PARTS + r) * SLOT
        for y in range(Y):
            out_ref[y, first : first + SLOT, :] = part_ref[PARTS * (HEADS_HERE - 1) + r]


def order_rows(place_ref, weight_ref, mine_ref, other_ref):
    core, side = place_ref[0], place_ref[1]
    depth = weight_ref.shape[0] // Z
    member = lax.rem(side, PAIR)
    places = []
    for m in range(depth // GRANULE):
        number = 2 * m + member
        holder, n = lax.div(number, X + 1), lax.rem(number, X + 1)
        away = lax.rem(holder + X - side, X)
        base = jnp.where(away == 0, 0, jnp.where(away == 1, 8, jnp.where(away == 2, 3, 6)))
        places.append((base + lax.div(n, 2)) * GRANULE)
    per_head = SHARE // GRANULE
    for which, out_ref in ((core, mine_ref), (1 - core, other_ref)):
        for y in range(Y):
            rows = []
            for n in range(HEADS_HERE * per_head):
                first = ((C * y + which) * 2 + n // len(places)) * depth + places[n % len(places)]
                rows.append(weight_ref[pl.ds(pl.multiple_of(first, GRANULE), GRANULE), :])
            rows += rows[4 * per_head :]
            for n, row in enumerate(rows):
                first = (y * len(rows) + n) * GRANULE
                out_ref[first : first + GRANULE, :] = row


def multiply(packed_ref, weight_ref):
    span = PARTS * SLOT
    halves = lax.broadcasted_iota(jnp.int32, (span, HEAD), 1) < SHARE
    inputs = [[] for _ in range(PAIR)]
    for y in range(Y):
        fifth = packed_ref[y, 2 * PAIR * span :, :].astype(F32)
        for x in range(PAIR):
            inputs[x] += [packed_ref[y, (2 * x + two) * span : (2 * x + two + 1) * span, :] for two in range(2)]
            inputs[x].append(jnp.where(halves == (x == 0), fifth, 0.0).astype(BF16))
    weights = weight_ref[...]
    return [
        jnp.dot(jnp.concatenate(blocks, axis=1), weights, preferred_element_type=F32) for blocks in inputs
    ]


def project_mine(packed_ref, weight_ref, sum_ref):
    for x, total in enumerate(multiply(packed_ref, weight_ref)):
        sum_ref[x] = total


def project_other(place_ref, packed_ref, weight_ref, sum_ref, own_ref, send_ref):
    totals = []
    for x, total in enumerate(multiply(packed_ref, weight_ref)):
        total = total + sum_ref[x]
        total = [total[r * SLOT : r * SLOT + length] for r, length in enumerate(LENGTHS)]
        totals.append(jnp.concatenate(total, axis=0))
    first = lax.rem(place_ref[1], PAIR) == 0
    own_ref[...] = jnp.where(first, totals[0], totals[1])
    send_ref[...] = jnp.where(first, totals[1], totals[0]).astype(BF16)


def share_rows(granules):
    even = jnp.concatenate([granules[n] for n in range(0, X + 1, 2)], axis=0)
    odd = jnp.concatenate([granules[n] for n in range(1, X + 1, 2)], axis=0)
    blocks = [even]
    for block, away in ((even, 2), (odd, 1), (odd, X - 1)):
        blocks.append(lax.ppermute(block, "x", [(x, (x + away) % X) for x in range(X)]))
    return jnp.concatenate(blocks, axis=0)


def local(queries, keys_in, values, cluster_ids, out_weight):
    plane, side, core = lax.axis_index("z"), lax.axis_index("x"), lax.axis_index("c")
    third = lax.rem(plane, PARTS)
    width = out_weight.shape[1]

    send, granules = vmem_call(
        scatter_heads,
        56,
        [(Z, SLOT + 2 * ROWS, HEAD), (X + 1, GRANULE, width)],
        queries,
        keys_in,
        values,
        cluster_ids.reshape(1, TOK),
        out_weight,
    )
    here = lax.all_to_all(send, "z", 0, 0, tiled=True)
    weight = lax.all_gather(share_rows(granules), "z", axis=0, tiled=True)
    kv = here[:, SLOT:, :]
    turns = [
        [(PARTS * h + r, PARTS * h + (r + k) % PARTS) for h in range(HEADS_HERE) for r in range(PARTS)]
        for k in (1, 2)
    ]
    kv_others = [lax.ppermute(kv, "z", turn) for turn in turns]
    query = jnp.broadcast_to(here[:, :SLOT, :].reshape(1, Z * SLOT, HEAD), (X, Z * SLOT, HEAD))
    query = lax.all_to_all(query, "x", 0, 0, tiled=True)

    home = (X * jnp.arange(Z, dtype=jnp.int32) + side) * TOK
    key_code = here[:, ID_ROW + 1, :].astype(F32) * POSITIONS + (
        home[:, None] + jnp.arange(HEAD, dtype=jnp.int32)[None, :]
    ).astype(F32)
    key_code = jnp.stack(
        [
            jnp.pad(
                key_code[:, start : start + length], ((0, 0), (0, SLOT - length)), constant_values=NEVER
            ).reshape(Z * SLOT)
            for start, length in zip(STARTS, LENGTHS)
        ]
    )
    (part,) = vmem_call(
        attend,
        20,
        [(X, (Z + 1) * SLOT, HEAD)],
        query,
        kv,
        kv_others[0],
        kv_others[1],
        key_code,
        scalars=third.reshape(1),
        cost=pl.CostEstimate(flops=1 << 36, bytes_accessed=1 << 22, transcendentals=1 << 22),
    )
    part = lax.all_to_all(part, "x", 0, 0, tiled=True)
    (joined,) = vmem_call(join, 8, [(Z, SLOT, HEAD)], part)
    joined = lax.all_to_all(joined, "z", 0, 0, tiled=True)
    (packed,) = vmem_call(assemble, 8, [(Y, (2 * PAIR + 1) * PARTS * SLOT, HEAD)], joined)
    packed = lax.all_to_all(packed, "y", 0, 0, tiled=True)
    place = jnp.stack([core, side])
    depth = Y * (HEADS_HERE + 1) * SHARE
    weight_mine, weight_other = vmem_call(
        order_rows,
        12,
        [(depth, width), (depth, width)],
        weight,
        scalars=place,
        cost=pl.CostEstimate(flops=0, bytes_accessed=1 << 24, transcendentals=0),
    )
    packed, weight_other = lax.optimization_barrier((packed, weight_other))
    others = lax.ppermute(packed, "c", [(0, 1), (1, 0)])
    (sums,) = vmem_call(
        project_mine,
        16,
        [(PAIR, PARTS * SLOT, width)],
        packed,
        weight_mine,
        kinds=[F32],
        cost=pl.CostEstimate(flops=1 << 31, bytes_accessed=1 << 23, transcendentals=0),
    )
    own, send = vmem_call(
        project_other,
        16,
        [(TOK, width), (TOK, width)],
        others,
        weight_other,
        sums,
        scalars=place,
        kinds=[F32, BF16],
    )
    came = lax.ppermute(send, "x", [(x, x + 1 - 2 * (x % PAIR)) for x in range(X)])
    return (own + came.astype(F32)).astype(BF16)


def solution(mesh):
    fine = Mesh(mesh.devices.reshape(Z, X, Y, C), ("z", "x", "y", "c"))
    both = P(("z", "x"), ("y", "c"))
    return jax.shard_map(
        local,
        mesh=fine,
        in_specs=(both, both, both, P(("z", "x"), None), both),
        out_specs=both,
        check_vma=False,
    )
```

```python
import functools

import jax
import jax.numpy as jnp
from jax import lax
from jax.experimental import pallas as pl
from jax.experimental.pallas import tpu as pltpu
from jax.sharding import Mesh
from jax.sharding import PartitionSpec as P

HEAD = 128
HEADS_HERE = 5
TOK = 128
Z, X, Y, C = 16, 4, 4, 2
PARTS = 3
STARTS = (0, 44, 88)
LENGTHS = (44, 44, 40)
SLOT = 48
ROWS = 44
ID_ROW = 46
POSITIONS = 8192
NEVER = 1e9
BLOCKED = -1e30
F32 = jnp.float32
BF16 = jnp.bfloat16
LOG2E = 1.4426950408889634
PAIR = 2
SHARE = 64
GRANULE = 16


def vmem_call(body, mebibytes, shapes, *operands, scalars=None, kinds=None, cost=None):
    specs = [pl.BlockSpec(memory_space=pltpu.VMEM)] * len(operands)
    if scalars is not None:
        specs = [pl.BlockSpec(memory_space=pltpu.SMEM)] + specs
        operands = (scalars,) + operands
    kinds = kinds or [BF16] * len(shapes)
    return pl.pallas_call(
        body,
        out_shape=[jax.ShapeDtypeStruct(shape, kind) for shape, kind in zip(shapes, kinds)],
        in_specs=specs,
        out_specs=[pl.BlockSpec(memory_space=pltpu.VMEM)] * len(shapes),
        cost_estimate=cost,
        compiler_params=pltpu.CompilerParams(vmem_limit_bytes=mebibytes * 1024 * 1024),
    )(*operands)


def scatter_heads(q_ref, k_ref, v_ref, ids_ref, weight_ref, out_ref, granules_ref):
    for n in range(X + 1):
        granules_ref[n] = weight_ref[n * GRANULE : (n + 1) * GRANULE, :]
    ids = ids_ref[...].astype(F32)
    lane = lax.broadcasted_iota(jnp.int32, (SLOT, HEAD), 1)
    row = lax.broadcasted_iota(jnp.int32, (SLOT, HEAD), 0)
    id_rows = []
    for start, length in zip(STARTS, LENGTHS):
        moved = ids if start == 0 else pltpu.roll(ids, TOK - start, 1)
        id_rows.append(jnp.where(lane < length, jnp.broadcast_to(moved, (SLOT, HEAD)), -1.0))
    every = jnp.broadcast_to(ids, (SLOT, HEAD))
    source = lax.broadcasted_iota(jnp.int32, (HEAD, HEAD), 0)
    to = lax.broadcasted_iota(jnp.int32, (HEAD, HEAD), 1)
    origin = (to % SHARE) // GRANULE * (PAIR * GRANULE) + to // SHARE * GRANULE + to % GRANULE
    turn = jnp.where(source == origin, 1.0, 0.0).astype(BF16)
    for h in range(HEADS_HERE):
        blocks = []
        for part, ref in enumerate((q_ref, k_ref, v_ref)):
            block = ref[:, h * HEAD : (h + 1) * HEAD]
            if part == 2:
                block = jnp.dot(block, turn, preferred_element_type=F32)
            blocks.append(jnp.concatenate([block.astype(F32), jnp.zeros((16, HEAD), F32)], axis=0))
        for r, (start, length) in enumerate(zip(STARTS, LENGTHS)):
            query, key, value = [
                jnp.where(row < length, block[start : start + SLOT], 0.0) for block in blocks
            ]
            query = jnp.where(row == ID_ROW, id_rows[r], query)
            query = jnp.where(row == ID_ROW + 1, every, query)
            slot = jnp.concatenate([query, key[:ROWS], value[:ROWS]], axis=0)
            out_ref[PARTS * h + r] = slot.astype(BF16)
    out_ref[PARTS * HEADS_HERE] = jnp.zeros((SLOT + 2 * ROWS, HEAD), BF16)


def attend(third_ref, q_ref, kv0_ref, kv1_ref, kv2_ref, kcode_ref, out_ref):
    rows = Z * SLOT
    third = third_ref[0]
    order = [third, lax.rem(third + 2, PARTS), lax.rem(third + 1, PARTS)]
    key_codes = [kcode_ref[pl.ds(j, 1), :] for j in order]
    parts = [ref[...].astype(F32) for ref in (kv0_ref, kv1_ref, kv2_ref)]
    keys = [part[:, :SLOT].astype(BF16).reshape(rows, HEAD) for part in parts]
    ones = jnp.ones((rows, HEAD), BF16)
    vals = []
    for part in parts:
        turned = [pltpu.roll(part[z, 2 * ROWS - SLOT :], ROWS, 0) for z in range(Z)]
        vals.append(jnp.concatenate([jnp.concatenate(turned, axis=0).astype(BF16), ones], axis=1))
    tile = 16
    at = ID_ROW % tile
    ids = jnp.concatenate(
        [
            q_ref[x, z * SLOT + ID_ROW - at : z * SLOT + ID_ROW - at + tile, :].astype(F32)[at : at + 1]
            for x in range(X)
            for z in range(Z)
        ],
        axis=0,
    )
    which = lax.broadcasted_iota(jnp.int32, (X * Z, HEAD), 0)
    home = (X * (which % Z) + which // Z) * TOK + third * STARTS[1]
    first = ids * POSITIONS
    last = first + (home + lax.broadcasted_iota(jnp.int32, (X * Z, HEAD), 1)).astype(F32)
    codes = jnp.concatenate([first, last], axis=0).T
    lane = lax.broadcasted_iota(jnp.int32, (SLOT, HEAD), 1)
    group = 4
    halves = lax.broadcasted_iota(jnp.int32, (group * SLOT, HEAD), 1) < SHARE
    stats = [jnp.zeros((SLOT, HEAD), F32) for _ in range(X // PAIR)]
    for g in range(Z // group):
        count = -(-(g + 1) * group * SLOT // HEAD) * HEAD
        zs = range(g * group, (g + 1) * group)
        normals = []
        for x in range(X):
            low_code = jnp.concatenate([codes[:SLOT, x * Z + z : x * Z + z + 1] for z in zs], axis=0)
            high_code = jnp.concatenate(
                [codes[:SLOT, (X + x) * Z + z : (X + x) * Z + z + 1] for z in zs], axis=0
            )
            query = q_ref[x, g * group * SLOT : (g + 1) * group * SLOT, :]
            scores = []
            for j in range(PARTS):
                score = lax.dot_general(
                    query, keys[j][:count], (((1,), (1,)), ((), ())), preferred_element_type=F32
                ) * (HEAD ** (-0.5) * LOG2E)
                key_code = key_codes[j][:, :count]
                allowed = (key_code <= high_code) & (key_code >= low_code)
                scores.append(jnp.where(allowed, score, BLOCKED))
            peak = functools.reduce(jnp.maximum, [jnp.max(s, axis=1, keepdims=True) for s in scores])
            output = jnp.zeros((group * SLOT, 2 * HEAD), F32)
            for j in range(PARTS):
                expo = jnp.exp2(scores[j] - peak)
                output = output + jnp.dot(
                    expo.astype(BF16), vals[j][:count], preferred_element_type=F32
                )
            normals.append(output[:, :HEAD] / output[:, HEAD:])
            logsum = peak + jnp.log2(output[:, HEAD:])
            for n in range(group):
                at = x % PAIR * Z + g * group + n
                stats[x // PAIR] = jnp.where(lane == at, logsum[n * SLOT : (n + 1) * SLOT], stats[x // PAIR])
        for first in range(0, X, PAIR):
            one, two = normals[first : first + PAIR]
            span = slice(g * group * SLOT, (g + 1) * group * SLOT)
            out_ref[first, span, :] = jnp.where(halves, one, pltpu.roll(two, SHARE, 1)).astype(BF16)
            out_ref[first + 1, span, :] = jnp.where(halves, pltpu.roll(one, SHARE, 1), two).astype(BF16)
    for pair, logsum in enumerate(stats):
        high = logsum.astype(BF16).astype(F32)
        rest = logsum - high
        middle = rest.astype(BF16).astype(F32)
        low = rest - middle
        table = high + pltpu.roll(middle, PAIR * Z, 1) + pltpu.roll(low, 2 * PAIR * Z, 1)
        for x in range(PAIR):
            out_ref[PAIR * pair + x, rows:, :] = table.astype(BF16)


def join(part_ref, out_ref):
    rows = Z * SLOT
    sums = []
    for x in range(X):
        stat = part_ref[x, rows:, :].astype(F32)
        sums.append(stat + pltpu.roll(stat, HEAD - PAIR * Z, 1) + pltpu.roll(stat, HEAD - 2 * PAIR * Z, 1))
    peak = functools.reduce(jnp.maximum, sums)
    weights = [jnp.exp2(s - peak) for s in sums]
    total = functools.reduce(jnp.add, weights)
    weights = [w / total for w in weights]
    half = lax.broadcasted_iota(jnp.int32, (SLOT, HEAD), 1) // SHARE
    for z in range(Z):
        joined = functools.reduce(
            jnp.add,
            [
                jnp.take_along_axis(weights[x], half * Z + z, axis=1)
                * part_ref[x, z * SLOT : (z + 1) * SLOT, :].astype(F32)
                for x in range(X)
            ],
        )
        out_ref[z] = joined.astype(BF16)


def assemble(part_ref, out_ref):
    halves = lax.broadcasted_iota(jnp.int32, (SLOT, HEAD), 1) < SHARE
    for r in range(PARTS):
        for two in range(2):
            one, other = [part_ref[PARTS * (2 * two + n) + r].astype(F32) for n in range(2)]
            blocks = (
                jnp.where(halves, one, pltpu.roll(other, SHARE, 1)),
                jnp.where(halves, pltpu.roll(one, SHARE, 1), other),
            )
            for x, block in enumerate(blocks):
                first = ((2 * x + two) * PARTS + r) * SLOT
                for y in range(Y):
                    out_ref[y, first : first + SLOT, :] = block.astype(BF16)
        first = (2 * PAIR * PARTS + r) * SLOT
        for y in range(Y):
            out_ref[y, first : first + SLOT, :] = part_ref[PARTS * (HEADS_HERE - 1) + r]


def order_rows(place_ref, weight_ref, mine_ref, other_ref):
    core, side = place_ref[0], place_ref[1]
    depth = weight_ref.shape[0] // Z
    member = lax.rem(side, PAIR)
    places = []
    for m in range(depth // GRANULE):
        number = 2 * m + member
        holder, n = lax.div(number, X + 1), lax.rem(number, X + 1)
        away = lax.rem(holder + X - side, X)
        base = jnp.where(away == 0, 0, jnp.where(away == 1, 8, jnp.where(away == 2, 3, 6)))
        places.append((base + lax.div(n, 2)) * GRANULE)
    per_head = SHARE // GRANULE
    for which, out_ref in ((core, mine_ref), (1 - core, other_ref)):
        for y in range(Y):
            rows = []
            for n in range(HEADS_HERE * per_head):
                first = ((C * y + which) * 2 + n // len(places)) * depth + places[n % len(places)]
                rows.append(weight_ref[pl.ds(pl.multiple_of(first, GRANULE), GRANULE), :])
            rows += rows[4 * per_head :]
            for n, row in enumerate(rows):
                first = (y * len(rows) + n) * GRANULE
                out_ref[first : first + GRANULE, :] = row


def multiply(packed_ref, weight_ref):
    span = PARTS * SLOT
    halves = lax.broadcasted_iota(jnp.int32, (span, HEAD), 1) < SHARE
    inputs = [[] for _ in range(PAIR)]
    for y in range(Y):
        fifth = packed_ref[y, 2 * PAIR * span :, :].astype(F32)
        for x in range(PAIR):
            inputs[x] += [packed_ref[y, (2 * x + two) * span : (2 * x + two + 1) * span, :] for two in range(2)]
            inputs[x].append(jnp.where(halves == (x == 0), fifth, 0.0).astype(BF16))
    weights = weight_ref[...]
    return [
        jnp.dot(jnp.concatenate(blocks, axis=1), weights, preferred_element_type=F32) for blocks in inputs
    ]


def project_mine(packed_ref, weight_ref, sum_ref):
    for x, total in enumerate(multiply(packed_ref, weight_ref)):
        sum_ref[x] = total


def project_other(place_ref, packed_ref, weight_ref, sum_ref, out_ref):
    x = place_ref[0]
    span = PARTS * SLOT
    halves = lax.broadcasted_iota(jnp.int32, (span, HEAD), 1) // SHARE
    blocks = []
    for y in range(Y):
        fifth = packed_ref[y, 2 * PAIR * span :, :].astype(F32)
        for two in range(2):
            first = pl.multiple_of((2 * x + two) * span, GRANULE)
            blocks.append(packed_ref[y, pl.ds(first, span), :])
        blocks.append(jnp.where(halves == x, fifth, 0.0).astype(BF16))
    total = jnp.dot(jnp.concatenate(blocks, axis=1), weight_ref[...], preferred_element_type=F32)
    total = total + sum_ref[x]
    total = [total[r * SLOT : r * SLOT + length] for r, length in enumerate(LENGTHS)]
    out_ref[...] = jnp.concatenate(total, axis=0).astype(out_ref.dtype)


def share_rows(granules):
    even = jnp.concatenate([granules[n] for n in range(0, X + 1, 2)], axis=0)
    odd = jnp.concatenate([granules[n] for n in range(1, X + 1, 2)], axis=0)
    blocks = [even]
    for block, away in ((even, 2), (odd, 1), (odd, X - 1)):
        blocks.append(lax.ppermute(block, "x", [(x, (x + away) % X) for x in range(X)]))
    return jnp.concatenate(blocks, axis=0)


def local(queries, keys_in, values, cluster_ids, out_weight):
    plane, side, core = lax.axis_index("z"), lax.axis_index("x"), lax.axis_index("c")
    third = lax.rem(plane, PARTS)
    width = out_weight.shape[1]

    send, granules = vmem_call(
        scatter_heads,
        56,
        [(Z, SLOT + 2 * ROWS, HEAD), (X + 1, GRANULE, width)],
        queries,
        keys_in,
        values,
        cluster_ids.reshape(1, TOK),
        out_weight,
    )
    here = lax.all_to_all(send, "z", 0, 0, tiled=True)
    weight = lax.all_gather(share_rows(granules), "z", axis=0, tiled=True)
    kv = here[:, SLOT:, :]
    turns = [
        [(PARTS * h + r, PARTS * h + (r + k) % PARTS) for h in range(HEADS_HERE) for r in range(PARTS)]
        for k in (1, 2)
    ]
    kv_others = [lax.ppermute(kv, "z", turn) for turn in turns]
    query = jnp.broadcast_to(here[:, :SLOT, :].reshape(1, Z * SLOT, HEAD), (X, Z * SLOT, HEAD))
    query = lax.all_to_all(query, "x", 0, 0, tiled=True)

    home = (X * jnp.arange(Z, dtype=jnp.int32) + side) * TOK
    key_code = here[:, ID_ROW + 1, :].astype(F32) * POSITIONS + (
        home[:, None] + jnp.arange(HEAD, dtype=jnp.int32)[None, :]
    ).astype(F32)
    key_code = jnp.stack(
        [
            jnp.pad(
                key_code[:, start : start + length], ((0, 0), (0, SLOT - length)), constant_values=NEVER
            ).reshape(Z * SLOT)
            for start, length in zip(STARTS, LENGTHS)
        ]
    )
    (part,) = vmem_call(
        attend,
        20,
        [(X, (Z + 1) * SLOT, HEAD)],
        query,
        kv,
        kv_others[0],
        kv_others[1],
        key_code,
        scalars=third.reshape(1),
        cost=pl.CostEstimate(flops=1 << 36, bytes_accessed=1 << 22, transcendentals=1 << 22),
    )
    part = lax.all_to_all(part, "x", 0, 0, tiled=True)
    (joined,) = vmem_call(join, 8, [(Z, SLOT, HEAD)], part)
    joined = lax.all_to_all(joined, "z", 0, 0, tiled=True)
    (packed,) = vmem_call(assemble, 8, [(Y, (2 * PAIR + 1) * PARTS * SLOT, HEAD)], joined)
    packed = lax.all_to_all(packed, "y", 0, 0, tiled=True)
    place = jnp.stack([core, side])
    depth = Y * (HEADS_HERE + 1) * SHARE
    weight_mine, weight_other = vmem_call(
        order_rows,
        12,
        [(depth, width), (depth, width)],
        weight,
        scalars=place,
        cost=pl.CostEstimate(flops=0, bytes_accessed=1 << 24, transcendentals=0),
    )
    packed, weight_other = lax.optimization_barrier((packed, weight_other))
    others = lax.ppermute(packed, "c", [(0, 1), (1, 0)])
    (sums,) = vmem_call(
        project_mine,
        16,
        [(PAIR, PARTS * SLOT, width)],
        packed,
        weight_mine,
        kinds=[F32],
        cost=pl.CostEstimate(flops=1 << 31, bytes_accessed=1 << 23, transcendentals=0),
    )
    member = lax.rem(side, PAIR)
    own, send = [
        vmem_call(
            project_other,
            16,
            [(TOK, width)],
            others,
            weight_other,
            sums,
            scalars=which.reshape(1),
            kinds=[kind],
            cost=pl.CostEstimate(flops=1 << 31, bytes_accessed=1 << 23, transcendentals=0),
        )[0]
        for which, kind in ((member, F32), (1 - member, BF16))
    ]
    came = lax.ppermute(send, "x", [(x, x + 1 - 2 * (x % PAIR)) for x in range(X)])
    return (own + came.astype(F32)).astype(BF16)


def solution(mesh):
    fine = Mesh(mesh.devices.reshape(Z, X, Y, C), ("z", "x", "y", "c"))
    both = P(("z", "x"), ("y", "c"))
    return jax.shard_map(
        local,
        mesh=fine,
        in_specs=(both, both, both, P(("z", "x"), None), both),
        out_specs=both,
        check_vma=False,
    )
```

```python
import functools

import jax
import jax.numpy as jnp
from jax import lax
from jax.experimental import pallas as pl
from jax.experimental.pallas import tpu as pltpu
from jax.sharding import Mesh
from jax.sharding import PartitionSpec as P

HEAD = 128
HEADS_HERE = 5
TOK = 128
Z, X, Y, C = 16, 4, 4, 2
PARTS = 3
STARTS = (0, 44, 88)
LENGTHS = (44, 44, 40)
SLOT = 48
ROWS = 44
ID_ROW = 46
POSITIONS = 8192
NEVER = 1e9
BLOCKED = -1e30
F32 = jnp.float32
BF16 = jnp.bfloat16
LOG2E = 1.4426950408889634
PAIR = 2
SHARE = 64
GRANULE = 16


def vmem_call(body, mebibytes, shapes, *operands, scalars=None, kinds=None, cost=None):
    specs = [pl.BlockSpec(memory_space=pltpu.VMEM)] * len(operands)
    if scalars is not None:
        specs = [pl.BlockSpec(memory_space=pltpu.SMEM)] + specs
        operands = (scalars,) + operands
    kinds = kinds or [BF16] * len(shapes)
    return pl.pallas_call(
        body,
        out_shape=[jax.ShapeDtypeStruct(shape, kind) for shape, kind in zip(shapes, kinds)],
        in_specs=specs,
        out_specs=[pl.BlockSpec(memory_space=pltpu.VMEM)] * len(shapes),
        cost_estimate=cost,
        compiler_params=pltpu.CompilerParams(vmem_limit_bytes=mebibytes * 1024 * 1024),
    )(*operands)


def scatter_heads(q_ref, k_ref, v_ref, ids_ref, weight_ref, out_ref, granules_ref):
    for n in range(X + 1):
        granules_ref[n] = weight_ref[n * GRANULE : (n + 1) * GRANULE, :]
    ids = ids_ref[...].astype(F32)
    lane = lax.broadcasted_iota(jnp.int32, (SLOT, HEAD), 1)
    row = lax.broadcasted_iota(jnp.int32, (SLOT, HEAD), 0)
    id_rows = []
    for start, length in zip(STARTS, LENGTHS):
        moved = ids if start == 0 else pltpu.roll(ids, TOK - start, 1)
        id_rows.append(jnp.where(lane < length, jnp.broadcast_to(moved, (SLOT, HEAD)), -1.0))
    every = jnp.broadcast_to(ids, (SLOT, HEAD))
    source = lax.broadcasted_iota(jnp.int32, (HEAD, HEAD), 0)
    to = lax.broadcasted_iota(jnp.int32, (HEAD, HEAD), 1)
    origin = (to % SHARE) // GRANULE * (PAIR * GRANULE) + to // SHARE * GRANULE + to % GRANULE
    turn = jnp.where(source == origin, 1.0, 0.0).astype(BF16)
    for h in range(HEADS_HERE):
        blocks = []
        for part, ref in enumerate((q_ref, k_ref, v_ref)):
            block = ref[:, h * HEAD : (h + 1) * HEAD]
            if part == 2:
                block = jnp.dot(block, turn, preferred_element_type=F32)
            blocks.append(jnp.concatenate([block.astype(F32), jnp.zeros((16, HEAD), F32)], axis=0))
        for r, (start, length) in enumerate(zip(STARTS, LENGTHS)):
            query, key, value = [
                jnp.where(row < length, block[start : start + SLOT], 0.0) for block in blocks
            ]
            query = jnp.where(row == ID_ROW, id_rows[r], query)
            query = jnp.where(row == ID_ROW + 1, every, query)
            slot = jnp.concatenate([query, key[:ROWS], value[:ROWS]], axis=0)
            out_ref[PARTS * h + r] = slot.astype(BF16)
    out_ref[PARTS * HEADS_HERE] = jnp.zeros((SLOT + 2 * ROWS, HEAD), BF16)


def attend(third_ref, q_ref, kv0_ref, kv1_ref, kv2_ref, kcode_ref, out_ref):
    rows = Z * SLOT
    third = third_ref[0]
    order = [third, lax.rem(third + 2, PARTS), lax.rem(third + 1, PARTS)]
    key_codes = [kcode_ref[pl.ds(j, 1), :] for j in order]
    parts = [ref[...].astype(F32) for ref in (kv0_ref, kv1_ref, kv2_ref)]
    keys = [part[:, :SLOT].astype(BF16).reshape(rows, HEAD) for part in parts]
    ones = jnp.ones((rows, HEAD), BF16)
    vals = []
    for part in parts:
        turned = [pltpu.roll(part[z, 2 * ROWS - SLOT :], ROWS, 0) for z in range(Z)]
        vals.append(jnp.concatenate([jnp.concatenate(turned, axis=0).astype(BF16), ones], axis=1))
    tile = 16
    at = ID_ROW % tile
    ids = jnp.concatenate(
        [
            q_ref[x, z * SLOT + ID_ROW - at : z * SLOT + ID_ROW - at + tile, :].astype(F32)[at : at + 1]
            for x in range(X)
            for z in range(Z)
        ],
        axis=0,
    )
    which = lax.broadcasted_iota(jnp.int32, (X * Z, HEAD), 0)
    home = (X * (which % Z) + which // Z) * TOK + third * STARTS[1]
    first = ids * POSITIONS
    last = first + (home + lax.broadcasted_iota(jnp.int32, (X * Z, HEAD), 1)).astype(F32)
    codes = jnp.concatenate([first, last], axis=0).T
    lane = lax.broadcasted_iota(jnp.int32, (SLOT, HEAD), 1)
    group = 4
    halves = lax.broadcasted_iota(jnp.int32, (group * SLOT, HEAD), 1) < SHARE
    stats = [jnp.zeros((SLOT, HEAD), F32) for _ in range(X // PAIR)]
    for g in range(Z // group):
        count = -(-(g + 1) * group * SLOT // HEAD) * HEAD
        zs = range(g * group, (g + 1) * group)
        normals = []
        for x in range(X):
            low_code = jnp.concatenate([codes[:SLOT, x * Z + z : x * Z + z + 1] for z in zs], axis=0)
            high_code = jnp.concatenate(
                [codes[:SLOT, (X + x) * Z + z : (X + x) * Z + z + 1] for z in zs], axis=0
            )
            query = q_ref[x, g * group * SLOT : (g + 1) * group * SLOT, :]
            scores = []
            for j in range(PARTS):
                score = lax.dot_general(
                    query, keys[j][:count], (((1,), (1,)), ((), ())), preferred_element_type=F32
                ) * (HEAD ** (-0.5) * LOG2E)
                key_code = key_codes[j][:, :count]
                allowed = (key_code <= high_code) & (key_code >= low_code)
                scores.append(jnp.where(allowed, score, BLOCKED))
            peak = functools.reduce(jnp.maximum, [jnp.max(s, axis=1, keepdims=True) for s in scores])
            output = jnp.zeros((group * SLOT, 2 * HEAD), F32)
            for j in range(PARTS):
                expo = jnp.exp2(scores[j] - peak)
                output = output + jnp.dot(
                    expo.astype(BF16), vals[j][:count], preferred_element_type=F32
                )
            normals.append(output[:, :HEAD] / output[:, HEAD:])
            logsum = peak + jnp.log2(output[:, HEAD:])
            for n in range(group):
                at = x % PAIR * Z + g * group + n
                stats[x // PAIR] = jnp.where(lane == at, logsum[n * SLOT : (n + 1) * SLOT], stats[x // PAIR])
        for first in range(0, X, PAIR):
            one, two = normals[first : first + PAIR]
            span = slice(g * group * SLOT, (g + 1) * group * SLOT)
            out_ref[first, span, :] = jnp.where(halves, one, pltpu.roll(two, SHARE, 1)).astype(BF16)
            out_ref[first + 1, span, :] = jnp.where(halves, pltpu.roll(one, SHARE, 1), two).astype(BF16)
    for pair, logsum in enumerate(stats):
        high = logsum.astype(BF16).astype(F32)
        rest = logsum - high
        middle = rest.astype(BF16).astype(F32)
        low = rest - middle
        table = high + pltpu.roll(middle, PAIR * Z, 1) + pltpu.roll(low, 2 * PAIR * Z, 1)
        for x in range(PAIR):
            out_ref[PAIR * pair + x, rows:, :] = table.astype(BF16)


def join(part_ref, out_ref):
    rows = Z * SLOT
    sums = []
    for x in range(X):
        stat = part_ref[x, rows:, :].astype(F32)
        sums.append(stat + pltpu.roll(stat, HEAD - PAIR * Z, 1) + pltpu.roll(stat, HEAD - 2 * PAIR * Z, 1))
    peak = functools.reduce(jnp.maximum, sums)
    weights = [jnp.exp2(s - peak) for s in sums]
    total = functools.reduce(jnp.add, weights)
    weights = [w / total for w in weights]
    half = lax.broadcasted_iota(jnp.int32, (SLOT, HEAD), 1) // SHARE
    for z in range(Z):
        joined = functools.reduce(
            jnp.add,
            [
                jnp.take_along_axis(weights[x], half * Z + z, axis=1)
                * part_ref[x, z * SLOT : (z + 1) * SLOT, :].astype(F32)
                for x in range(X)
            ],
        )
        out_ref[z] = joined.astype(BF16)


def assemble(part_ref, out_ref):
    halves = lax.broadcasted_iota(jnp.int32, (SLOT, HEAD), 1) < SHARE
    for r in range(PARTS):
        for two in range(2):
            one, other = [part_ref[PARTS * (2 * two + n) + r].astype(F32) for n in range(2)]
            blocks = (
                jnp.where(halves, one, pltpu.roll(other, SHARE, 1)),
                jnp.where(halves, pltpu.roll(one, SHARE, 1), other),
            )
            for x, block in enumerate(blocks):
                first = ((2 * x + two) * PARTS + r) * SLOT
                for y in range(Y):
                    out_ref[y, first : first + SLOT, :] = block.astype(BF16)
        first = (2 * PAIR * PARTS + r) * SLOT
        for y in range(Y):
            out_ref[y, first : first + SLOT, :] = part_ref[PARTS * (HEADS_HERE - 1) + r]


def order_rows(place_ref, weight_ref, mine_ref, other_ref):
    core, side = place_ref[0], place_ref[1]
    depth = weight_ref.shape[0] // Z
    member = lax.rem(side, PAIR)
    places = []
    for m in range(depth // GRANULE):
        number = 2 * m + member
        holder, n = lax.div(number, X + 1), lax.rem(number, X + 1)
        away = lax.rem(holder + X - side, X)
        base = jnp.where(away == 0, 0, jnp.where(away == 1, 8, jnp.where(away == 2, 3, 6)))
        places.append((base + lax.div(n, 2)) * GRANULE)
    per_head = SHARE // GRANULE
    for which, out_ref in ((core, mine_ref), (1 - core, other_ref)):
        for y in range(Y):
            rows = []
            for n in range(HEADS_HERE * per_head):
                first = ((C * y + which) * 2 + n // len(places)) * depth + places[n % len(places)]
                rows.append(weight_ref[pl.ds(pl.multiple_of(first, GRANULE), GRANULE), :])
            rows += rows[4 * per_head :]
            for n, row in enumerate(rows):
                first = (y * len(rows) + n) * GRANULE
                out_ref[first : first + GRANULE, :] = row


def multiply(packed_ref, weight_ref):
    span = PARTS * SLOT
    halves = lax.broadcasted_iota(jnp.int32, (span, HEAD), 1) < SHARE
    inputs = [[] for _ in range(PAIR)]
    for y in range(Y):
        fifth = packed_ref[y, 2 * PAIR * span :, :].astype(F32)
        for x in range(PAIR):
            inputs[x] += [packed_ref[y, (2 * x + two) * span : (2 * x + two + 1) * span, :] for two in range(2)]
            inputs[x].append(jnp.where(halves == (x == 0), fifth, 0.0).astype(BF16))
    weights = weight_ref[...]
    return [
        jnp.dot(jnp.concatenate(blocks, axis=1), weights, preferred_element_type=F32) for blocks in inputs
    ]


def project_mine(packed_ref, weight_ref, sum_ref):
    for x, total in enumerate(multiply(packed_ref, weight_ref)):
        sum_ref[x] = total


def project_other(place_ref, packed_ref, weight_ref, sum_ref, out_ref):
    x = place_ref[0]
    span = PARTS * SLOT
    halves = lax.broadcasted_iota(jnp.int32, (span, HEAD), 1) // SHARE
    blocks = []
    for y in range(Y):
        fifth = packed_ref[y, 2 * PAIR * span :, :].astype(F32)
        for two in range(2):
            first = pl.multiple_of((2 * x + two) * span, GRANULE)
            blocks.append(packed_ref[y, pl.ds(first, span), :])
        blocks.append(jnp.where(halves == x, fifth, 0.0).astype(BF16))
    total = jnp.dot(jnp.concatenate(blocks, axis=1), weight_ref[...], preferred_element_type=F32)
    total = total + sum_ref[x]
    total = [total[r * SLOT : r * SLOT + length] for r, length in enumerate(LENGTHS)]
    out_ref[...] = jnp.concatenate(total, axis=0).astype(out_ref.dtype)


def share_rows(granules):
    even = jnp.concatenate([granules[n] for n in range(0, X + 1, 2)], axis=0)
    odd = jnp.concatenate([granules[n] for n in range(1, X + 1, 2)], axis=0)
    blocks = [even]
    for block, away in ((even, 2), (odd, 1), (odd, X - 1)):
        blocks.append(lax.ppermute(block, "x", [(x, (x + away) % X) for x in range(X)]))
    return jnp.concatenate(blocks, axis=0)


def local(queries, keys_in, values, cluster_ids, out_weight):
    plane, side, core = lax.axis_index("z"), lax.axis_index("x"), lax.axis_index("c")
    third = lax.rem(plane, PARTS)
    width = out_weight.shape[1]

    send, granules = vmem_call(
        scatter_heads,
        56,
        [(Z, SLOT + 2 * ROWS, HEAD), (X + 1, GRANULE, width)],
        queries,
        keys_in,
        values,
        cluster_ids.reshape(1, TOK),
        out_weight,
    )
    here = lax.all_to_all(send, "z", 0, 0, tiled=True)
    weight = lax.all_gather(share_rows(granules), "z", axis=0, tiled=True)
    kv = here[:, SLOT:, :]
    turns = [
        [(PARTS * h + r, PARTS * h + (r + k) % PARTS) for h in range(HEADS_HERE) for r in range(PARTS)]
        for k in (1, 2)
    ]
    kv_others = [lax.ppermute(kv, "z", turn) for turn in turns]
    query = lax.all_gather(here[:, :SLOT, :].reshape(Z * SLOT, HEAD), "x", axis=0)

    home = (X * jnp.arange(Z, dtype=jnp.int32) + side) * TOK
    key_code = here[:, ID_ROW + 1, :].astype(F32) * POSITIONS + (
        home[:, None] + jnp.arange(HEAD, dtype=jnp.int32)[None, :]
    ).astype(F32)
    key_code = jnp.stack(
        [
            jnp.pad(
                key_code[:, start : start + length], ((0, 0), (0, SLOT - length)), constant_values=NEVER
            ).reshape(Z * SLOT)
            for start, length in zip(STARTS, LENGTHS)
        ]
    )
    (part,) = vmem_call(
        attend,
        20,
        [(X, (Z + 1) * SLOT, HEAD)],
        query,
        kv,
        kv_others[0],
        kv_others[1],
        key_code,
        scalars=third.reshape(1),
        cost=pl.CostEstimate(flops=1 << 36, bytes_accessed=1 << 22, transcendentals=1 << 22),
    )
    part = lax.all_to_all(part, "x", 0, 0, tiled=True)
    (joined,) = vmem_call(join, 8, [(Z, SLOT, HEAD)], part)
    joined = lax.all_to_all(joined, "z", 0, 0, tiled=True)
    (packed,) = vmem_call(assemble, 8, [(Y, (2 * PAIR + 1) * PARTS * SLOT, HEAD)], joined)
    packed = lax.all_to_all(packed, "y", 0, 0, tiled=True)
    place = jnp.stack([core, side])
    depth = Y * (HEADS_HERE + 1) * SHARE
    weight_mine, weight_other = vmem_call(
        order_rows,
        12,
        [(depth, width), (depth, width)],
        weight,
        scalars=place,
        cost=pl.CostEstimate(flops=0, bytes_accessed=1 << 24, transcendentals=0),
    )
    packed, weight_other = lax.optimization_barrier((packed, weight_other))
    others = lax.ppermute(packed, "c", [(0, 1), (1, 0)])
    (sums,) = vmem_call(
        project_mine,
        16,
        [(PAIR, PARTS * SLOT, width)],
        packed,
        weight_mine,
        kinds=[F32],
        cost=pl.CostEstimate(flops=1 << 31, bytes_accessed=1 << 23, transcendentals=0),
    )
    member = lax.rem(side, PAIR)
    own, send = [
        vmem_call(
            project_other,
            16,
            [(TOK, width)],
            others,
            weight_other,
            sums,
            scalars=which.reshape(1),
            kinds=[kind],
            cost=pl.CostEstimate(flops=1 << 31, bytes_accessed=1 << 23, transcendentals=0),
        )[0]
        for which, kind in ((member, F32), (1 - member, BF16))
    ]
    came = lax.ppermute(send, "x", [(x, x + 1 - 2 * (x % PAIR)) for x in range(X)])
    return (own + came.astype(F32)).astype(BF16)


def solution(mesh):
    fine = Mesh(mesh.devices.reshape(Z, X, Y, C), ("z", "x", "y", "c"))
    both = P(("z", "x"), ("y", "c"))
    return jax.shard_map(
        local,
        mesh=fine,
        in_specs=(both, both, both, P(("z", "x"), None), both),
        out_specs=both,
        check_vma=False,
    )
```
